32 devices in a mesh: replica: 4 (over x, core), group: 8 (over z, y).
Axes of the slice: x: 2, y: 2, z: 4, core: 2. Of those that a mesh axis runs over, the one named last changes fastest.
Arguments:
- tokens: bfloat16 [4096, 1024], P(('replica', 'group')), may hold values from -6 to 6
- lengths: int32 [32, 4], P(('replica', 'group')), may hold values from 0 to 128, as said below
- cotangent: bfloat16 [4096, 1024], P(('replica', 'group')), may hold values from -6 to 6
- attention_in: bfloat16 [1024, 3072], P('group'), may hold values from -0.1875 to 0.1875
- query_bias: bfloat16 [1024], P('group'), may hold values from -3 to 3
- value_bias: bfloat16 [1024], P('group'), may hold values from -3 to 3
- attention_out: bfloat16 [1024, 1024], P('group'), may hold values from -0.75 to 0.75
- out_bias: bfloat16 [1024], P('group'), may hold values from -3 to 3
- first_gain: bfloat16 [1024], P('group'), may hold values from 0.5 to 1.5
- first_shift: bfloat16 [1024], P('group'), may hold values from -3 to 3
- hidden_in: bfloat16 [1024, 4096], P('group'), may hold values from -0.1875 to 0.1875
- hidden_bias: bfloat16 [4096], P('group'), may hold values from -3 to 3
- hidden_out: bfloat16 [4096, 1024], P('group'), may hold values from -0.09375 to 0.09375
- output_bias: bfloat16 [1024], P('group'), may hold values from -3 to 3
- second_gain: bfloat16 [1024], P('group'), may hold values from 0.5 to 1.5
- second_shift: bfloat16 [1024], P('group'), may hold values from -3 to 3
Outputs:
- layer_out: bfloat16 [4096, 1024], P(('replica', 'group'))
- grad_tokens: float32 [4096, 1024], P(('replica', 'group'))
- grad_attention_in: float32 [1024, 3072], P('group')
- grad_query_bias: float32 [1024], P('group')
- grad_value_bias: float32 [1024], P('group')
- grad_attention_out: float32 [1024, 1024], P('group')
- grad_out_bias: float32 [1024], P('group')
- grad_first_gain: float32 [1024], P('group')
- grad_first_shift: float32 [1024], P('group')
- grad_hidden_in: float32 [1024, 4096], P('group')
- grad_hidden_bias: float32 [4096], P('group')
- grad_hidden_out: float32 [4096, 1024], P('group')
- grad_output_bias: float32 [1024], P('group')
- grad_second_gain: float32 [1024], P('group')
- grad_second_shift: float32 [1024], P('group')
The draws below stay inside these ranges and needn't reach their ends.
Inputs may be any that keep to these rules, and one draw needn't show every extreme that they name: Row b lists the lengths of the sequences dealt to buffer b, packed one after another; the 4 lengths of a row sum to at most 128, so that buffers are filled unevenly, some lengths are zero, and some row holds a single sequence of 128 tokens.
All inputs are finite; a program needn't handle non-finite values.
Results may differ from the reference program's by a relative error of at most 0.019.
Values may be sent and summed in bfloat16 or wider, within the bound.
No kernel may reach another device: no remote copies, remote signals or barrier semaphores. Data moves between devices by JAX's collectives and lax.ppermute only.
A program may use at most 192 MiB of HBM per device.

```python
import jax
import jax.numpy as jnp
from jax import lax

D = 1024
H = 16
HD = 64
FF = 4096
TOK_DEV = 128
SEQS = 4
BUFFERS = 32
TOKENS = 4096
N_REPLICA = 4
N_GROUP = 8


def draw_lengths(key, part):
    key = jax.random.fold_in(key, 11)
    first, second, third = jax.random.split(key, 3)
    totals = jax.random.randint(first, (BUFFERS,), TOK_DEV // 4, TOK_DEV + 1)
    cuts = jax.random.randint(second, (BUFFERS, SEQS - 1), 0, totals[:, None] + 1)
    cuts = jnp.sort(cuts, axis=-1)
    zeros = jnp.zeros((BUFFERS, 1), jnp.int32)
    bounds = jnp.concatenate([zeros, cuts.astype(jnp.int32), totals[:, None].astype(jnp.int32)], axis=1)
    parts = bounds[:, 1:] - bounds[:, :-1]
    chosen = jax.random.randint(third, (), 0, BUFFERS)
    single = jnp.where(jnp.arange(SEQS) == 0, TOK_DEV, 0).astype(jnp.int32)
    rows = jnp.arange(BUFFERS)[:, None] == chosen
    return jnp.where(rows, single[None, :], parts).astype(jnp.int32)


def steps_of(stream_key, extent, shards, low, high):
    factor_of = 1.0
    for axis_at, shards_of in shards:
        steps = jax.random.uniform(jax.random.fold_in(jax.random.fold_in(stream_key, 6), axis_at), (shards_of,), jnp.float32, low / len(shards), high / len(shards))
        factor_of = factor_of * jnp.repeat(jnp.exp(steps), extent[axis_at] // shards_of).reshape((-1,) + (1,) * (len(extent) - 1 - axis_at))
    return factor_of


def gaussian(key, extent, deviation, bound, shards=(), held_as=jnp.bfloat16):
    entries = deviation * jax.random.normal(key, extent, jnp.float32)
    if shards:
        entries = entries * steps_of(key, extent, shards, -0.22, 0.18)
    return jnp.clip(entries, -bound, bound).astype(held_as)


def setup_inputs(seed: int = 0) -> dict:
    arg_keys = jax.random.split(jax.random.key(seed), 17)
    tokens = gaussian(arg_keys[0], (TOKENS, D), 1.0, 6.0, ((0, 32),))
    lengths = draw_lengths(jax.random.fold_in(arg_keys[16], 71), 0)
    cotangent = gaussian(arg_keys[2], (TOKENS, D), 1.0, 6.0, ((0, 32),))
    attention_in = gaussian(arg_keys[3], (D, 3 * D), D ** -0.5, 0.1875, ((0, 8),))
    query_bias = gaussian(arg_keys[4], (D,), 0.5, 3.0, ((0, 8),))
    value_bias = gaussian(arg_keys[5], (D,), 0.5, 3.0, ((0, 8),))
    attention_out = gaussian(arg_keys[6], (D, D), (D // 16) ** -0.5, 0.75, ((0, 8),))
    out_bias = gaussian(arg_keys[7], (D,), 0.5, 3.0, ((0, 8),))
    first_gain = jnp.clip(1.0 + 0.1 * jax.random.normal(arg_keys[8], (D,), jnp.float32), 0.5, 1.5).astype(jnp.bfloat16)
    first_shift = gaussian(arg_keys[9], (D,), 0.5, 3.0, ((0, 8),))
    hidden_in = gaussian(arg_keys[10], (D, FF), D ** -0.5, 0.1875, ((0, 8),))
    hidden_bias = gaussian(arg_keys[11], (FF,), 0.5, 3.0, ((0, 8),))
    hidden_out = gaussian(arg_keys[12], (FF, D), FF ** -0.5, 0.09375, ((0, 8),))
    output_bias = gaussian(arg_keys[13], (D,), 0.5, 3.0, ((0, 8),))
    second_gain = jnp.clip(1.0 + 0.1 * jax.random.normal(arg_keys[14], (D,), jnp.float32), 0.5, 1.5).astype(jnp.bfloat16)
    second_shift = gaussian(arg_keys[15], (D,), 0.5, 3.0, ((0, 8),))
    return {"tokens": tokens, "lengths": lengths, "cotangent": cotangent, "attention_in": attention_in, "query_bias": query_bias, "value_bias": value_bias, "attention_out": attention_out, "out_bias": out_bias, "first_gain": first_gain, "first_shift": first_shift, "hidden_in": hidden_in, "hidden_bias": hidden_bias, "hidden_out": hidden_out, "output_bias": output_bias, "second_gain": second_gain, "second_shift": second_shift}


@jax.custom_vjp
def low(v):
    return lax.optimization_barrier(v.astype(jnp.bfloat16)).astype(jnp.float32)

@jax.custom_vjp
def low_back(v):
    return v

def low_keep(v):
    return (low(v), None)

def low_pass(kept, grad):
    return (grad,)

def back_keep(v):
    return (v, None)

def back_low(kept, grad):
    return (low(grad),)
low.defvjp(low_keep, low_pass)
low_back.defvjp(back_keep, back_low)

def both_ways(value):
    return low_back(low(value))

def matmul(left, right):
    return jnp.einsum('...i,ij->...j', left, right, precision=lax.Precision.HIGHEST, preferred_element_type=jnp.float32)

def layer_norm(value, gain, shift):
    centre = lax.optimization_barrier(jnp.mean(value, -1, keepdims=True))
    offset = value - centre
    spread = lax.optimization_barrier(jnp.mean(offset * offset, -1, keepdims=True))
    return offset * lax.rsqrt(spread + 1e-06) * gain + shift

def segments(lengths):
    ends = jnp.cumsum(lengths, -1, dtype=jnp.int32)
    place = jnp.arange(TOK_DEV, dtype=jnp.int32)
    return lax.optimization_barrier(jnp.sum((place[:, None] >= ends[..., None, :]).astype(jnp.int32), -1, dtype=jnp.int32))

def block_forward(params, inputs, segment):
    attention_in, query_bias, value_bias, attention_out, out_bias, first_gain, first_shift, hidden_in, hidden_bias, hidden_out, output_bias, second_gain, second_shift = params
    batch = inputs.shape[0]
    joint = matmul(inputs, attention_in)
    query = both_ways(joint[..., :D] + query_bias).reshape(batch, TOK_DEV, H, HD)
    keys = both_ways(joint[..., D:2 * D]).reshape(batch, TOK_DEV, H, HD)
    values = both_ways(joint[..., 2 * D:] + value_bias).reshape(batch, TOK_DEV, H, HD)
    scale = HD ** (-0.5)
    raw = jnp.einsum('bqhd,bkhd->bhqk', query, keys, precision=lax.Precision.HIGHEST) * scale
    scores = low_back(raw)
    same = segment[:, None, :, None] == segment[:, None, None, :]
    probs = jax.nn.softmax(jnp.where(same, scores, -1000000000.0), axis=-1)
    mixed = jnp.einsum('bhqk,bkhd->bqhd', low(probs), values, precision=lax.Precision.HIGHEST)
    mixed = both_ways(mixed.reshape(batch, TOK_DEV, D))
    attn = low_back(matmul(mixed, attention_out) + out_bias)
    first = inputs + attn
    normed = layer_norm(first, first_gain, first_shift)
    pre = low_back(matmul(low(normed), hidden_in) + hidden_bias)
    active = low(jax.nn.gelu(pre, approximate=False))
    out = low_back(matmul(active, hidden_out) + output_bias)
    second = normed + out
    live = (segment < SEQS).astype(jnp.float32)[..., None]
    return layer_norm(second, second_gain, second_shift) * live

def reference(tokens, lengths, cotangent, attention_in, query_bias, value_bias, attention_out, out_bias, first_gain, first_shift, hidden_in, hidden_bias, hidden_out, output_bias, second_gain, second_shift):
    params = tuple((p.astype(jnp.float32) for p in (attention_in, query_bias, value_bias, attention_out, out_bias, first_gain, first_shift, hidden_in, hidden_bias, hidden_out, output_bias, second_gain, second_shift)))
    inputs = tokens.astype(jnp.float32).reshape(N_REPLICA, N_GROUP, TOK_DEV, D)
    segment = segments(lengths).reshape(N_REPLICA, N_GROUP, TOK_DEV)
    stepper = jax.checkpoint(block_forward)

    def forward(weights, values):
        return lax.map(lambda pair: stepper(weights, pair[0], pair[1]), (values, segment))
    result, pullback = jax.vjp(forward, params, inputs)
    grads, grad_inputs = pullback(cotangent.astype(jnp.float32).reshape(result.shape))
    return (result.reshape(TOKENS, D).astype(jnp.bfloat16), grad_inputs.reshape(TOKENS, D), grads[0], grads[1], grads[2], grads[3], grads[4], grads[5], grads[6], grads[7], grads[8], grads[9], grads[10], grads[11], grads[12])
```

```python
from functools import partial

import jax
import jax.numpy as jnp
from jax import lax
from jax.sharding import PartitionSpec as P

H = 16
HD = 64
SEQS = 4
TEAM = 4
BF = jnp.bfloat16
F32 = jnp.float32


def layer_norm(value, gain, shift):
    centre = jnp.mean(value, -1, keepdims=True)
    offset = value - centre
    spread = jnp.mean(offset * offset, -1, keepdims=True)
    return offset * lax.rsqrt(spread + 1e-06) * gain + shift


def segments(lengths, slots):
    ends = jnp.cumsum(lengths, -1, dtype=jnp.int32)
    place = jnp.arange(slots, dtype=jnp.int32)
    return jnp.sum((place[:, None] >= ends[..., None, :]).astype(jnp.int32), -1, dtype=jnp.int32)


def times(left, right):
    return jnp.dot(left, right, preferred_element_type=F32)


def against(left, weight):
    return lax.dot_general(
        left, weight, (((1,), (1,)), ((), ())), preferred_element_type=F32
    )


def outer(left, right):
    return lax.dot_general(
        left, right, (((0,), (0,)), ((), ())), preferred_element_type=F32
    )


def pick(index, cases):
    result = cases[-1]
    for at in range(len(cases) - 2, -1, -1):
        result = jnp.where(index == at, cases[at], result)
    return result


class Places:
    def __init__(self):
        self.n_group = lax.axis_size("group")
        self.n_replica = lax.axis_size("replica")
        self.depth = self.n_group // 2
        place = lax.axis_index("group")
        self.z = place // 2
        self.y = place % 2
        self.t = lax.axis_index("replica") % TEAM

    def send_z(self, value, step):
        depth = self.depth
        pairs = [
            (z * 2 + y, (z + step) % depth * 2 + y) for z in range(depth) for y in range(2)
        ]
        return lax.ppermute(value, "group", pairs)

    def send_y(self, value):
        return lax.ppermute(value, "group", [(g, g ^ 1) for g in range(self.n_group)])

    def send_team(self, value, flip):
        return lax.ppermute(value, "replica", [(r, r ^ flip) for r in range(self.n_replica)])

    def turn_group(self, blocks):
        depth = self.depth
        out = []
        for dy in range(2):
            column = [
                jnp.where(self.y == dy, blocks[2 * z], blocks[2 * z + 1]) for z in range(depth)
            ]
            for k in range(depth):
                out.append(pick(self.z, [column[(z - k) % depth] for z in range(depth)]))
        return out

    def untwist(self, blocks):
        depth = self.depth
        out = []
        for z in range(depth):
            pair = [
                pick(self.z, [blocks[dy * depth + (mine - z) % depth] for mine in range(depth)])
                for dy in range(2)
            ]
            out.append(jnp.where(self.y == 0, pair[0], pair[1]))
            out.append(jnp.where(self.y == 0, pair[1], pair[0]))
        return out

    def turn_columns(self, value):
        return jnp.concatenate(self.turn_group(jnp.split(value, self.n_group, -1)), -1)

    def untwist_columns(self, value):
        return jnp.concatenate(self.untwist(jnp.split(value, self.n_group, -1)), -1)

    def turn_team(self, blocks):
        a, b, c, d = blocks
        odd = self.t % 2 == 1
        a, b, c, d = (
            jnp.where(odd, b, a),
            jnp.where(odd, a, b),
            jnp.where(odd, d, c),
            jnp.where(odd, c, d),
        )
        high = self.t >= 2
        return [
            jnp.where(high, c, a),
            jnp.where(high, d, b),
            jnp.where(high, a, c),
            jnp.where(high, b, d),
        ]

    def gather_group(self, block):
        column = [block] + [self.send_z(block, k) for k in range(1, self.depth)]
        return column + [self.send_y(value) for value in column]

    def scatter_group(self, own, other):
        got = self.send_y(other.astype(BF))
        parts = jnp.split(own + got.astype(F32), self.depth, 0)
        total = parts[0]
        for k in range(1, self.depth):
            total = total + self.send_z(parts[k].astype(BF), -k).astype(F32)
        return total

    def gather_team(self, block):
        far = self.send_team(block, 2)
        near = self.send_team(block, 1)
        return [block, near, far, self.send_team(far, 1)]

    def scatter_team(self, value):
        a, b, c, d = jnp.split(value, TEAM, 0)
        got = self.send_team(jnp.concatenate([b, d], 0).astype(BF), 1).astype(F32)
        near, far = jnp.split(got, 2, 0)
        return (a + near) + self.send_team((c + far).astype(BF), 2).astype(F32)

    def over_copies(self, value):
        teams = self.n_replica // TEAM
        if teams == 1:
            return value
        return lax.psum(
            value.astype(BF),
            "replica",
            axis_index_groups=[
                [team * TEAM + t for team in range(teams)] for t in range(TEAM)
            ],
        ).astype(F32)


def shards(
    tokens,
    lengths,
    cotangent,
    attention_in,
    query_bias,
    value_bias,
    attention_out,
    out_bias,
    first_gain,
    first_shift,
    hidden_in,
    hidden_bias,
    hidden_out,
    output_bias,
    second_gain,
    second_shift,
):
    at = Places()
    n_group = at.n_group
    rows, width = tokens.shape
    d = attention_in.shape[0]
    f = hidden_bias.shape[0]
    part = width // TEAM
    heads = H // TEAM
    t = at.t

    def mine(value, axis, count):
        return lax.dynamic_slice_in_dim(value, t * count, count, axis)

    small = jnp.concatenate(
        [
            query_bias,
            value_bias,
            out_bias,
            first_gain,
            first_shift,
            hidden_bias,
            output_bias,
            second_gain,
            second_shift,
        ]
    )
    small_rows = -(-small.shape[0] // (3 * part))
    pad_rows = -(-small_rows // 16) * 16

    def small_block(flat):
        flat = jnp.pad(flat, (0, pad_rows * 3 * part - flat.shape[0]))
        return flat.reshape(pad_rows, 3 * part)

    token_low = at.turn_columns(tokens)
    extra = jnp.pad(lengths.astype(BF), ((0, 15), (0, width - lengths.shape[1])))
    packed = at.gather_team(jnp.concatenate([token_low, extra], 0))

    joint_mine = jnp.concatenate(
        [mine(attention_in[:, i * width : (i + 1) * width], 1, part) for i in range(3)], 1
    )
    first_blocks = at.gather_group(jnp.concatenate([joint_mine, small_block(small)], 0))
    out_rows = d // TEAM
    w = f // TEAM
    second_blocks = at.gather_group(mine(attention_out, 0, out_rows))
    hidden_mine = jnp.concatenate(
        [mine(hidden_in[:, i * f : (i + 1) * f], 1, w) for i in range(n_group)], 1
    )
    third_blocks = at.gather_group(hidden_mine)
    fourth_blocks = at.gather_group(mine(hidden_out, 0, w))

    w_joint = jnp.concatenate([block[:d] for block in first_blocks], 0)
    smalls = jnp.stack(
        at.untwist([block[d:].reshape(-1)[: small.shape[0]] for block in first_blocks])
    )
    offsets = [0]
    for size in (d, d, d, d, d, f, d, d, d):
        offsets.append(offsets[-1] + size)
    q_bias, v_bias, o_bias, gain1, shift1, h_bias, out_b, gain2, shift2 = (
        smalls[:, offsets[i] : offsets[i + 1]].reshape(-1).astype(F32) for i in range(9)
    )

    members = n_group // TEAM
    out_all = at.untwist(second_blocks)
    by_owner = at.turn_team(
        [jnp.concatenate(out_all[i * members : (i + 1) * members], 0) for i in range(TEAM)]
    )
    traded = at.turn_team(
        [by_owner[0]] + [at.send_team(by_owner[flip], flip) for flip in range(1, TEAM)]
    )
    w_out = jnp.stack([v.reshape(members, out_rows, width) for v in traded], 1).reshape(
        part, width
    )
    w_hidden = jnp.concatenate(third_blocks, 0)
    w_back = jnp.concatenate(fourth_blocks, 0)

    scale = HD ** (-0.5)
    token4 = jnp.concatenate([block[:rows] for block in packed], 0)
    length4 = jnp.stack([block[rows, : lengths.shape[1]] for block in packed]).astype(jnp.int32)
    segment4 = segments(length4, rows)
    same = (segment4[:, :, None] == segment4[:, None, :])[:, None]
    live = (segment4[0] < SEQS).astype(F32)[:, None]

    def split(value):
        return value.reshape(TEAM, rows, heads, HD)

    joint = times(token4, w_joint)
    query = split((joint[:, :part] + mine(q_bias, 0, part)).astype(BF))
    keys = split(joint[:, part : 2 * part].astype(BF))
    values = split((joint[:, 2 * part :] + mine(v_bias, 0, part)).astype(BF))
    scores = jnp.einsum("bqhd,bkhd->bhqk", query, keys, preferred_element_type=F32) * scale
    scores = jnp.where(same, scores, -1000000000.0)
    highest = jnp.max(scores, -1, keepdims=True)
    expo = jnp.exp(scores - highest)
    probs = expo / jnp.sum(expo, -1, keepdims=True)
    mixed = jnp.einsum("bhqk,bkhd->bqhd", probs.astype(BF), values, preferred_element_type=F32)
    mixed = mixed.reshape(TEAM * rows, part).astype(BF)
    attn = at.scatter_team(times(mixed, w_out)) + o_bias

    first = tokens.astype(F32) + attn
    normed, first_back = jax.vjp(layer_norm, first, gain1, shift1)
    normed4 = jnp.concatenate(at.gather_team(at.turn_columns(normed.astype(BF))), 0)
    bias4 = mine(h_bias.reshape(n_group, f), 1, w).reshape(1, -1)
    pre = at.turn_columns(times(normed4, w_hidden) + bias4)
    active, gelu_back = jax.vjp(partial(jax.nn.gelu, approximate=False), pre)
    active_low = active.astype(BF)
    out = at.scatter_team(times(active_low, w_back)) + out_b
    second = normed + out
    final, second_back = jax.vjp(layer_norm, second, gain2, shift2)
    layer_out = (final * live).astype(BF)

    d_second, g_gain2, g_shift2 = second_back(cotangent.astype(F32) * live)
    d_out = d_second.astype(BF)
    d_out4 = jnp.concatenate(at.gather_team(d_out), 0)
    half = n_group // 2

    def scatter_grad(left, right):
        middle = left.shape[1] // 2
        other = outer(left[:, middle:], right)
        own = outer(left[:, :middle], right)
        return at.over_copies(at.scatter_group(own, other)).astype(BF)

    g_back = scatter_grad(active_low, d_out4)
    d_active = against(d_out4, w_back)
    d_pre_turned = gelu_back(d_active)[0].astype(BF)
    d_pre = at.untwist_columns(d_pre_turned)
    g_hidden = scatter_grad(normed4, d_pre)
    d_normed = d_second + at.untwist_columns(at.scatter_team(against(d_pre, w_hidden)))
    d_first, g_gain1, g_shift1 = first_back(d_normed)
    d_attn = d_first.astype(BF)
    d_attn4 = jnp.concatenate(at.gather_team(d_attn), 0)

    g_out_heads = outer(mixed, d_attn4).astype(BF).reshape(members, TEAM, out_rows, width)
    to_trade = at.turn_team(
        [g_out_heads[:, i].reshape(members * out_rows, width) for i in range(TEAM)]
    )
    by_member = at.turn_team(
        [to_trade[0]] + [at.send_team(to_trade[flip], flip) for flip in range(1, TEAM)]
    )
    g_out_blocks = at.turn_group(
        [block for piece in by_member for block in jnp.split(piece, members, 0)]
    )
    g_attn_out = at.over_copies(
        at.scatter_group(
            jnp.concatenate(g_out_blocks[:half], 0).astype(F32),
            jnp.concatenate(g_out_blocks[half:], 0),
        )
    ).astype(BF)

    d_mixed = split(against(d_attn4, w_out).astype(BF))
    d_values = jnp.einsum(
        "bhqk,bqhd->bkhd", probs.astype(BF), d_mixed, preferred_element_type=F32
    ).astype(BF)
    d_probs = jnp.einsum("bqhd,bkhd->bhqk", d_mixed, values, preferred_element_type=F32)
    d_scores = (probs * (d_probs - jnp.sum(probs * d_probs, -1, keepdims=True))).astype(BF)
    d_query = (
        jnp.einsum("bhqk,bkhd->bqhd", d_scores, keys, preferred_element_type=F32) * scale
    ).astype(BF)
    d_keys = (
        jnp.einsum("bhqk,bqhd->bkhd", d_scores, query, preferred_element_type=F32) * scale
    ).astype(BF)
    d_joint = jnp.concatenate(
        [v.reshape(TEAM * rows, part) for v in (d_query, d_keys, d_values)], 1
    )

    def column_sum(value):
        return jnp.sum(value.astype(F32), 0)

    def at_mine(value, axis):
        zeros = jnp.zeros_like(value)
        return jnp.concatenate([jnp.where(t == i, value, zeros) for i in range(TEAM)], axis)

    joint_sums = column_sum(d_joint)
    g_small = jnp.concatenate(
        [
            at_mine(joint_sums[:part], 0).reshape(n_group, d),
            at_mine(joint_sums[2 * part :], 0).reshape(n_group, d),
            column_sum(d_attn).reshape(n_group, d),
            g_gain1.reshape(n_group, d),
            g_shift1.reshape(n_group, d),
            at_mine(column_sum(d_pre).reshape(n_group, w), 1),
            column_sum(d_out).reshape(n_group, d),
            g_gain2.reshape(n_group, d),
            g_shift2.reshape(n_group, d),
        ],
        1,
    )
    small_parts = at.turn_group([small_block(g_small[i]) for i in range(n_group)])
    middle = width // 2
    joint_other = outer(token4[:, middle:], d_joint).reshape(half, d, 3 * part)
    joint_own = outer(token4[:, :middle], d_joint).reshape(half, d, 3 * part)
    sent = d + pad_rows

    def with_small(grad, parts):
        return jnp.concatenate([grad, jnp.stack(parts)], 1).reshape(half * sent, 3 * part)

    g_joint = at.over_copies(
        at.scatter_group(
            with_small(joint_own, small_parts[:half]), with_small(joint_other, small_parts[half:])
        )
    ).astype(BF)
    grad_tokens = d_first + at.untwist_columns(at.scatter_team(against(d_joint, w_joint)))

    back_all = at.turn_team(at.gather_team(g_back))
    hidden_all = at.turn_team(at.gather_team(g_hidden))
    attn_out_all = at.turn_team(at.gather_team(g_attn_out))
    joint_all = at.turn_team(at.gather_team(g_joint))
    g_hidden_out = jnp.concatenate(back_all, 0).astype(F32)
    g_hidden_in = (
        jnp.stack([v.reshape(d, n_group, w) for v in hidden_all], 2).reshape(d, -1).astype(F32)
    )
    g_attention_out = jnp.concatenate(attn_out_all, 0).astype(F32)
    g_attention_in = (
        jnp.stack([v[:d].reshape(d, 3, part) for v in joint_all], 2)
        .reshape(d, 3 * width)
        .astype(F32)
    )
    s = sum(v[d:].reshape(-1)[: small.shape[0]].astype(F32) for v in joint_all)
    g_qb, g_vb, g_ob, g_g1, g_s1, g_hb, g_outb, g_g2, g_s2 = (
        s[offsets[i] : offsets[i + 1]] for i in range(9)
    )
    return (
        layer_out,
        grad_tokens,
        g_attention_in,
        g_qb,
        g_vb,
        g_attention_out,
        g_ob,
        g_g1,
        g_s1,
        g_hidden_in,
        g_hb,
        g_hidden_out,
        g_outb,
        g_g2,
        g_s2,
    )


def solution(mesh):
    rows = P(("replica", "group"), None)
    matrix = P("group", None)
    vector = P("group")
    params = (
        matrix,
        vector,
        vector,
        matrix,
        vector,
        vector,
        vector,
        matrix,
        vector,
        matrix,
        vector,
        vector,
        vector,
    )
    return jax.shard_map(
        shards,
        mesh=mesh,
        in_specs=(rows, rows, rows) + params,
        out_specs=(rows, rows) + params,
        check_vma=False,
    )
```

```python
from functools import partial

import jax
import jax.numpy as jnp
from jax import lax
from jax.experimental import pallas as pl
from jax.experimental.pallas import tpu as pltpu
from jax.sharding import PartitionSpec as P

H = 16
HD = 64
SEQS = 4
TEAM = 4
EXTRA = 16
PAIR = 2 * HD
BF = jnp.bfloat16
F32 = jnp.float32


class Places:
    def __init__(self):
        self.n_group = lax.axis_size("group")
        self.n_replica = lax.axis_size("replica")
        self.depth = self.n_group // 2
        self.heads_at = self.depth // TEAM
        place = lax.axis_index("group")
        self.z = place // 2
        self.y = place % 2
        self.t = lax.axis_index("replica") % TEAM
        self.place = jnp.stack([self.t, self.z, self.y]).astype(jnp.int32)

    def send_z(self, value, step):
        depth = self.depth
        pairs = [
            (z * 2 + y, (z + step) % depth * 2 + y) for z in range(depth) for y in range(2)
        ]
        return lax.ppermute(value, "group", pairs)

    def send_y(self, value):
        return lax.ppermute(value, "group", [(g, g ^ 1) for g in range(self.n_group)])

    def send_team(self, value, flip):
        return lax.ppermute(value, "replica", [(r, r ^ flip) for r in range(self.n_replica)])

    def send_heads(self, value, at, step, back):
        pairs = []
        for r in range(self.n_replica):
            z = r % TEAM * self.heads_at + at
            for y in range(2):
                home = r * self.n_group + z * 2 + y
                away = r * self.n_group + (z + step) % self.depth * 2 + y
                pairs.append((away, home) if back else (home, away))
        return lax.ppermute(value, ("replica", "group"), pairs)

    def gather_team(self, block):
        far = self.send_team(block, 2)
        near = self.send_team(block, 1)
        return [block, near, far, self.send_team(far, 1)]

    def scatter_team(self, near, keep):
        n = near.shape[0] // 2
        got = self.send_team(near, 1)
        far = self.send_team((keep[n:] + got[n:].astype(F32)).astype(BF), 2)
        return keep, got, far

    def over_copies(self, value):
        teams = self.n_replica // TEAM
        if teams == 1:
            return value
        return lax.psum(
            value,
            "replica",
            axis_index_groups=[
                [team * TEAM + t for team in range(teams)] for t in range(TEAM)
            ],
        )


def call(kernel, outs, place, *args, flops=0, scratch=()):
    size = sum(a.size * a.dtype.itemsize for a in args)
    size += sum(o.size * o.dtype.itemsize for o in outs)
    return pl.pallas_call(
        kernel,
        out_shape=outs,
        in_specs=[pl.BlockSpec(memory_space=pltpu.SMEM)]
        + [pl.BlockSpec(memory_space=pltpu.VMEM)] * len(args),
        out_specs=[pl.BlockSpec(memory_space=pltpu.VMEM)] * len(outs),
        scratch_shapes=list(scratch),
        compiler_params=pltpu.CompilerParams(vmem_limit_bytes=40 << 20),
        cost_estimate=pl.CostEstimate(flops=flops, bytes_accessed=size, transcendentals=0),
    )(place, *args)


def shape(dims, dtype):
    return jax.ShapeDtypeStruct(tuple(dims), dtype)


def times(left, right):
    return jnp.dot(left, right, preferred_element_type=F32)


def against(left, weight):
    return lax.dot_general(left, weight, (((1,), (1,)), ((), ())), preferred_element_type=F32)


def outer(left, right):
    return lax.dot_general(left, right, (((0,), (0,)), ((), ())), preferred_element_type=F32)


def chosen(index, cases):
    result = cases[-1]
    for at in range(len(cases) - 2, -1, -1):
        result = jnp.where(index == at, cases[at], result)
    return result


def of_member(t, member, blocks):
    return chosen(t, [blocks[i ^ member] for i in range(TEAM)])


def column_sum(value):
    return jnp.sum(value, 0, keepdims=True)


def ends_of(block, n):
    row = block[n : n + EXTRA, 0:128].astype(F32)[0:1]
    lane = lax.broadcasted_iota(jnp.int32, (1, 128), 1)
    return [
        jnp.sum(jnp.where(lane <= s, row, 0.0), axis=1, keepdims=True) for s in range(SEQS)
    ]


def segments(ends, dims, axis):
    place = lax.broadcasted_iota(jnp.int32, dims, axis).astype(F32)
    total = jnp.zeros(dims, F32)
    for end in ends:
        total = total + jnp.where(place >= end, 1.0, 0.0)
    return total


def normalise(value):
    centre = jnp.mean(value, -1, keepdims=True)
    offset = value - centre
    spread = jnp.mean(offset * offset, -1, keepdims=True)
    factor = lax.rsqrt(spread + 1e-06)
    return offset * factor, factor


def normalise_back(d_hat, hat, factor):
    return factor * (
        d_hat
        - jnp.mean(d_hat, -1, keepdims=True)
        - hat * jnp.mean(d_hat * hat, -1, keepdims=True)
    )


def grad_tiles(place, n_group, width, left, right, own, other, tile):
    depth = n_group // 2
    z, y = place[1], place[2]

    def step(at, carry):
        tile[...] = outer(left[:, pl.ds(pl.multiple_of(at * 2 * width, 2 * width), 2 * width)], right[...])
        k = lax.rem(z - at + depth, depth)
        own[k, 0:width, :] = tile[pl.ds(pl.multiple_of(y * width, width), width), :]
        other[k, 0:width, :] = tile[
            pl.ds(pl.multiple_of((1 - y) * width, width), width), :
        ].astype(BF)
        return carry

    lax.fori_loop(0, depth, step, 0)


def to_team(value, n, near, keep, columns):
    keep[0:n, columns] = value[0:n]
    near[0:n, columns] = value[n : 2 * n].astype(BF)
    keep[n : 2 * n, columns] = value[2 * n : 3 * n]
    near[n : 2 * n, columns] = value[3 * n : 4 * n].astype(BF)


def prepare_kernel(n_group, place, att, hid, back, small, first_o, rest_o):
    t = place[0]
    d, joint = att.shape
    width = joint // 3
    part = width // TEAM
    f = hid.shape[1] // n_group
    w = f // TEAM
    for i in range(3):
        first_o[0:d, i * part : (i + 1) * part] = chosen(
            t,
            [
                att[:, i * width + s * part : i * width + (s + 1) * part]
                for s in range(TEAM)
            ],
        )
    first_o[d : d + EXTRA, :] = small[...]
    for g in range(n_group):
        rest_o[0:d, g * w : (g + 1) * w] = chosen(
            t, [hid[:, g * f + s * w : g * f + (s + 1) * w] for s in range(TEAM)]
        )
    rest_o[d : d + w, :] = back[pl.ds(pl.multiple_of(t * w, w), w), :]


def attention_kernel(
    n_group, d, f, n, place, p0, p1, p2, p3, first, own_out, other_out,
    joint_o, probs_o, mixed_o, near_o, keep_o, vec_o, hb_o, wout_o, token_s,
):
    blocks = (p0, p1, p2, p3)
    t, y = place[0], place[2]
    part = wout_o.shape[0]
    width = wout_o.shape[1]
    w = f // TEAM
    small = [first[g, d : d + EXTRA, :].astype(F32) for g in range(n_group)]
    vec_o[...] = jnp.concatenate([s[0:8, 0:d] for s in small], 1)
    hb_o[...] = jnp.concatenate(
        [chosen(t, [s[8:9, i * w : (i + 1) * w] for i in range(TEAM)]) for s in small], 1
    )
    for at in range(part // (2 * d)):
        wout_o[pl.ds(pl.multiple_of((at * 2 + y) * d, d), d), :] = own_out[
            at * d : (at + 1) * d
        ]
        wout_o[pl.ds(pl.multiple_of((at * 2 + 1 - y) * d, d), d), :] = other_out[
            at * d : (at + 1) * d
        ]
    for b in range(TEAM):
        token_s[b * n : (b + 1) * n] = blocks[b][0:n]
    mine = pl.ds(pl.multiple_of(t * part, part), part)
    for i in range(3):
        weight = first[:, 0:d, i * part : (i + 1) * part].reshape(n_group * d, part)
        value = times(token_s[...], weight)
        if i == 0:
            value = value + vec_o[0:1, mine]
        if i == 2:
            value = value + vec_o[1:2, mine]
        joint_o[:, i * part : (i + 1) * part] = value.astype(BF)
    scale = HD ** (-0.5)
    low = lax.broadcasted_iota(jnp.int32, (1, PAIR), 1) < HD
    zero = jnp.zeros((), BF)
    for b in range(TEAM):
        rows = slice(b * n, (b + 1) * n)
        ends = ends_of(blocks[b], n)
        same = segments(ends, (n, 1), 0) == segments(ends, (1, n), 1)
        for pair in range(part // PAIR):
            at = pair * PAIR
            query = joint_o[rows, at : at + PAIR]
            keys = joint_o[rows, part + at : part + at + PAIR]
            values = joint_o[rows, 2 * part + at : 2 * part + at + PAIR]
            mixed = []
            for h in range(2):
                sided = jnp.where(low, query, zero) if h == 0 else jnp.where(low, zero, query)
                scores = jnp.where(same, against(sided, keys) * scale, -1000000000.0)
                expo = jnp.exp(scores - jnp.max(scores, -1, keepdims=True))
                probs = expo / jnp.sum(expo, -1, keepdims=True)
                probs_o[(b * (part // PAIR) + pair) * 2 + h] = probs
                mixed.append(times(probs.astype(BF), values))
            mixed_o[rows, at : at + PAIR] = jnp.where(low, mixed[0], mixed[1]).astype(BF)
    for at in range(0, width, part):
        columns = slice(at, at + part)
        to_team(times(mixed_o[...], wout_o[:, columns]), n, near_o, keep_o, columns)


def norm_kernel(place, tokens, keep, got, far, vec, normed_o, low_o, hat_o, factor_o):
    n = tokens.shape[0]
    attn = keep[0:n] + got[0:n].astype(F32) + far[...].astype(F32) + vec[2:3]
    hat, factor = normalise(tokens[...].astype(F32) + attn)
    normed = hat * vec[3:4] + vec[4:5]
    normed_o[...] = normed
    low_o[...] = normed.astype(BF)
    hat_o[...] = hat
    factor_o[...] = jnp.broadcast_to(factor, factor_o.shape)


def gelu_parts(pre):
    bell = 0.5 * (1.0 + lax.erf(pre * (2.0**-0.5)))
    return bell, jnp.exp(-0.5 * pre * pre) * (2.0 * 3.141592653589793) ** -0.5


def feed_kernel(
    n_group, d, place, x0, x1, x2, x3, rest, hb, pre_o, act_o, near_o, keep_o, x_o
):
    n = x0.shape[0]
    w = rest.shape[1] - d
    inner = rest.shape[2]
    for b, block in enumerate((x0, x1, x2, x3)):
        x_o[b * n : (b + 1) * n] = block[...]
    step = 256

    def hidden(at, carry):
        columns = pl.ds(pl.multiple_of(at * step, step), step)
        weight = rest[:, 0:d, columns].reshape(n_group * d, step)
        pre = times(x_o[...], weight) + hb[:, columns]
        pre_o[:, columns] = pre
        act_o[:, columns] = (pre * gelu_parts(pre)[0]).astype(BF)
        return carry

    lax.fori_loop(0, inner // step, hidden, 0)

    def back(at, carry):
        columns = pl.ds(pl.multiple_of(at * step, step), step)
        weight = rest[:, d : d + w, columns].reshape(n_group * w, step)
        to_team(times(act_o[...], weight), n, near_o, keep_o, columns)
        return carry

    lax.fori_loop(0, inner // step, back, 0)


def second_kernel(
    place, normed, keep, got, far, vec, cotangent, packed, layer_o, d_second_o, d_out_o, sums_o
):
    n = normed.shape[0]
    out = keep[0:n] + got[0:n].astype(F32) + far[...].astype(F32) + vec[5:6]
    hat, factor = normalise(normed[...] + out)
    live = jnp.where(segments(ends_of(packed, n), (n, 1), 0) < SEQS, 1.0, 0.0)
    layer_o[...] = ((hat * vec[6:7] + vec[7:8]) * live).astype(BF)
    d_final = cotangent[...].astype(F32) * live
    d_second = normalise_back(d_final * vec[6:7], hat, factor)
    d_second_o[...] = d_second
    d_out = d_second.astype(BF)
    d_out_o[...] = d_out
    sums_o[...] = jnp.zeros_like(sums_o)
    sums_o[0:1] = column_sum(d_out.astype(F32))
    sums_o[1:2] = column_sum(d_final * hat)
    sums_o[2:3] = column_sum(d_final)


def back_grad_kernel(n_group, place, d0, d1, d2, d3, act, own_o, other_o, d_out_o, tile):
    n = d0.shape[0]
    for b, block in enumerate((d0, d1, d2, d3)):
        d_out_o[b * n : (b + 1) * n] = block[...]
    grad_tiles(place, n_group, act.shape[1] // n_group, act, d_out_o, own_o, other_o, tile)


def feed_back_kernel(
    n_group, d, n, place, d_out, rest, pre, d_pre_o, near_o, keep_o, hb_o
):
    w = rest.shape[1] - d
    per = 256 // w

    def hidden(at, carry):
        columns = pl.ds(pl.multiple_of(at * 256, 256), 256)
        weight = rest[pl.ds(at * per, per), d : d + w, :].reshape(256, rest.shape[2])
        d_act = against(d_out[...], weight)
        value = pre[:, columns]
        bell, slope = gelu_parts(value)
        d_pre = (d_act * (bell + value * slope)).astype(BF)
        d_pre_o[:, columns] = d_pre
        hb_o[:, columns] = column_sum(d_pre.astype(F32))
        return carry

    lax.fori_loop(0, pre.shape[1] // 256, hidden, 0)
    rows = 256 // d

    def back(at, carry):
        columns = pl.ds(pl.multiple_of(at * 256, 256), 256)
        weight = rest[pl.ds(at * rows, rows), 0:d, :].reshape(256, rest.shape[2])
        to_team(against(d_pre_o[...], weight), n, near_o, keep_o, columns)
        return carry

    lax.fori_loop(0, keep_o.shape[1] // 256, back, 0)


def hidden_grad_kernel(n_group, d, place, x, d_pre, own_o, other_o, tile):
    grad_tiles(place, n_group, d, x, d_pre, own_o, other_o, tile)


def norm_back_kernel(
    place, d_second, keep, got, far, hat, factor, vec, d_first_o, d_attn_o, sums_o
):
    n = d_second.shape[0]
    d_normed = d_second[...] + keep[0:n] + got[0:n].astype(F32) + far[...].astype(F32)
    d_first = normalise_back(d_normed * vec[3:4], hat[...], factor[:, 0:1])
    d_first_o[...] = d_first
    d_attn = d_first.astype(BF)
    d_attn_o[...] = d_attn
    sums_o[...] = jnp.zeros_like(sums_o)
    sums_o[0:1] = column_sum(d_attn.astype(F32))
    sums_o[1:2] = column_sum(d_normed * hat[...])
    sums_o[2:3] = column_sum(d_normed)


def attention_back_kernel(
    n_group, d, f, n, place, a0, a1, a2, a3, wout, joint, probs_in, mixed, p0, p1, p2, p3,
    sums1, sums2, d_hb,
    d_joint_o, own_o, other_o, out_own_o, out_other_o, token_s, attn_s, tile, heads_s, vec_s,
    small_s,
):
    t, z, y = place[0], place[1], place[2]
    depth = n_group // 2
    part, width = wout.shape
    w = f // TEAM
    for b in range(TEAM):
        token_s[b * n : (b + 1) * n] = (p0, p1, p2, p3)[b][0:n]
        attn_s[b * n : (b + 1) * n] = (a0, a1, a2, a3)[b][...]
    heads_s[...] = outer(mixed[...], attn_s[...])
    for at in range(part // (2 * d)):
        out_own_o[at * d : (at + 1) * d] = heads_s[
            pl.ds(pl.multiple_of((at * 2 + y) * d, d), d), :
        ]
        out_other_o[at * d : (at + 1) * d] = heads_s[
            pl.ds(pl.multiple_of((at * 2 + 1 - y) * d, d), d), :
        ].astype(BF)
    d_mixed = against(attn_s[...], wout[...]).astype(BF)
    scale = HD ** (-0.5)
    low = lax.broadcasted_iota(jnp.int32, (1, PAIR), 1) < HD
    zero = jnp.zeros((), BF)
    for b in range(TEAM):
        rows = slice(b * n, (b + 1) * n)
        for pair in range(part // PAIR):
            at = pair * PAIR
            query = joint[rows, at : at + PAIR]
            keys = joint[rows, part + at : part + at + PAIR]
            values = joint[rows, 2 * part + at : 2 * part + at + PAIR]
            d_mix = d_mixed[rows, at : at + PAIR]
            d_query, d_keys, d_values = [], [], []
            for h in range(2):
                probs = probs_in[(b * (part // PAIR) + pair) * 2 + h]
                sided = jnp.where(low, d_mix, zero) if h == 0 else jnp.where(low, zero, d_mix)
                d_probs = against(sided, values)
                d_scores = (
                    probs * (d_probs - jnp.sum(probs * d_probs, -1, keepdims=True))
                ).astype(BF)
                d_values.append(outer(probs.astype(BF), d_mix))
                d_query.append(times(d_scores, keys))
                d_keys.append(outer(d_scores, query))
            for i, (value, factor) in enumerate(
                ((d_query, scale), (d_keys, scale), (d_values, 1.0))
            ):
                d_joint_o[rows, i * part + at : i * part + at + PAIR] = (
                    jnp.where(low, value[0], value[1]) * factor
                ).astype(BF)
    vec_s[...] = jnp.zeros_like(vec_s)
    mine = pl.ds(pl.multiple_of(t * part, part), part)
    vec_s[0:1, mine] = column_sum(d_joint_o[:, 0:part].astype(F32))
    vec_s[1:2, mine] = column_sum(d_joint_o[:, 2 * part : 3 * part].astype(F32))
    vec_s[2:5, :] = sums1[0:3]
    vec_s[5:8, :] = sums2[0:3]
    small_s[...] = jnp.zeros_like(small_s)
    for g in range(n_group):
        small_s[g, 0:8, 0:d] = vec_s[:, g * d : (g + 1) * d]
        row = d_hb[:, g * w : (g + 1) * w]
        small_s[g, 8:9, 0:f] = jnp.concatenate(
            [jnp.where(t == i, row, jnp.zeros_like(row)) for i in range(TEAM)], 1
        )
    grad_tiles(place, n_group, d, token_s, d_joint_o, own_o, other_o, tile)
    for k in range(depth):
        g = lax.rem(z - k + depth, depth) * 2
        own_o[k, d : d + EXTRA, :] = small_s[g + y]
        other_o[k, d : d + EXTRA, :] = small_s[g + 1 - y].astype(BF)


def token_back_kernel(n_group, d, n, place, d_joint, first, near_o, keep_o):
    per = 256 // d

    def back(at, carry):
        columns = pl.ds(pl.multiple_of(at * 256, 256), 256)
        weight = first[pl.ds(at * per, per), 0:d, :].reshape(256, first.shape[2])
        to_team(against(d_joint[...], weight), n, near_o, keep_o, columns)
        return carry

    lax.fori_loop(0, keep_o.shape[1] // 256, back, 0)


def add_kernel(place, own, got, keep_o, *sends_o):
    keep_o[...] = own[0] + got[0].astype(F32)
    for k, send in enumerate(sends_o):
        send[...] = (own[k + 1] + got[k + 1].astype(F32)).astype(BF)


def feed_out_kernel(n_group, place, b0, b1, b2, b3, h0, h1, h2, h3, back_o, hidden_o):
    t = place[0]
    w = b0.shape[0]
    for i in range(TEAM):
        back_o[i * w : (i + 1) * w] = of_member(
            t, i, [b[...] for b in (b0, b1, b2, b3)]
        ).astype(F32)
        block = of_member(t, i, [h[...] for h in (h0, h1, h2, h3)]).astype(F32)
        for g in range(n_group):
            at = (g * TEAM + i) * w
            hidden_o[:, at : at + w] = block[:, g * w : (g + 1) * w]


def attention_out_kernel(
    heads_at, f, place, j0, j1, j2, j3, o0, o1, o2, o3, joint_o, out_o, *small_o
):
    t, z = place[0], place[1]
    d = out_o.shape[0]
    part = j0.shape[1] // 3
    width = part * TEAM
    total = jnp.zeros((EXTRA, 3 * part), F32)
    for i in range(TEAM):
        block = of_member(t, i, [j[...] for j in (j0, j1, j2, j3)]).astype(F32)
        for s in range(3):
            at = s * width + i * part
            joint_o[:, at : at + part] = block[0:d, s * part : (s + 1) * part]
        total = total + block[d : d + EXTRA]
    outs = [o[...] for o in (o0, o1, o2, o3)]
    out = of_member(t, TEAM - 1, outs)
    for i in range(TEAM - 1):
        out = jnp.where(z // heads_at == i, of_member(t, i, outs), out)
    out_o[...] = out.astype(F32)
    for i in range(8):
        small_o[i][...] = total[i : i + 1, 0:d]
    small_o[8][...] = total[8:9, 0:f]


def shards(
    tokens,
    lengths,
    cotangent,
    attention_in,
    query_bias,
    value_bias,
    attention_out,
    out_bias,
    first_gain,
    first_shift,
    hidden_in,
    hidden_bias,
    hidden_out,
    output_bias,
    second_gain,
    second_shift,
):
    at = Places()
    n_group, depth, place = at.n_group, at.depth, at.place
    n, width = tokens.shape
    d = attention_in.shape[0]
    f = hidden_bias.shape[0]
    w = f // TEAM
    part = width // TEAM
    inner = w * n_group
    all_rows = TEAM * n

    vectors = (
        query_bias,
        value_bias,
        out_bias,
        first_gain,
        first_shift,
        output_bias,
        second_gain,
        second_shift,
    )
    small = jnp.concatenate(
        [
            jnp.pad(jnp.stack(vectors), ((0, 0), (0, 3 * part - d))),
            jnp.pad(hidden_bias[None], ((0, EXTRA - 9), (0, 3 * part - f))),
        ],
        0,
    )
    first_mine, rest_mine = call(
        partial(prepare_kernel, n_group),
        [shape((d + EXTRA, 3 * part), BF), shape((d + w, width), BF)],
        place,
        attention_in,
        hidden_in,
        hidden_out,
        small,
    )
    first_all = lax.all_gather(first_mine, "group", axis=0)
    rest_all = lax.all_gather(rest_mine, "group", axis=0)
    extra = jnp.pad(lengths.astype(BF), ((0, EXTRA - 1), (0, width - lengths.shape[1])))
    packed = at.gather_team(jnp.concatenate([tokens, extra], 0))
    heads_mine = []
    for i in range(at.heads_at):
        here = at.z == at.t * at.heads_at + i
        value = jnp.where(here, attention_out, jnp.zeros_like(attention_out))
        for k in range(1, depth):
            value = value + at.send_heads(attention_out, i, k, False)
        heads_mine.append(value)
    out_mine = jnp.concatenate(heads_mine, 0)
    out_other = at.send_y(out_mine)

    joint, probs, mixed, near, keep, vec, hb, w_out = call(
        partial(attention_kernel, n_group, d, f, n),
        [
            shape((all_rows, 3 * part), BF),
            shape((TEAM * H // TEAM, n, n), F32),
            shape((all_rows, part), BF),
            shape((2 * n, width), BF),
            shape((2 * n, width), F32),
            shape((8, width), F32),
            shape((1, inner), F32),
            shape((part, width), BF),
        ],
        place,
        *packed,
        first_all,
        out_mine,
        out_other,
        flops=2 * all_rows * width * 4 * part,
        scratch=[pltpu.VMEM((all_rows, width), BF)],
    )
    normed, normed_low, hat, factor = call(
        norm_kernel,
        [
            shape((n, width), F32),
            shape((n, width), BF),
            shape((n, width), F32),
            shape((n, 128), F32),
        ],
        place,
        tokens,
        *at.scatter_team(near, keep),
        vec,
    )

    pre, act, near, keep, normed4 = call(
        partial(feed_kernel, n_group, d),
        [
            shape((all_rows, inner), F32),
            shape((all_rows, inner), BF),
            shape((2 * n, width), BF),
            shape((2 * n, width), F32),
            shape((all_rows, width), BF),
        ],
        place,
        *at.gather_team(normed_low),
        rest_all,
        hb,
        flops=4 * all_rows * width * inner,
    )
    layer_out, d_second, d_out, sums2 = call(
        second_kernel,
        [
            shape((n, width), BF),
            shape((n, width), F32),
            shape((n, width), BF),
            shape((8, width), F32),
        ],
        place,
        normed,
        *at.scatter_team(near, keep),
        vec,
        cotangent,
        packed[0],
    )

    def scatter_group(own, other):
        rows, columns = own.shape[1:]
        keep, *sends = call(
            add_kernel,
            [shape((rows, columns), F32)] + [shape((rows, columns), BF)] * (depth - 1),
            place,
            own,
            at.send_y(other),
        )
        for k, send in enumerate(sends):
            keep = keep + at.send_z(send, -(k + 1)).astype(F32)
        return at.over_copies(keep.astype(BF))

    own, other, d_out4 = call(
        partial(back_grad_kernel, n_group),
        [
            shape((depth, w, width), F32),
            shape((depth, w, width), BF),
            shape((all_rows, width), BF),
        ],
        place,
        *at.gather_team(d_out),
        act,
        flops=2 * all_rows * width * inner,
        scratch=[pltpu.VMEM((2 * w, width), F32)],
    )
    g_back = scatter_group(own, other)
    d_pre, near, keep, d_hb = call(
        partial(feed_back_kernel, n_group, d, n),
        [
            shape((all_rows, inner), BF),
            shape((2 * n, width), BF),
            shape((2 * n, width), F32),
            shape((1, inner), F32),
        ],
        place,
        d_out4,
        rest_all,
        pre,
        flops=4 * all_rows * width * inner,
    )
    own, other = call(
        partial(hidden_grad_kernel, n_group, d),
        [shape((depth, d, inner), F32), shape((depth, d, inner), BF)],
        place,
        normed4,
        d_pre,
        flops=2 * all_rows * width * inner,
        scratch=[pltpu.VMEM((2 * d, inner), F32)],
    )
    g_hidden = scatter_group(own, other)
    d_first, d_attn, sums1 = call(
        norm_back_kernel,
        [shape((n, width), F32), shape((n, width), BF), shape((8, width), F32)],
        place,
        d_second,
        *at.scatter_team(near, keep),
        hat,
        factor,
        vec,
    )
    heads_rows = at.heads_at * d
    d_joint, own, other, out_own, out_sent = call(
        partial(attention_back_kernel, n_group, d, f, n),
        [
            shape((all_rows, 3 * part), BF),
            shape((depth, d + EXTRA, 3 * part), F32),
            shape((depth, d + EXTRA, 3 * part), BF),
            shape((heads_rows, width), F32),
            shape((heads_rows, width), BF),
        ],
        place,
        *at.gather_team(d_attn),
        w_out,
        joint,
        probs,
        mixed,
        *packed,
        sums1,
        sums2,
        d_hb,
        flops=2 * all_rows * width * 5 * part,
        scratch=[
            pltpu.VMEM((all_rows, width), BF),
            pltpu.VMEM((all_rows, width), BF),
            pltpu.VMEM((2 * d, 3 * part), F32),
            pltpu.VMEM((part, width), F32),
            pltpu.VMEM((8, width), F32),
            pltpu.VMEM((n_group, EXTRA, 3 * part), F32),
        ],
    )
    g_joint = scatter_group(own, other)
    near, keep = call(
        partial(token_back_kernel, n_group, d, n),
        [shape((2 * n, width), BF), shape((2 * n, width), F32)],
        place,
        d_joint,
        first_all,
        flops=2 * all_rows * width * 3 * part,
    )
    out_sum = out_own + at.send_y(out_sent).astype(F32)
    g_out = jnp.zeros((d, width), F32)
    for i in range(at.heads_at):
        block = out_sum[i * d : (i + 1) * d]
        low = block.astype(BF)
        here = at.z == at.t * at.heads_at + i
        g_out = g_out + jnp.where(here, block, jnp.zeros_like(block))
        for k in range(1, depth):
            g_out = g_out + at.send_heads(low, i, k, True).astype(F32)
    g_out = at.over_copies(g_out.astype(BF))
    kept, got, far = at.scatter_team(near, keep)
    grad_tokens = d_first + kept[:n] + got[:n].astype(F32) + far.astype(F32)

    g_hidden_out, g_hidden_in = call(
        partial(feed_out_kernel, n_group),
        [shape((f, width), F32), shape((d, TEAM * inner), F32)],
        place,
        *at.gather_team(g_back),
        *at.gather_team(g_hidden),
    )
    g_attention_in, g_attention_out, *g_small = call(
        partial(attention_out_kernel, at.heads_at, f),
        [shape((d, 3 * width), F32), shape((d, width), F32)]
        + [shape((1, d), F32)] * 8
        + [shape((1, f), F32)],
        place,
        *at.gather_team(g_joint),
        *at.gather_team(g_out),
    )
    g_qb, g_vb, g_ob, g_g1, g_s1, g_outb, g_g2, g_s2, g_hb = (v.reshape(-1) for v in g_small)
    return (
        layer_out,
        grad_tokens,
        g_attention_in,
        g_qb,
        g_vb,
        g_attention_out,
        g_ob,
        g_g1,
        g_s1,
        g_hidden_in,
        g_hb,
        g_hidden_out,
        g_outb,
        g_g2,
        g_s2,
    )


def solution(mesh):
    rows = P(("replica", "group"), None)
    matrix = P("group", None)
    vector = P("group")
    params = (
        matrix,
        vector,
        vector,
        matrix,
        vector,
        vector,
        vector,
        matrix,
        vector,
        matrix,
        vector,
        vector,
        vector,
    )
    return jax.shard_map(
        shards,
        mesh=mesh,
        in_specs=(rows, rows, rows) + params,
        out_specs=(rows, rows) + params,
        check_vma=False,
    )
```

```python
from functools import partial

import jax
import jax.numpy as jnp
from jax import lax
from jax.experimental import pallas as pl
from jax.experimental.pallas import tpu as pltpu
from jax.sharding import PartitionSpec as P

H = 16
HD = 64
SEQS = 4
TEAM = 4
EXTRA = 16
PAIR = 2 * HD
BF = jnp.bfloat16
F32 = jnp.float32


class Places:
    def __init__(self):
        self.n_group = lax.axis_size("group")
        self.n_replica = lax.axis_size("replica")
        self.depth = self.n_group // 2
        self.half = self.depth // 2
        self.heads_at = self.depth // TEAM
        place = lax.axis_index("group")
        self.z = place // 2
        self.t = lax.axis_index("replica") % TEAM
        self.place = jnp.stack([self.t, self.z, place % 2]).astype(jnp.int32)

    def send_z(self, value, flip):
        return lax.ppermute(
            value, "group", [(g, g ^ (2 * flip)) for g in range(self.n_group)]
        )

    def send_y(self, value):
        return lax.ppermute(value, "group", [(g, g ^ 1) for g in range(self.n_group)])

    def send_team(self, value, flip):
        return lax.ppermute(value, "replica", [(r, r ^ flip) for r in range(self.n_replica)])

    def send_heads(self, value, at, flip, back):
        pairs = []
        for r in range(self.n_replica):
            home = r % TEAM * self.heads_at + at
            for z in range(self.depth):
                if (z ^ home) & (2 * flip - 1) == 0:
                    for y in range(2):
                        near = r * self.n_group + z * 2 + y
                        pairs.append((near ^ (2 * flip), near) if back else (near, near ^ (2 * flip)))
        return lax.ppermute(value, ("replica", "group"), pairs)

    def steps_down(self, top):
        while top >= 1:
            yield top
            top //= 2

    def other_half(self, blocks):
        return self.send_z(blocks, self.half)

    def gather_team(self, block):
        far = self.send_team(block, 2)
        near = self.send_team(block, 1)
        return [block, near, far, self.send_team(far, 1)]

    def scatter_near(self, near, keep):
        n = near.shape[0] // 2
        got = self.send_team(near, 1)
        return got, (keep[n:] + got[n:].astype(F32)).astype(BF)

    def scatter_team(self, near, keep):
        got, sent = self.scatter_near(near, keep)
        return keep, got, self.send_team(sent, 2)

    def over_copies(self, value):
        teams = self.n_replica // TEAM
        if teams == 1:
            return value
        return lax.psum(
            value,
            "replica",
            axis_index_groups=[
                [team * TEAM + t for team in range(teams)] for t in range(TEAM)
            ],
        )


def call(kernel, outs, place, *args, scratch=(), after=()):
    specs = [pl.BlockSpec(memory_space=pltpu.VMEM)] * len(args)
    body = kernel
    if after:
        read = len(args)
        specs += [pl.BlockSpec(memory_space=pl.ANY)] * len(after)
        args = (*args, *after)

        def body(place, *refs):
            kernel(place, *refs[:read], *refs[read + len(after) :])

    return pl.pallas_call(
        body,
        name=getattr(kernel, "func", kernel).__name__,
        out_shape=outs,
        in_specs=[pl.BlockSpec(memory_space=pltpu.SMEM)] + specs,
        out_specs=[pl.BlockSpec(memory_space=pltpu.VMEM)] * len(outs),
        scratch_shapes=list(scratch),
        compiler_params=pltpu.CompilerParams(vmem_limit_bytes=32 << 20),
        cost_estimate=pl.CostEstimate(flops=0, bytes_accessed=0, transcendentals=0),
    )(place, *args)


def shape(dims, dtype):
    return jax.ShapeDtypeStruct(tuple(dims), dtype)


def times(left, right):
    return jnp.dot(left, right, preferred_element_type=F32)


def against(left, weight):
    return lax.dot_general(left, weight, (((1,), (1,)), ((), ())), preferred_element_type=F32)


def outer(left, right):
    return lax.dot_general(left, right, (((0,), (0,)), ((), ())), preferred_element_type=F32)


def chosen(index, cases):
    result = cases[-1]
    for at in range(len(cases) - 2, -1, -1):
        result = jnp.where(index == at, cases[at], result)
    return result


def of_member(t, member, blocks):
    return chosen(t, [blocks[i ^ member] for i in range(TEAM)])


def column_sum(value):
    return jnp.sum(value, 0, keepdims=True)


def ends_of(block, n):
    row = block[n : n + EXTRA, 0:128].astype(F32)[0:1]
    lane = lax.broadcasted_iota(jnp.int32, (1, 128), 1)
    return [
        jnp.sum(jnp.where(lane <= s, row, 0.0), axis=1, keepdims=True) for s in range(SEQS)
    ]


def segments(ends, dims, axis):
    place = lax.broadcasted_iota(jnp.int32, dims, axis).astype(F32)
    total = jnp.zeros(dims, F32)
    for end in ends:
        total = total + jnp.where(place >= end, 1.0, 0.0)
    return total


def normalise(value):
    centre = jnp.mean(value, -1, keepdims=True)
    offset = value - centre
    spread = jnp.mean(offset * offset, -1, keepdims=True)
    factor = lax.rsqrt(spread + 1e-06)
    return offset * factor, factor


def normalise_back(d_hat, hat, factor):
    return factor * (
        d_hat
        - jnp.mean(d_hat, -1, keepdims=True)
        - hat * jnp.mean(d_hat * hat, -1, keepdims=True)
    )


def grad_tiles(place, n_group, width, left, right, own, near, far, tile):
    depth = n_group // 2
    half = depth // 2
    z, y = place[1], place[2]

    def step(at, carry):
        tile[...] = outer(left[:, pl.ds(pl.multiple_of(at * 2 * width, 2 * width), 2 * width)], right[...])
        k = lax.bitwise_xor(z, at)
        own[k, 0:width, :] = tile[pl.ds(pl.multiple_of(y * width, width), width), :]
        sent = tile[pl.ds(pl.multiple_of((1 - y) * width, width), width), :].astype(BF)

        @pl.when(k < half)
        def _():
            near[k, 0:width, :] = sent

        @pl.when(k >= half)
        def _():
            far[k - half, 0:width, :] = sent

        return carry

    lax.fori_loop(0, depth, step, 0)


def to_team(value, n, near, keep, columns):
    keep[0:n, columns] = value[0:n]
    near[0:n, columns] = value[n : 2 * n].astype(BF)
    keep[n : 2 * n, columns] = value[2 * n : 3 * n]
    near[n : 2 * n, columns] = value[3 * n : 4 * n].astype(BF)


def at_group(place, n_group, i):
    depth = n_group // 2
    dy, k = divmod(i, depth)
    y = place[2]
    return lax.rem(place[1] - k + depth, depth) * 2 + (y if dy == 0 else 1 - y)


def relay_kernel(counts, place, *refs):
    outs = refs[sum(counts) :]
    for out, count in zip(outs, counts):
        parts, refs = refs[:count], refs[count:]
        at = 0
        for part in parts:
            out[at : at + part.shape[0]] = part[...]
            at += part.shape[0]


def relay(place, *tasks, after=()):
    outs = [
        shape((sum(part.shape[0] for part in task), *task[0].shape[1:]), task[0].dtype)
        for task in tasks
    ]
    flat = [part for task in tasks for part in task]
    return call(
        partial(relay_kernel, [len(task) for task in tasks]), outs, place, *flat, after=after
    )


def group_blocks(place, quarters):
    half = quarters[0].shape[0]
    for q, quarter in enumerate(quarters):
        for i in range(half):
            dz, dy = q % 2 * half + i, q // 2
            z = lax.bitwise_xor(place[1], dz)
            yield z * 2 + lax.bitwise_xor(place[2], dy), quarter.at[i]


def assemble(place, quarters, rows, whole):
    for g, block in group_blocks(place, quarters):
        whole[pl.ds(pl.multiple_of(g * rows, rows), rows), :] = block[0:rows]


def prepare_first_kernel(place, att, small, first_o):
    t = place[0]
    d, joint = att.shape
    width = joint // 3
    part = width // TEAM
    for i in range(3):
        first_o[0, 0:d, i * part : (i + 1) * part] = chosen(
            t,
            [
                att[:, i * width + s * part : i * width + (s + 1) * part]
                for s in range(TEAM)
            ],
        )
    first_o[0, d : d + EXTRA, :] = small[...]


def prepare_rest_kernel(n_group, place, hid, back, rest_o):
    t = place[0]
    d = hid.shape[0]
    f = hid.shape[1] // n_group
    w = f // TEAM
    for g in range(n_group):
        rest_o[0:d, g * w : (g + 1) * w] = chosen(
            t, [hid[:, g * f + s * w : g * f + (s + 1) * w] for s in range(TEAM)]
        )
    rest_o[d : d + w, :] = back[pl.ds(pl.multiple_of(t * w, w), w), :]


def attention_kernel(
    n_group, d, f, n, place, p0, p1, p2, p3, own_out, other_out, *refs
):
    first, refs = refs[:4], refs[4:]
    (
        joint_o, probs_o, mixed_o, near_o, keep_o, vec_o, hb_o, wout_o, wfirst_o, token_s, small_s,
    ) = refs
    blocks = (p0, p1, p2, p3)
    t, y = place[0], place[2]
    part = wout_o.shape[0]
    width = wout_o.shape[1]
    w = f // TEAM
    assemble(place, first, d, wfirst_o)
    for g, block in group_blocks(place, first):
        small_s[g] = block[d : d + EXTRA, :].astype(F32)
    small = [small_s[g] for g in range(n_group)]
    vec_o[...] = jnp.concatenate([s[0:8, 0:d] for s in small], 1)
    hb_o[...] = jnp.concatenate(
        [chosen(t, [s[8:9, i * w : (i + 1) * w] for i in range(TEAM)]) for s in small], 1
    )
    for at in range(part // (2 * d)):
        wout_o[pl.ds(pl.multiple_of((at * 2 + y) * d, d), d), :] = own_out[
            at * d : (at + 1) * d
        ]
        wout_o[pl.ds(pl.multiple_of((at * 2 + 1 - y) * d, d), d), :] = other_out[
            at * d : (at + 1) * d
        ]
    for b in range(TEAM):
        token_s[b * n : (b + 1) * n] = blocks[b][0:n]
    mine = pl.ds(pl.multiple_of(t * part, part), part)
    for i in range(3):
        value = times(token_s[...], wfirst_o[:, i * part : (i + 1) * part])
        if i == 0:
            value = value + vec_o[0:1, mine]
        if i == 2:
            value = value + vec_o[1:2, mine]
        joint_o[:, i * part : (i + 1) * part] = value.astype(BF)
    scale = HD ** (-0.5)
    low = lax.broadcasted_iota(jnp.int32, (1, PAIR), 1) < HD
    zero = jnp.zeros((), BF)
    for b in range(TEAM):
        rows = slice(b * n, (b + 1) * n)
        ends = ends_of(blocks[b], n)
        same = segments(ends, (n, 1), 0) == segments(ends, (1, n), 1)
        for pair in range(part // PAIR):
            at = pair * PAIR
            query = joint_o[rows, at : at + PAIR]
            keys = joint_o[rows, part + at : part + at + PAIR]
            values = joint_o[rows, 2 * part + at : 2 * part + at + PAIR]
            mixed = []
            for h in range(2):
                sided = jnp.where(low, query, zero) if h == 0 else jnp.where(low, zero, query)
                scores = jnp.where(same, against(sided, keys) * scale, -1000000000.0)
                expo = jnp.exp(scores - jnp.max(scores, -1, keepdims=True))
                probs = expo / jnp.sum(expo, -1, keepdims=True)
                probs_o[(b * (part // PAIR) + pair) * 2 + h] = probs
                mixed.append(times(probs.astype(BF), values))
            mixed_o[rows, at : at + PAIR] = jnp.where(low, mixed[0], mixed[1]).astype(BF)
    for at in range(0, width, part):
        columns = slice(at, at + part)
        to_team(times(mixed_o[...], wout_o[:, columns]), n, near_o, keep_o, columns)


def norm_kernel(place, tokens, keep, got, far, vec, normed_o, low_o, hat_o, factor_o):
    n = tokens.shape[0]
    attn = keep[0:n] + got[0:n].astype(F32) + far[...].astype(F32) + vec[2:3]
    hat, factor = normalise(tokens[...].astype(F32) + attn)
    normed = hat * vec[3:4] + vec[4:5]
    normed_o[...] = normed
    low_o[...] = normed.astype(BF)
    hat_o[...] = hat
    factor_o[...] = jnp.broadcast_to(factor, factor_o.shape)


def gelu_parts(pre):
    bell = 0.5 * (1.0 + lax.erf(pre * (2.0**-0.5)))
    return bell, jnp.exp(-0.5 * pre * pre) * (2.0 * 3.141592653589793) ** -0.5


def feed_kernel(
    n_group, d, place, x0, x1, x2, x3, hb, rest, pre_o, act_o, near_o, keep_o, x_o
):
    n = x0.shape[0]
    w = rest.shape[1] - d
    for b, block in enumerate((x0, x1, x2, x3)):
        x_o[b * n : (b + 1) * n] = block[...]

    def entering(at, carry):
        columns = pl.ds(pl.multiple_of(at * 256, 256), 256)
        weight = rest[:, 0:d, columns].reshape(n_group * d, 256)
        pre = times(x_o[...], weight) + hb[:, columns]
        pre_o[:, columns] = pre
        act_o[:, columns] = (pre * gelu_parts(pre)[0]).astype(BF)
        return carry

    lax.fori_loop(0, pre_o.shape[1] // 256, entering, 0)

    def leaving(at, carry):
        columns = pl.ds(pl.multiple_of(at * 256, 256), 256)
        weight = rest[:, d : d + w, columns].reshape(n_group * w, 256)
        to_team(times(act_o[...], weight), n, near_o, keep_o, columns)
        return carry

    lax.fori_loop(0, keep_o.shape[1] // 256, leaving, 0)


def second_kernel(
    place, normed, keep, got, far, vec, cotangent, packed, layer_o, d_second_o, d_out_o, sums_o
):
    n = normed.shape[0]
    out = keep[0:n] + got[0:n].astype(F32) + far[...].astype(F32) + vec[5:6]
    hat, factor = normalise(normed[...] + out)
    live = jnp.where(segments(ends_of(packed, n), (n, 1), 0) < SEQS, 1.0, 0.0)
    layer_o[...] = ((hat * vec[6:7] + vec[7:8]) * live).astype(BF)
    d_final = cotangent[...].astype(F32) * live
    d_second = normalise_back(d_final * vec[6:7], hat, factor)
    d_second_o[...] = d_second
    d_out = d_second.astype(BF)
    d_out_o[...] = d_out
    sums_o[...] = jnp.zeros_like(sums_o)
    sums_o[0:1] = column_sum(d_out.astype(F32))
    sums_o[1:2] = column_sum(d_final * hat)
    sums_o[2:3] = column_sum(d_final)


def back_grad_kernel(place, d0, d1, d2, d3, act, grad_o, d_out_o):
    n = d0.shape[0]
    for b, block in enumerate((d0, d1, d2, d3)):
        d_out_o[b * n : (b + 1) * n] = block[...]

    def step(at, carry):
        rows = pl.ds(pl.multiple_of(at * 256, 256), 256)
        grad_o[rows, :] = outer(act[:, rows], d_out_o[...]).astype(BF)
        return carry

    lax.fori_loop(0, grad_o.shape[0] // 256, step, 0)


def feed_back_kernel(n_group, d, n, place, d_out, rest, pre, d_pre_o, near_o, keep_o, hb_o):
    w = rest.shape[1] - d
    per = 256 // w

    def through(at, carry):
        columns = pl.ds(pl.multiple_of(at * 256, 256), 256)
        weight = rest[pl.ds(at * per, per), d : d + w, :].reshape(256, rest.shape[2])
        d_act = against(d_out[...], weight)
        value = pre[:, columns]
        bell, slope = gelu_parts(value)
        d_pre = (d_act * (bell + value * slope)).astype(BF)
        d_pre_o[:, columns] = d_pre
        hb_o[:, columns] = column_sum(d_pre.astype(F32))
        return carry

    lax.fori_loop(0, pre.shape[1] // 256, through, 0)
    rows = 256 // d

    def entering(at, carry):
        columns = pl.ds(pl.multiple_of(at * 256, 256), 256)
        weight = rest[pl.ds(at * rows, rows), 0:d, :].reshape(256, rest.shape[2])
        to_team(against(d_pre_o[...], weight), n, near_o, keep_o, columns)
        return carry

    lax.fori_loop(0, keep_o.shape[1] // 256, entering, 0)


def hidden_grad_kernel(n_group, d, place, x, d_pre, own_o, near_o, far_o, tile):
    grad_tiles(place, n_group, d, x, d_pre, own_o, near_o, far_o, tile)


def norm_back_kernel(
    place, d_second, keep, got, far, hat, factor, vec, d_first_o, d_attn_o, sums_o
):
    n = d_second.shape[0]
    d_normed = d_second[...] + keep[0:n] + got[0:n].astype(F32) + far[...].astype(F32)
    d_first = normalise_back(d_normed * vec[3:4], hat[...], factor[:, 0:1])
    d_first_o[...] = d_first
    d_attn = d_first.astype(BF)
    d_attn_o[...] = d_attn
    sums_o[...] = jnp.zeros_like(sums_o)
    sums_o[0:1] = column_sum(d_attn.astype(F32))
    sums_o[1:2] = column_sum(d_normed * hat[...])
    sums_o[2:3] = column_sum(d_normed)


def attention_back_kernel(
    n_group, d, f, n, place, a0, a1, a2, a3, wout, joint, probs_in, mixed, p0, p1, p2, p3,
    sums1, sums2, d_hb,
    d_joint_o, own_o, near_o, far_o, out_own_o, out_other_o, token_s, attn_s, tile, heads_s, vec_s,
    small_s,
):
    t, z, y = place[0], place[1], place[2]
    depth = n_group // 2
    part, width = wout.shape
    w = f // TEAM
    for b in range(TEAM):
        token_s[b * n : (b + 1) * n] = (p0, p1, p2, p3)[b][0:n]
        attn_s[b * n : (b + 1) * n] = (a0, a1, a2, a3)[b][...]
    heads_s[...] = outer(mixed[...], attn_s[...])
    for at in range(part // (2 * d)):
        out_own_o[at * d : (at + 1) * d] = heads_s[
            pl.ds(pl.multiple_of((at * 2 + y) * d, d), d), :
        ]
        out_other_o[at * d : (at + 1) * d] = heads_s[
            pl.ds(pl.multiple_of((at * 2 + 1 - y) * d, d), d), :
        ].astype(BF)
    d_mixed = against(attn_s[...], wout[...]).astype(BF)
    scale = HD ** (-0.5)
    low = lax.broadcasted_iota(jnp.int32, (1, PAIR), 1) < HD
    zero = jnp.zeros((), BF)
    for b in range(TEAM):
        rows = slice(b * n, (b + 1) * n)
        for pair in range(part // PAIR):
            at = pair * PAIR
            query = joint[rows, at : at + PAIR]
            keys = joint[rows, part + at : part + at + PAIR]
            values = joint[rows, 2 * part + at : 2 * part + at + PAIR]
            d_mix = d_mixed[rows, at : at + PAIR]
            d_query, d_keys, d_values = [], [], []
            for h in range(2):
                probs = probs_in[(b * (part // PAIR) + pair) * 2 + h]
                sided = jnp.where(low, d_mix, zero) if h == 0 else jnp.where(low, zero, d_mix)
                d_probs = against(sided, values)
                d_scores = (
                    probs * (d_probs - jnp.sum(probs * d_probs, -1, keepdims=True))
                ).astype(BF)
                d_values.append(outer(probs.astype(BF), d_mix))
                d_query.append(times(d_scores, keys))
                d_keys.append(outer(d_scores, query))
            for i, (value, factor) in enumerate(
                ((d_query, scale), (d_keys, scale), (d_values, 1.0))
            ):
                d_joint_o[rows, i * part + at : i * part + at + PAIR] = (
                    jnp.where(low, value[0], value[1]) * factor
                ).astype(BF)
    vec_s[...] = jnp.zeros_like(vec_s)
    mine = pl.ds(pl.multiple_of(t * part, part), part)
    vec_s[0:1, mine] = column_sum(d_joint_o[:, 0:part].astype(F32))
    vec_s[1:2, mine] = column_sum(d_joint_o[:, 2 * part : 3 * part].astype(F32))
    vec_s[2:5, :] = sums1[0:3]
    vec_s[5:8, :] = sums2[0:3]
    small_s[...] = jnp.zeros_like(small_s)
    for g in range(n_group):
        small_s[g, 0:8, 0:d] = vec_s[:, g * d : (g + 1) * d]
        row = d_hb[:, g * w : (g + 1) * w]
        small_s[g, 8:9, 0:f] = jnp.concatenate(
            [jnp.where(t == i, row, jnp.zeros_like(row)) for i in range(TEAM)], 1
        )
    grad_tiles(place, n_group, d, token_s, d_joint_o, own_o, near_o, far_o, tile)
    for k in range(depth):
        g = lax.bitwise_xor(z, k) * 2
        own_o[k, d : d + EXTRA, :] = small_s[g + y]
        sent = small_s[g + 1 - y].astype(BF)
        if k < depth // 2:
            near_o[k, d : d + EXTRA, :] = sent
        else:
            far_o[k - depth // 2, d : d + EXTRA, :] = sent


def token_back_kernel(n, place, d_joint, first, near_o, keep_o):
    def step(at, carry):
        columns = pl.ds(pl.multiple_of(at * 256, 256), 256)
        to_team(against(d_joint[...], first[columns, :]), n, near_o, keep_o, columns)
        return carry

    lax.fori_loop(0, keep_o.shape[1] // 256, step, 0)


def add_far_kernel(place, own, got, sum_o):
    half = sum_o.shape[0]
    sum_o[...] = (own[half : 2 * half] + got[0:half].astype(F32)).astype(BF)


def add_near_kernel(place, own, got, far, keep_o, send_o):
    half = far.shape[0]
    total = own[0:half] + got[got.shape[0] - half :].astype(F32) + far[...].astype(F32)
    keep_o[...] = total[0 : half // 2]
    send_o[...] = total[half // 2 :].astype(BF)


def back_out_kernel(place, b0, b1, b2, b3, back_o):
    w = b0.shape[0]
    for i in range(TEAM):
        block = of_member(place[0], i, [b[...] for b in (b0, b1, b2, b3)])
        back_o[i * w : (i + 1) * w] = block.astype(F32)


def hidden_out_kernel(n_group, place, h0, h1, h2, h3, hidden_o):
    w = h0.shape[1] // n_group
    for i in range(TEAM):
        block = of_member(place[0], i, [h[...] for h in (h0, h1, h2, h3)]).astype(F32)
        for g in range(n_group):
            at = (g * TEAM + i) * w
            hidden_o[:, at : at + w] = block[:, g * w : (g + 1) * w]


def attention_out_kernel(
    heads_at, f, place, j0, j1, j2, j3, o0, o1, o2, o3, joint_o, out_o, *small_o
):
    t, z = place[0], place[1]
    d = out_o.shape[0]
    part = j0.shape[1] // 3
    width = part * TEAM
    total = jnp.zeros((EXTRA, 3 * part), F32)
    for i in range(TEAM):
        block = of_member(t, i, [j[...] for j in (j0, j1, j2, j3)]).astype(F32)
        for s in range(3):
            at = s * width + i * part
            joint_o[:, at : at + part] = block[0:d, s * part : (s + 1) * part]
        total = total + block[d : d + EXTRA]
    outs = [o[...] for o in (o0, o1, o2, o3)]
    out = of_member(t, TEAM - 1, outs)
    for i in range(TEAM - 1):
        out = jnp.where(z // heads_at == i, of_member(t, i, outs), out)
    out_o[...] = out.astype(F32)
    for i in range(8):
        small_o[i][...] = total[i : i + 1, 0:d]
    small_o[8][...] = total[8:9, 0:f]


def shards(
    tokens,
    lengths,
    cotangent,
    attention_in,
    query_bias,
    value_bias,
    attention_out,
    out_bias,
    first_gain,
    first_shift,
    hidden_in,
    hidden_bias,
    hidden_out,
    output_bias,
    second_gain,
    second_shift,
):
    at = Places()
    n_group, depth, place = at.n_group, at.depth, at.place
    n, width = tokens.shape
    d = attention_in.shape[0]
    f = hidden_bias.shape[0]
    w = f // TEAM
    part = width // TEAM
    inner = w * n_group
    all_rows = TEAM * n

    vectors = (
        query_bias,
        value_bias,
        out_bias,
        first_gain,
        first_shift,
        output_bias,
        second_gain,
        second_shift,
    )
    small = jnp.concatenate(
        [
            jnp.pad(jnp.stack(vectors), ((0, 0), (0, 3 * part - d))),
            jnp.pad(hidden_bias[None], ((0, EXTRA - 9), (0, 3 * part - f))),
        ],
        0,
    )
    extra = jnp.pad(lengths.astype(BF), ((0, EXTRA - 1), (0, width - lengths.shape[1])))
    packed = jnp.concatenate([tokens, extra], 0)
    (first_near,) = call(
        prepare_first_kernel,
        [shape((1, d + EXTRA, 3 * part), BF)],
        place,
        attention_in,
        small,
    )
    (rest_mine,) = call(
        partial(prepare_rest_kernel, n_group),
        [shape((d + w, width), BF)],
        place,
        hidden_in,
        hidden_out,
    )
    rest_all = lax.all_gather(rest_mine, "group", axis=0)

    def widen(blocks):
        for flip in list(at.steps_down(at.half // 2))[::-1]:
            blocks = (blocks, at.send_z(blocks, flip))
            if flip < at.half // 2:
                (blocks,) = relay(place, blocks)
        return blocks

    heads_mine = []
    for i in range(at.heads_at):
        home = at.t * at.heads_at + i
        value = jnp.where(at.z == home, attention_out, jnp.zeros_like(attention_out))
        for flip in at.steps_down(at.half):
            value = value + at.send_heads(value, i, flip, False)
        heads_mine.append(value)
    out_mine = jnp.concatenate(heads_mine, 0)

    packed = at.gather_team(packed)
    (first_near,) = relay(place, widen(first_near))
    first_far = at.other_half(first_near)
    first_all = [first_near, first_far, at.send_y(first_near), at.send_y(first_far)]
    out_other = at.send_y(out_mine)

    joint, probs, mixed, near, keep, vec, hb, w_out, w_first = call(
        partial(attention_kernel, n_group, d, f, n),
        [
            shape((all_rows, 3 * part), BF),
            shape((TEAM * H // TEAM, n, n), F32),
            shape((all_rows, part), BF),
            shape((2 * n, width), BF),
            shape((2 * n, width), F32),
            shape((8, width), F32),
            shape((1, inner), F32),
            shape((part, width), BF),
            shape((width, 3 * part), BF),
        ],
        place,
        *packed,
        out_mine,
        out_other,
        *first_all,
        scratch=[
            pltpu.VMEM((all_rows, width), BF),
            pltpu.VMEM((n_group, EXTRA, 3 * part), F32),
        ],
    )
    normed, normed_low, hat, factor = call(
        norm_kernel,
        [
            shape((n, width), F32),
            shape((n, width), BF),
            shape((n, width), F32),
            shape((n, 128), F32),
        ],
        place,
        tokens,
        *at.scatter_team(near, keep),
        vec,
    )

    pre, act, near, keep, normed4 = call(
        partial(feed_kernel, n_group, d),
        [
            shape((all_rows, inner), F32),
            shape((all_rows, inner), BF),
            shape((2 * n, width), BF),
            shape((2 * n, width), F32),
            shape((all_rows, width), BF),
        ],
        place,
        *at.gather_team(normed_low),
        hb,
        rest_all,
    )
    layer_out, d_second, d_out, sums2 = call(
        second_kernel,
        [
            shape((n, width), BF),
            shape((n, width), F32),
            shape((n, width), BF),
            shape((8, width), F32),
        ],
        place,
        normed,
        *at.scatter_team(near, keep),
        vec,
        cotangent,
        packed[0],
    )

    def add_far(own, came, after=()):
        half, rest = own.shape[0] // 2, own.shape[1:]
        return call(add_far_kernel, [shape((half, *rest), BF)], place, own, came, after=after)[0]

    def add_near(own, came_y, came_z, after=()):
        half, *rest = came_z.shape
        return call(
            add_near_kernel,
            [shape((half // 2, *rest), F32), shape((half // 2, *rest), BF)],
            place,
            own,
            came_y,
            came_z,
            after=after,
        )

    def sum_group(keep, send):
        flip = at.half // 2
        while flip > 1:
            total = keep + at.send_z(send, flip).astype(F32)
            flip //= 2
            keep, send = total[:flip], total[flip:].astype(BF)
        return at.over_copies((keep + at.send_z(send, 1).astype(F32))[0].astype(BF))

    half = depth // 2
    grad_back, d_out4 = call(
        back_grad_kernel,
        [shape((inner, width), BF), shape((all_rows, width), BF)],
        place,
        *at.gather_team(d_out),
        act,
    )
    g_back = at.over_copies(
        lax.psum_scatter(grad_back, "group", scatter_dimension=0, tiled=True)
    )
    d_pre, near, keep, d_hb = call(
        partial(feed_back_kernel, n_group, d, n),
        [
            shape((all_rows, inner), BF),
            shape((2 * n, width), BF),
            shape((2 * n, width), F32),
            shape((1, inner), F32),
        ],
        place,
        d_out4,
        rest_all,
        pre,
    )
    own_hidden, near_hidden, far_hidden = call(
        partial(hidden_grad_kernel, n_group, d),
        [shape((depth, d, inner), F32)] + [shape((half, d, inner), BF)] * 2,
        place,
        normed4,
        d_pre,
        scratch=[pltpu.VMEM((2 * d, inner), F32)],
    )
    d_first, d_attn, sums1 = call(
        norm_back_kernel,
        [shape((n, width), F32), shape((n, width), BF), shape((8, width), F32)],
        place,
        d_second,
        *at.scatter_team(near, keep),
        hat,
        factor,
        vec,
        after=[far_hidden],
    )
    heads_rows = at.heads_at * d
    d_joint, own_joint, near_joint, far_joint, out_own, out_sent = call(
        partial(attention_back_kernel, n_group, d, f, n),
        [
            shape((all_rows, 3 * part), BF),
            shape((depth, d + EXTRA, 3 * part), F32),
            shape((half, d + EXTRA, 3 * part), BF),
            shape((half, d + EXTRA, 3 * part), BF),
            shape((heads_rows, width), F32),
            shape((heads_rows, width), BF),
        ],
        place,
        *at.gather_team(d_attn),
        w_out,
        joint,
        probs,
        mixed,
        *packed,
        sums1,
        sums2,
        d_hb,
        scratch=[
            pltpu.VMEM((all_rows, width), BF),
            pltpu.VMEM((all_rows, width), BF),
            pltpu.VMEM((2 * d, 3 * part), F32),
            pltpu.VMEM((part, width), F32),
            pltpu.VMEM((8, width), F32),
            pltpu.VMEM((n_group, EXTRA, 3 * part), F32),
        ],
    )
    sent_hidden = add_far(own_hidden, at.send_y(far_hidden))
    came_hidden = at.other_half(sent_hidden)
    near, keep = call(
        partial(token_back_kernel, n),
        [shape((2 * n, width), BF), shape((2 * n, width), F32)],
        place,
        d_joint,
        w_first,
    )
    kept, got, far = at.scatter_team(near, keep)
    sent_joint = add_far(own_joint, at.send_y(far_joint))
    came_joint = at.other_half(sent_joint)
    hidden_parts = add_near(own_hidden, at.send_y(near_hidden), came_hidden, [sent_joint])
    g_hidden = sum_group(*hidden_parts)
    out_sum = out_own + at.send_y(out_sent).astype(F32)
    g_out = jnp.zeros((d, width), F32)
    for i in range(at.heads_at):
        block = out_sum[i * d : (i + 1) * d]
        flips = list(at.steps_down(at.half))[::-1]
        for flip in flips:
            block = block + at.send_heads(block.astype(BF), i, flip, True).astype(F32)
        here = at.z == at.t * at.heads_at + i
        g_out = g_out + jnp.where(here, block, jnp.zeros_like(block))
    g_out = at.over_copies(g_out.astype(BF))
    joint_parts = add_near(
        own_joint, at.send_y(near_joint), came_joint, [g_hidden, far]
    )
    g_joint = sum_group(*joint_parts)
    grad_tokens = d_first + kept[:n] + got[:n].astype(F32) + far.astype(F32)

    (g_hidden_out,) = call(
        back_out_kernel, [shape((f, width), F32)], place, *at.gather_team(g_back)
    )
    (g_hidden_in,) = call(
        partial(hidden_out_kernel, n_group),
        [shape((d, TEAM * inner), F32)],
        place,
        *at.gather_team(g_hidden),
    )
    g_attention_in, g_attention_out, *g_small = call(
        partial(attention_out_kernel, at.heads_at, f),
        [shape((d, 3 * width), F32), shape((d, width), F32)]
        + [shape((1, d), F32)] * 8
        + [shape((1, f), F32)],
        place,
        *at.gather_team(g_joint),
        *at.gather_team(g_out),
    )
    g_qb, g_vb, g_ob, g_g1, g_s1, g_outb, g_g2, g_s2, g_hb = (v.reshape(-1) for v in g_small)
    return (
        layer_out,
        grad_tokens,
        g_attention_in,
        g_qb,
        g_vb,
        g_attention_out,
        g_ob,
        g_g1,
        g_s1,
        g_hidden_in,
        g_hb,
        g_hidden_out,
        g_outb,
        g_g2,
        g_s2,
    )


def solution(mesh):
    rows = P(("replica", "group"), None)
    matrix = P("group", None)
    vector = P("group")
    params = (
        matrix,
        vector,
        vector,
        matrix,
        vector,
        vector,
        vector,
        matrix,
        vector,
        matrix,
        vector,
        vector,
        vector,
    )
    return jax.shard_map(
        shards,
        mesh=mesh,
        in_specs=(rows, rows, rows) + params,
        out_specs=(rows, rows) + params,
        check_vma=False,
    )
```

```python
from functools import partial

import jax
import jax.numpy as jnp
from jax import lax
from jax.experimental import pallas as pl
from jax.experimental.pallas import tpu as pltpu
from jax.sharding import PartitionSpec as P

H = 16
HD = 64
SEQS = 4
TEAM = 4
EXTRA = 16
PAIR = 2 * HD
BF = jnp.bfloat16
F32 = jnp.float32


class Places:
    def __init__(self):
        self.n_group = lax.axis_size("group")
        self.n_replica = lax.axis_size("replica")
        self.depth = self.n_group // 2
        self.half = self.depth // 2
        self.heads_at = self.depth // TEAM
        place = lax.axis_index("group")
        self.z = place // 2
        self.t = lax.axis_index("replica") % TEAM
        self.place = jnp.stack([self.t, self.z, place % 2]).astype(jnp.int32)

    def send_z(self, value, flip):
        return lax.ppermute(
            value, "group", [(g, g ^ (2 * flip)) for g in range(self.n_group)]
        )

    def send_y(self, value):
        return lax.ppermute(value, "group", [(g, g ^ 1) for g in range(self.n_group)])

    def send_team(self, value, flip):
        return lax.ppermute(value, "replica", [(r, r ^ flip) for r in range(self.n_replica)])

    def send_heads(self, value, at, flip, back):
        pairs = []
        for r in range(self.n_replica):
            home = r % TEAM * self.heads_at + at
            for z in range(self.depth):
                if (z ^ home) & (2 * flip - 1) == 0:
                    for y in range(2):
                        near = r * self.n_group + z * 2 + y
                        pairs.append((near ^ (2 * flip), near) if back else (near, near ^ (2 * flip)))
        return lax.ppermute(value, ("replica", "group"), pairs)

    def steps_down(self, top):
        while top >= 1:
            yield top
            top //= 2

    def other_half(self, blocks):
        return self.send_z(blocks, self.half)

    def gather_team(self, block):
        far = self.send_team(block, 2)
        near = self.send_team(block, 1)
        return [block, near, far, self.send_team(far, 1)]

    def scatter_near(self, near, keep):
        n = near.shape[0] // 2
        got = self.send_team(near, 1)
        return got, (keep[n:] + got[n:].astype(F32)).astype(BF)

    def scatter_team(self, near, keep):
        got, sent = self.scatter_near(near, keep)
        return keep, got, self.send_team(sent, 2)

    def over_copies(self, value):
        teams = self.n_replica // TEAM
        if teams == 1:
            return value
        return lax.psum(
            value,
            "replica",
            axis_index_groups=[
                [team * TEAM + t for team in range(teams)] for t in range(TEAM)
            ],
        )


def call(kernel, outs, place, *args, scratch=(), after=()):
    specs = [pl.BlockSpec(memory_space=pltpu.VMEM)] * len(args)
    body = kernel
    if after:
        read = len(args)
        specs += [pl.BlockSpec(memory_space=pl.ANY)] * len(after)
        args = (*args, *after)

        def body(place, *refs):
            kernel(place, *refs[:read], *refs[read + len(after) :])

    return pl.pallas_call(
        body,
        name=getattr(kernel, "func", kernel).__name__,
        out_shape=outs,
        in_specs=[pl.BlockSpec(memory_space=pltpu.SMEM)] + specs,
        out_specs=[pl.BlockSpec(memory_space=pltpu.VMEM)] * len(outs),
        scratch_shapes=list(scratch),
        compiler_params=pltpu.CompilerParams(vmem_limit_bytes=16 << 20),
        cost_estimate=pl.CostEstimate(flops=0, bytes_accessed=0, transcendentals=0),
    )(place, *args)


def shape(dims, dtype):
    return jax.ShapeDtypeStruct(tuple(dims), dtype)


def times(left, right):
    return jnp.dot(left, right, preferred_element_type=F32)


def against(left, weight):
    return lax.dot_general(left, weight, (((1,), (1,)), ((), ())), preferred_element_type=F32)


def outer(left, right):
    return lax.dot_general(left, right, (((0,), (0,)), ((), ())), preferred_element_type=F32)


def chosen(index, cases):
    result = cases[-1]
    for at in range(len(cases) - 2, -1, -1):
        result = jnp.where(index == at, cases[at], result)
    return result


def of_member(t, member, blocks):
    return chosen(t, [blocks[i ^ member] for i in range(TEAM)])


def column_sum(value):
    return jnp.sum(value, 0, keepdims=True)


def ends_of(block, n):
    row = block[n : n + EXTRA, 0:128].astype(F32)[0:1]
    lane = lax.broadcasted_iota(jnp.int32, (1, 128), 1)
    return [
        jnp.sum(jnp.where(lane <= s, row, 0.0), axis=1, keepdims=True) for s in range(SEQS)
    ]


def segments(ends, dims, axis):
    place = lax.broadcasted_iota(jnp.int32, dims, axis).astype(F32)
    total = jnp.zeros(dims, F32)
    for end in ends:
        total = total + jnp.where(place >= end, 1.0, 0.0)
    return total


def normalise(value):
    centre = jnp.mean(value, -1, keepdims=True)
    offset = value - centre
    spread = jnp.mean(offset * offset, -1, keepdims=True)
    factor = lax.rsqrt(spread + 1e-06)
    return offset * factor, factor


def normalise_back(d_hat, hat, factor):
    return factor * (
        d_hat
        - jnp.mean(d_hat, -1, keepdims=True)
        - hat * jnp.mean(d_hat * hat, -1, keepdims=True)
    )


def grad_tiles(place, n_group, width, left, right, own, sent, tile):
    depth = n_group // 2
    z, y = place[1], place[2]

    def step(at, carry):
        tile[...] = outer(left[:, pl.ds(pl.multiple_of(at * 2 * width, 2 * width), 2 * width)], right[...])
        k = lax.bitwise_xor(z, at)
        own[k, 0:width, :] = tile[pl.ds(pl.multiple_of(y * width, width), width), :]
        sent[lax.bitwise_xor(k, depth // 2), 0:width, :] = tile[
            pl.ds(pl.multiple_of((1 - y) * width, width), width), :
        ].astype(BF)
        return carry

    lax.fori_loop(0, depth, step, 0)


def to_team(value, n, near, keep, columns):
    keep[0:n, columns] = value[0:n]
    near[0:n, columns] = value[n : 2 * n].astype(BF)
    keep[n : 2 * n, columns] = value[2 * n : 3 * n]
    near[n : 2 * n, columns] = value[3 * n : 4 * n].astype(BF)


def at_group(place, n_group, i):
    depth = n_group // 2
    dy, k = divmod(i, depth)
    y = place[2]
    return lax.rem(place[1] - k + depth, depth) * 2 + (y if dy == 0 else 1 - y)


def relay_kernel(counts, place, *refs):
    outs = refs[sum(counts) :]
    for out, count in zip(outs, counts):
        parts, refs = refs[:count], refs[count:]
        at = 0
        for part in parts:
            out[at : at + part.shape[0]] = part[...]
            at += part.shape[0]


def relay(place, *tasks, after=()):
    outs = [
        shape((sum(part.shape[0] for part in task), *task[0].shape[1:]), task[0].dtype)
        for task in tasks
    ]
    flat = [part for task in tasks for part in task]
    return call(
        partial(relay_kernel, [len(task) for task in tasks]), outs, place, *flat, after=after
    )


def group_blocks(place, quarters):
    half = quarters[0].shape[0]
    for q, quarter in enumerate(quarters):
        for i in range(half):
            dz, dy = q % 2 * half + i, q // 2
            z = lax.bitwise_xor(place[1], dz)
            yield z * 2 + lax.bitwise_xor(place[2], dy), quarter.at[i]


def assemble(place, quarters, rows, whole):
    for g, block in group_blocks(place, quarters):
        whole[pl.ds(pl.multiple_of(g * rows, rows), rows), :] = block[0:rows]


def prepare_first_kernel(place, att, small, first_o):
    t = place[0]
    d, joint = att.shape
    width = joint // 3
    part = width // TEAM
    for i in range(3):
        first_o[0, 0:d, i * part : (i + 1) * part] = chosen(
            t,
            [
                att[:, i * width + s * part : i * width + (s + 1) * part]
                for s in range(TEAM)
            ],
        )
    first_o[0, d : d + EXTRA, :] = small[...]


def prepare_rest_kernel(n_group, place, hid, back, rest_o):
    t = place[0]
    d = hid.shape[0]
    f = hid.shape[1] // n_group
    w = f // TEAM
    for g in range(n_group):
        rest_o[0:d, g * w : (g + 1) * w] = chosen(
            t, [hid[:, g * f + s * w : g * f + (s + 1) * w] for s in range(TEAM)]
        )
    rest_o[d : d + w, :] = back[pl.ds(pl.multiple_of(t * w, w), w), :]


def attention_kernel(
    n_group, d, f, n, place, p0, p1, p2, p3, own_out, other_out, *refs
):
    first, refs = refs[:4], refs[4:]
    (
        joint_o, probs_o, mixed_o, near_o, keep_o, vec_o, hb_o, wout_o, wfirst_o, token_s, small_s,
    ) = refs
    blocks = (p0, p1, p2, p3)
    t, y = place[0], place[2]
    part = wout_o.shape[0]
    width = wout_o.shape[1]
    w = f // TEAM
    assemble(place, first, d, wfirst_o)
    for g, block in group_blocks(place, first):
        small_s[g] = block[d : d + EXTRA, :].astype(F32)
    small = [small_s[g] for g in range(n_group)]
    vec_o[...] = jnp.concatenate([s[0:8, 0:d] for s in small], 1)
    hb_o[...] = jnp.concatenate(
        [chosen(t, [s[8:9, i * w : (i + 1) * w] for i in range(TEAM)]) for s in small], 1
    )
    for at in range(part // (2 * d)):
        wout_o[pl.ds(pl.multiple_of((at * 2 + y) * d, d), d), :] = own_out[
            at * d : (at + 1) * d
        ]
        wout_o[pl.ds(pl.multiple_of((at * 2 + 1 - y) * d, d), d), :] = other_out[
            at * d : (at + 1) * d
        ]
    for b in range(TEAM):
        token_s[b * n : (b + 1) * n] = blocks[b][0:n]
    mine = pl.ds(pl.multiple_of(t * part, part), part)
    for i in range(3):
        value = times(token_s[...], wfirst_o[:, i * part : (i + 1) * part])
        if i == 0:
            value = value + vec_o[0:1, mine]
        if i == 2:
            value = value + vec_o[1:2, mine]
        joint_o[:, i * part : (i + 1) * part] = value.astype(BF)
    scale = HD ** (-0.5)
    low = lax.broadcasted_iota(jnp.int32, (1, PAIR), 1) < HD
    zero = jnp.zeros((), BF)
    for b in range(TEAM):
        rows = slice(b * n, (b + 1) * n)
        ends = ends_of(blocks[b], n)
        same = segments(ends, (n, 1), 0) == segments(ends, (1, n), 1)
        for pair in range(part // PAIR):
            at = pair * PAIR
            query = joint_o[rows, at : at + PAIR]
            keys = joint_o[rows, part + at : part + at + PAIR]
            values = joint_o[rows, 2 * part + at : 2 * part + at + PAIR]
            mixed = []
            for h in range(2):
                sided = jnp.where(low, query, zero) if h == 0 else jnp.where(low, zero, query)
                scores = jnp.where(same, against(sided, keys) * scale, -1000000000.0)
                expo = jnp.exp(scores - jnp.max(scores, -1, keepdims=True))
                probs = expo / jnp.sum(expo, -1, keepdims=True)
                probs_o[(b * (part // PAIR) + pair) * 2 + h] = probs
                mixed.append(times(probs.astype(BF), values))
            mixed_o[rows, at : at + PAIR] = jnp.where(low, mixed[0], mixed[1]).astype(BF)
    for at in range(0, width, part):
        columns = slice(at, at + part)
        to_team(times(mixed_o[...], wout_o[:, columns]), n, near_o, keep_o, columns)


def norm_kernel(place, tokens, keep, got, far, vec, normed_o, low_o, hat_o, factor_o):
    n = tokens.shape[0]
    attn = keep[0:n] + got[0:n].astype(F32) + far[...].astype(F32) + vec[2:3]
    hat, factor = normalise(tokens[...].astype(F32) + attn)
    normed = hat * vec[3:4] + vec[4:5]
    normed_o[...] = normed
    low_o[...] = normed.astype(BF)
    hat_o[...] = hat
    factor_o[...] = jnp.broadcast_to(factor, factor_o.shape)


def gelu_parts(pre):
    bell = 0.5 * (1.0 + lax.erf(pre * (2.0**-0.5)))
    return bell, jnp.exp(-0.5 * pre * pre) * (2.0 * 3.141592653589793) ** -0.5


def feed_kernel(
    n_group, d, place, x0, x1, x2, x3, hb, rest, pre_o, act_o, near_o, keep_o, x_o
):
    n = x0.shape[0]
    w = rest.shape[1] - d
    for b, block in enumerate((x0, x1, x2, x3)):
        x_o[b * n : (b + 1) * n] = block[...]

    def entering(at, carry):
        columns = pl.ds(pl.multiple_of(at * 256, 256), 256)
        weight = rest[:, 0:d, columns].reshape(n_group * d, 256)
        pre = times(x_o[...], weight) + hb[:, columns]
        pre_o[:, columns] = pre
        act_o[:, columns] = (pre * gelu_parts(pre)[0]).astype(BF)
        return carry

    lax.fori_loop(0, pre_o.shape[1] // 256, entering, 0)

    def leaving(at, carry):
        columns = pl.ds(pl.multiple_of(at * 256, 256), 256)
        weight = rest[:, d : d + w, columns].reshape(n_group * w, 256)
        to_team(times(act_o[...], weight), n, near_o, keep_o, columns)
        return carry

    lax.fori_loop(0, keep_o.shape[1] // 256, leaving, 0)


def second_kernel(
    place, normed, keep, got, far, vec, cotangent, packed, layer_o, d_second_o, d_out_o, sums_o
):
    n = normed.shape[0]
    out = keep[0:n] + got[0:n].astype(F32) + far[...].astype(F32) + vec[5:6]
    hat, factor = normalise(normed[...] + out)
    live = jnp.where(segments(ends_of(packed, n), (n, 1), 0) < SEQS, 1.0, 0.0)
    layer_o[...] = ((hat * vec[6:7] + vec[7:8]) * live).astype(BF)
    d_final = cotangent[...].astype(F32) * live
    d_second = normalise_back(d_final * vec[6:7], hat, factor)
    d_second_o[...] = d_second
    d_out = d_second.astype(BF)
    d_out_o[...] = d_out
    sums_o[...] = jnp.zeros_like(sums_o)
    sums_o[0:1] = column_sum(d_out.astype(F32))
    sums_o[1:2] = column_sum(d_final * hat)
    sums_o[2:3] = column_sum(d_final)


def back_grad_kernel(place, d0, d1, d2, d3, act, grad_o, d_out_o):
    n = d0.shape[0]
    for b, block in enumerate((d0, d1, d2, d3)):
        d_out_o[b * n : (b + 1) * n] = block[...]

    def step(at, carry):
        rows = pl.ds(pl.multiple_of(at * 256, 256), 256)
        grad_o[rows, :] = outer(act[:, rows], d_out_o[...]).astype(BF)
        return carry

    lax.fori_loop(0, grad_o.shape[0] // 256, step, 0)


def feed_back_kernel(n_group, d, n, place, d_out, rest, pre, d_pre_o, near_o, keep_o, hb_o):
    w = rest.shape[1] - d
    per = 256 // w

    def through(at, carry):
        columns = pl.ds(pl.multiple_of(at * 256, 256), 256)
        weight = rest[pl.ds(at * per, per), d : d + w, :].reshape(256, rest.shape[2])
        d_act = against(d_out[...], weight)
        value = pre[:, columns]
        bell, slope = gelu_parts(value)
        d_pre = (d_act * (bell + value * slope)).astype(BF)
        d_pre_o[:, columns] = d_pre
        hb_o[:, columns] = column_sum(d_pre.astype(F32))
        return carry

    lax.fori_loop(0, pre.shape[1] // 256, through, 0)
    rows = 256 // d

    def entering(at, carry):
        columns = pl.ds(pl.multiple_of(at * 256, 256), 256)
        weight = rest[pl.ds(at * rows, rows), 0:d, :].reshape(256, rest.shape[2])
        to_team(against(d_pre_o[...], weight), n, near_o, keep_o, columns)
        return carry

    lax.fori_loop(0, keep_o.shape[1] // 256, entering, 0)


def hidden_grad_kernel(n_group, d, place, x, d_pre, own_o, sent_o, tile):
    grad_tiles(place, n_group, d, x, d_pre, own_o, sent_o, tile)


def norm_back_kernel(
    place, d_second, keep, got, far, hat, factor, vec, d_first_o, d_attn_o, sums_o
):
    n = d_second.shape[0]
    d_normed = d_second[...] + keep[0:n] + got[0:n].astype(F32) + far[...].astype(F32)
    d_first = normalise_back(d_normed * vec[3:4], hat[...], factor[:, 0:1])
    d_first_o[...] = d_first
    d_attn = d_first.astype(BF)
    d_attn_o[...] = d_attn
    sums_o[...] = jnp.zeros_like(sums_o)
    sums_o[0:1] = column_sum(d_attn.astype(F32))
    sums_o[1:2] = column_sum(d_normed * hat[...])
    sums_o[2:3] = column_sum(d_normed)


def attention_back_kernel(
    n_group, d, f, n, place, a0, a1, a2, a3, wout, joint, probs_in, p0, p1, p2, p3,
    sums1, sums2, d_hb,
    d_joint_o, own_o, near_o, far_o, attn_o, token_s, tile, vec_s, small_s, sent_s,
):
    t, z, y = place[0], place[1], place[2]
    depth = n_group // 2
    part = wout.shape[0]
    w = f // TEAM
    for b in range(TEAM):
        token_s[b * n : (b + 1) * n] = (p0, p1, p2, p3)[b][0:n]
        attn_o[b * n : (b + 1) * n] = (a0, a1, a2, a3)[b][...]
    d_mixed = against(attn_o[...], wout[...]).astype(BF)
    scale = HD ** (-0.5)
    low = lax.broadcasted_iota(jnp.int32, (1, PAIR), 1) < HD
    zero = jnp.zeros((), BF)
    for b in range(TEAM):
        rows = slice(b * n, (b + 1) * n)
        for pair in range(part // PAIR):
            at = pair * PAIR
            query = joint[rows, at : at + PAIR]
            keys = joint[rows, part + at : part + at + PAIR]
            values = joint[rows, 2 * part + at : 2 * part + at + PAIR]
            d_mix = d_mixed[rows, at : at + PAIR]
            d_query, d_keys, d_values = [], [], []
            for h in range(2):
                probs = probs_in[(b * (part // PAIR) + pair) * 2 + h]
                sided = jnp.where(low, d_mix, zero) if h == 0 else jnp.where(low, zero, d_mix)
                d_probs = against(sided, values)
                d_scores = (
                    probs * (d_probs - jnp.sum(probs * d_probs, -1, keepdims=True))
                ).astype(BF)
                d_values.append(outer(probs.astype(BF), d_mix))
                d_query.append(times(d_scores, keys))
                d_keys.append(outer(d_scores, query))
            for i, (value, factor) in enumerate(
                ((d_query, scale), (d_keys, scale), (d_values, 1.0))
            ):
                d_joint_o[rows, i * part + at : i * part + at + PAIR] = (
                    jnp.where(low, value[0], value[1]) * factor
                ).astype(BF)
    vec_s[...] = jnp.zeros_like(vec_s)
    mine = pl.ds(pl.multiple_of(t * part, part), part)
    vec_s[0:1, mine] = column_sum(d_joint_o[:, 0:part].astype(F32))
    vec_s[1:2, mine] = column_sum(d_joint_o[:, 2 * part : 3 * part].astype(F32))
    vec_s[2:5, :] = sums1[0:3]
    vec_s[5:8, :] = sums2[0:3]
    small_s[...] = jnp.zeros_like(small_s)
    for g in range(n_group):
        small_s[g, 0:8, 0:d] = vec_s[:, g * d : (g + 1) * d]
        row = d_hb[:, g * w : (g + 1) * w]
        small_s[g, 8:9, 0:f] = jnp.concatenate(
            [jnp.where(t == i, row, jnp.zeros_like(row)) for i in range(TEAM)], 1
        )
    grad_tiles(place, n_group, d, token_s, d_joint_o, own_o, sent_s, tile)
    half = depth // 2
    for k in range(depth):
        g = lax.bitwise_xor(z, k) * 2
        own_o[k, d : d + EXTRA, :] = small_s[g + y]
        sent_o = far_o if k >= half else near_o
        sent_o[k % half, 0:d, :] = sent_s[k ^ half, 0:d, :]
        sent_o[k % half, d : d + EXTRA, :] = small_s[g + 1 - y].astype(BF)


def token_back_kernel(
    n, d, place, d_joint, first, mixed, d_attn, near_o, keep_o, out_own_o, out_other_o, heads_s
):
    y = place[2]
    heads_s[...] = outer(mixed[...], d_attn[...])
    for at in range(mixed.shape[1] // (2 * d)):
        out_own_o[at * d : (at + 1) * d] = heads_s[
            pl.ds(pl.multiple_of((at * 2 + y) * d, d), d), :
        ]
        out_other_o[at * d : (at + 1) * d] = heads_s[
            pl.ds(pl.multiple_of((at * 2 + 1 - y) * d, d), d), :
        ].astype(BF)

    def step(at, carry):
        columns = pl.ds(pl.multiple_of(at * 256, 256), 256)
        to_team(against(d_joint[...], first[columns, :]), n, near_o, keep_o, columns)
        return carry

    lax.fori_loop(0, keep_o.shape[1] // 256, step, 0)


def add_far_kernel(place, own, got, sum_o):
    half = sum_o.shape[0]
    sum_o[...] = (own[half : 2 * half] + got[0:half].astype(F32)).astype(BF)


def add_near_kernel(place, own, got, far, keep_o, send_o):
    half = far.shape[0]
    total = own[0:half] + got[got.shape[0] - half :].astype(F32) + far[...].astype(F32)
    keep_o[...] = total[0 : half // 2]
    send_o[...] = total[half // 2 :].astype(BF)


def back_out_kernel(place, b0, b1, b2, b3, back_o):
    w = b0.shape[0]
    for i in range(TEAM):
        block = of_member(place[0], i, [b[...] for b in (b0, b1, b2, b3)])
        back_o[i * w : (i + 1) * w] = block.astype(F32)


def hidden_out_kernel(n_group, place, h0, h1, h2, h3, hidden_o):
    w = h0.shape[1] // n_group
    for i in range(TEAM):
        block = of_member(place[0], i, [h[...] for h in (h0, h1, h2, h3)]).astype(F32)
        for g in range(n_group):
            at = (g * TEAM + i) * w
            hidden_o[:, at : at + w] = block[:, g * w : (g + 1) * w]


def attention_out_kernel(
    heads_at, f, place, j0, j1, j2, j3, o0, o1, o2, o3, joint_o, out_o, *small_o
):
    t, z = place[0], place[1]
    d = out_o.shape[0]
    part = j0.shape[1] // 3
    width = part * TEAM
    total = jnp.zeros((EXTRA, 3 * part), F32)
    for i in range(TEAM):
        block = of_member(t, i, [j[...] for j in (j0, j1, j2, j3)]).astype(F32)
        for s in range(3):
            at = s * width + i * part
            joint_o[:, at : at + part] = block[0:d, s * part : (s + 1) * part]
        total = total + block[d : d + EXTRA]
    outs = [o[...] for o in (o0, o1, o2, o3)]
    out = of_member(t, TEAM - 1, outs)
    for i in range(TEAM - 1):
        out = jnp.where(z // heads_at == i, of_member(t, i, outs), out)
    out_o[...] = out.astype(F32)
    for i in range(8):
        small_o[i][...] = total[i : i + 1, 0:d]
    small_o[8][...] = total[8:9, 0:f]


def shards(
    tokens,
    lengths,
    cotangent,
    attention_in,
    query_bias,
    value_bias,
    attention_out,
    out_bias,
    first_gain,
    first_shift,
    hidden_in,
    hidden_bias,
    hidden_out,
    output_bias,
    second_gain,
    second_shift,
):
    at = Places()
    n_group, depth, place = at.n_group, at.depth, at.place
    n, width = tokens.shape
    d = attention_in.shape[0]
    f = hidden_bias.shape[0]
    w = f // TEAM
    part = width // TEAM
    inner = w * n_group
    all_rows = TEAM * n

    vectors = (
        query_bias,
        value_bias,
        out_bias,
        first_gain,
        first_shift,
        output_bias,
        second_gain,
        second_shift,
    )
    small = jnp.concatenate(
        [
            jnp.pad(jnp.stack(vectors), ((0, 0), (0, 3 * part - d))),
            jnp.pad(hidden_bias[None], ((0, EXTRA - 9), (0, 3 * part - f))),
        ],
        0,
    )
    extra = jnp.pad(lengths.astype(BF), ((0, EXTRA - 1), (0, width - lengths.shape[1])))
    packed = jnp.concatenate([tokens, extra], 0)
    (first_near,) = call(
        prepare_first_kernel,
        [shape((1, d + EXTRA, 3 * part), BF)],
        place,
        attention_in,
        small,
    )
    def widen(blocks):
        for flip in list(at.steps_down(at.half // 2))[::-1]:
            blocks = (blocks, at.send_z(blocks, flip))
            if flip < at.half // 2:
                (blocks,) = relay(place, blocks)
        return blocks

    heads_mine, heads_first = [], []
    for i in range(at.heads_at):
        home = at.t * at.heads_at + i
        value = jnp.where(at.z == home, attention_out, jnp.zeros_like(attention_out))
        for flip in at.steps_down(at.half):
            value = value + at.send_heads(value, i, flip, False)
            if flip == at.half:
                heads_first.append(value)
        heads_mine.append(value)
    out_mine = jnp.concatenate(heads_mine, 0)
    out_other = at.send_y(out_mine)
    packed_far = at.send_team(packed, 2)
    packed = [packed, at.send_team(packed, 1), packed_far, at.send_team(packed_far, 1)]

    (first_near,) = relay(place, widen(first_near), after=heads_first)
    (rest_mine,) = call(
        partial(prepare_rest_kernel, n_group),
        [shape((d + w, width), BF)],
        place,
        hidden_in,
        hidden_out,
        after=[first_near],
    )
    rest_all = lax.all_gather(rest_mine, "group", axis=0)
    first_far = at.other_half(first_near)
    first_near_y = at.send_y(first_near)
    (first_sent,) = relay(place, (first_far,), after=[first_near_y, out_other, *packed])
    first_all = [first_near, first_far, first_near_y, at.send_y(first_sent)]

    joint, probs, mixed, near, keep, vec, hb, w_out, w_first = call(
        partial(attention_kernel, n_group, d, f, n),
        [
            shape((all_rows, 3 * part), BF),
            shape((TEAM * H // TEAM, n, n), F32),
            shape((all_rows, part), BF),
            shape((2 * n, width), BF),
            shape((2 * n, width), F32),
            shape((8, width), F32),
            shape((1, inner), F32),
            shape((part, width), BF),
            shape((width, 3 * part), BF),
        ],
        place,
        *packed,
        out_mine,
        out_other,
        *first_all,
        scratch=[
            pltpu.VMEM((all_rows, width), BF),
            pltpu.VMEM((n_group, EXTRA, 3 * part), F32),
        ],
    )
    normed, normed_low, hat, factor = call(
        norm_kernel,
        [
            shape((n, width), F32),
            shape((n, width), BF),
            shape((n, width), F32),
            shape((n, 128), F32),
        ],
        place,
        tokens,
        *at.scatter_team(near, keep),
        vec,
    )

    pre, act, near, keep, normed4 = call(
        partial(feed_kernel, n_group, d),
        [
            shape((all_rows, inner), F32),
            shape((all_rows, inner), BF),
            shape((2 * n, width), BF),
            shape((2 * n, width), F32),
            shape((all_rows, width), BF),
        ],
        place,
        *at.gather_team(normed_low),
        hb,
        rest_all,
    )
    layer_out, d_second, d_out, sums2 = call(
        second_kernel,
        [
            shape((n, width), BF),
            shape((n, width), F32),
            shape((n, width), BF),
            shape((8, width), F32),
        ],
        place,
        normed,
        *at.scatter_team(near, keep),
        vec,
        cotangent,
        packed[0],
    )

    def add_far(own, came, after=()):
        half, rest = own.shape[0] // 2, own.shape[1:]
        return call(add_far_kernel, [shape((half, *rest), BF)], place, own, came, after=after)[0]

    def add_near(own, came_y, came_z, after=()):
        half, *rest = came_z.shape
        return call(
            add_near_kernel,
            [shape((half // 2, *rest), F32), shape((half // 2, *rest), BF)],
            place,
            own,
            came_y,
            came_z,
            after=after,
        )

    def sum_group(keep, send):
        flip = at.half // 2
        while flip > 1:
            total = keep + at.send_z(send, flip).astype(F32)
            flip //= 2
            keep, send = total[:flip], total[flip:].astype(BF)
        return at.over_copies((keep + at.send_z(send, 1).astype(F32))[0].astype(BF))

    half = depth // 2
    grad_back, d_out4 = call(
        back_grad_kernel,
        [shape((inner, width), BF), shape((all_rows, width), BF)],
        place,
        *at.gather_team(d_out),
        act,
    )
    g_back = at.over_copies(
        lax.psum_scatter(grad_back, "group", scatter_dimension=0, tiled=True)
    )
    d_pre, near, keep, d_hb = call(
        partial(feed_back_kernel, n_group, d, n),
        [
            shape((all_rows, inner), BF),
            shape((2 * n, width), BF),
            shape((2 * n, width), F32),
            shape((1, inner), F32),
        ],
        place,
        d_out4,
        rest_all,
        pre,
    )
    own_hidden, sent_y = call(
        partial(hidden_grad_kernel, n_group, d),
        [shape((depth, d, inner), F32), shape((depth, d, inner), BF)],
        place,
        normed4,
        d_pre,
        scratch=[pltpu.VMEM((2 * d, inner), F32)],
    )
    d_first, d_attn, sums1 = call(
        norm_back_kernel,
        [shape((n, width), F32), shape((n, width), BF), shape((8, width), F32)],
        place,
        d_second,
        *at.scatter_team(near, keep),
        hat,
        factor,
        vec,
        after=[sent_y],
    )
    heads_rows = at.heads_at * d
    d_joint, own_joint, near_joint, far_joint, d_attn4 = call(
        partial(attention_back_kernel, n_group, d, f, n),
        [
            shape((all_rows, 3 * part), BF),
            shape((depth, d + EXTRA, 3 * part), F32),
            shape((half, d + EXTRA, 3 * part), BF),
            shape((half, d + EXTRA, 3 * part), BF),
            shape((all_rows, width), BF),
        ],
        place,
        *at.gather_team(d_attn),
        w_out,
        joint,
        probs,
        *packed,
        sums1,
        sums2,
        d_hb,
        scratch=[
            pltpu.VMEM((all_rows, width), BF),
            pltpu.VMEM((2 * d, 3 * part), F32),
            pltpu.VMEM((8, width), F32),
            pltpu.VMEM((n_group, EXTRA, 3 * part), F32),
            pltpu.VMEM((depth, d, 3 * part), BF),
        ],
    )
    came_y = at.send_y(sent_y)
    sent_hidden = add_far(own_hidden, came_y)
    came_hidden = at.other_half(sent_hidden)
    sent_joint = add_far(own_joint, at.send_y(far_joint))
    came_joint = at.other_half(sent_joint)
    near, keep, out_own, out_sent = call(
        partial(token_back_kernel, n, d),
        [
            shape((2 * n, width), BF),
            shape((2 * n, width), F32),
            shape((heads_rows, width), F32),
            shape((heads_rows, width), BF),
        ],
        place,
        d_joint,
        w_first,
        mixed,
        d_attn4,
        after=[sent_joint],
        scratch=[pltpu.VMEM((part, width), F32)],
    )
    kept, got, far = at.scatter_team(near, keep)
    hidden_parts = add_near(own_hidden, came_y, came_hidden, [sent_joint, g_back])
    g_hidden = sum_group(*hidden_parts)
    out_sum = out_own + at.send_y(out_sent).astype(F32)
    g_out = jnp.zeros((d, width), F32)
    for i in range(at.heads_at):
        block = out_sum[i * d : (i + 1) * d]
        flips = list(at.steps_down(at.half))[::-1]
        for flip in flips:
            block = block + at.send_heads(block.astype(BF), i, flip, True).astype(F32)
        here = at.z == at.t * at.heads_at + i
        g_out = g_out + jnp.where(here, block, jnp.zeros_like(block))
    g_out = at.over_copies(g_out.astype(BF))
    joint_parts = add_near(
        own_joint, at.send_y(near_joint), came_joint, [g_hidden, far]
    )
    g_joint = sum_group(*joint_parts)
    grad_tokens = d_first + kept[:n] + got[:n].astype(F32) + far.astype(F32)

    (g_hidden_out,) = call(
        back_out_kernel, [shape((f, width), F32)], place, *at.gather_team(g_back)
    )
    (g_hidden_in,) = call(
        partial(hidden_out_kernel, n_group),
        [shape((d, TEAM * inner), F32)],
        place,
        *at.gather_team(g_hidden),
    )
    g_attention_in, g_attention_out, *g_small = call(
        partial(attention_out_kernel, at.heads_at, f),
        [shape((d, 3 * width), F32), shape((d, width), F32)]
        + [shape((1, d), F32)] * 8
        + [shape((1, f), F32)],
        place,
        *at.gather_team(g_joint),
        *at.gather_team(g_out),
        after=[g_hidden_out, g_hidden_in],
    )
    g_qb, g_vb, g_ob, g_g1, g_s1, g_outb, g_g2, g_s2, g_hb = (v.reshape(-1) for v in g_small)
    return (
        layer_out,
        grad_tokens,
        g_attention_in,
        g_qb,
        g_vb,
        g_attention_out,
        g_ob,
        g_g1,
        g_s1,
        g_hidden_in,
        g_hb,
        g_hidden_out,
        g_outb,
        g_g2,
        g_s2,
    )


def solution(mesh):
    rows = P(("replica", "group"), None)
    matrix = P("group", None)
    vector = P("group")
    params = (
        matrix,
        vector,
        vector,
        matrix,
        vector,
        vector,
        vector,
        matrix,
        vector,
        matrix,
        vector,
        vector,
        vector,
    )
    return jax.shard_map(
        shards,
        mesh=mesh,
        in_specs=(rows, rows, rows) + params,
        out_specs=(rows, rows) + params,
        check_vma=False,
    )
```

```python
from functools import partial

import jax
import jax.numpy as jnp
from jax import lax
from jax.experimental import pallas as pl
from jax.experimental.pallas import tpu as pltpu
from jax.sharding import PartitionSpec as P

H = 16
HD = 64
SEQS = 4
TEAM = 4
EXTRA = 16
PAIR = 2 * HD
BF = jnp.bfloat16
F32 = jnp.float32


class Places:
    def __init__(self):
        self.n_group = lax.axis_size("group")
        self.n_replica = lax.axis_size("replica")
        self.depth = self.n_group // 2
        self.half = self.depth // 2
        self.heads_at = self.depth // TEAM
        place = lax.axis_index("group")
        self.z = place // 2
        self.t = lax.axis_index("replica") % TEAM
        self.place = jnp.stack([self.t, self.z, place % 2]).astype(jnp.int32)

    def send_z(self, value, flip):
        return lax.ppermute(
            value, "group", [(g, g ^ (2 * flip)) for g in range(self.n_group)]
        )

    def send_y(self, value):
        return lax.ppermute(value, "group", [(g, g ^ 1) for g in range(self.n_group)])

    def send_team(self, value, flip):
        return lax.ppermute(value, "replica", [(r, r ^ flip) for r in range(self.n_replica)])

    def send_heads(self, value, at, flip, back):
        pairs = []
        for r in range(self.n_replica):
            home = r % TEAM * self.heads_at + at
            for z in range(self.depth):
                if (z ^ home) & (2 * flip - 1) == 0:
                    for y in range(2):
                        near = r * self.n_group + z * 2 + y
                        pairs.append((near ^ (2 * flip), near) if back else (near, near ^ (2 * flip)))
        return lax.ppermute(value, ("replica", "group"), pairs)

    def steps_down(self, top):
        while top >= 1:
            yield top
            top //= 2

    def other_half(self, blocks):
        return self.send_z(blocks, self.half)

    def gather_team(self, block):
        far = self.send_team(block, 2)
        near = self.send_team(block, 1)
        return [block, near, far, self.send_team(far, 1)]

    def scatter_near(self, near, keep):
        n = near.shape[0] // 2
        got = self.send_team(near, 1)
        return got, (keep[n:] + got[n:].astype(F32)).astype(BF)

    def scatter_team(self, near, keep):
        got, sent = self.scatter_near(near, keep)
        return keep, got, self.send_team(sent, 2)

    def over_copies(self, value):
        teams = self.n_replica // TEAM
        if teams == 1:
            return value
        return lax.psum(
            value,
            "replica",
            axis_index_groups=[
                [team * TEAM + t for team in range(teams)] for t in range(TEAM)
            ],
        )


def call(kernel, outs, place, *args, scratch=(), after=(), copied=()):
    specs = [pl.BlockSpec(memory_space=pltpu.VMEM)] * len(args)
    specs += [pl.BlockSpec(memory_space=pl.ANY)] * len(copied)
    args = (*args, *copied)
    body = kernel
    if after:
        read = len(args)
        specs += [pl.BlockSpec(memory_space=pl.ANY)] * len(after)
        args = (*args, *after)

        def body(place, *refs):
            kernel(place, *refs[:read], *refs[read + len(after) :])

    return pl.pallas_call(
        body,
        name=getattr(kernel, "func", kernel).__name__,
        out_shape=outs,
        in_specs=[pl.BlockSpec(memory_space=pltpu.SMEM)] + specs,
        out_specs=[pl.BlockSpec(memory_space=pltpu.VMEM)] * len(outs),
        scratch_shapes=list(scratch),
        compiler_params=pltpu.CompilerParams(vmem_limit_bytes=24 << 20),
        cost_estimate=pl.CostEstimate(flops=0, bytes_accessed=0, transcendentals=0),
    )(place, *args)


def shape(dims, dtype):
    return jax.ShapeDtypeStruct(tuple(dims), dtype)


def times(left, right):
    return jnp.dot(left, right, preferred_element_type=F32)


def against(left, weight):
    return lax.dot_general(left, weight, (((1,), (1,)), ((), ())), preferred_element_type=F32)


def outer(left, right):
    return lax.dot_general(left, right, (((0,), (0,)), ((), ())), preferred_element_type=F32)


def chosen(index, cases):
    result = cases[-1]
    for at in range(len(cases) - 2, -1, -1):
        result = jnp.where(index == at, cases[at], result)
    return result


def of_member(t, member, blocks):
    return chosen(t, [blocks[i ^ member] for i in range(TEAM)])


def column_sum(value):
    return jnp.sum(value, 0, keepdims=True)


def ends_of(block, n):
    row = block[n : n + EXTRA, 0:128].astype(F32)[0:1]
    lane = lax.broadcasted_iota(jnp.int32, (1, 128), 1)
    return [
        jnp.sum(jnp.where(lane <= s, row, 0.0), axis=1, keepdims=True) for s in range(SEQS)
    ]


def segments(ends, dims, axis):
    place = lax.broadcasted_iota(jnp.int32, dims, axis).astype(F32)
    total = jnp.zeros(dims, F32)
    for end in ends:
        total = total + jnp.where(place >= end, 1.0, 0.0)
    return total


def normalise(value):
    centre = jnp.mean(value, -1, keepdims=True)
    offset = value - centre
    spread = jnp.mean(offset * offset, -1, keepdims=True)
    factor = lax.rsqrt(spread + 1e-06)
    return offset * factor, factor


def normalise_back(d_hat, hat, factor):
    return factor * (
        d_hat
        - jnp.mean(d_hat, -1, keepdims=True)
        - hat * jnp.mean(d_hat * hat, -1, keepdims=True)
    )


def grad_tiles(place, n_group, width, left, right, own, near, far, tile):
    depth = n_group // 2
    half = depth // 2
    z, y = place[1], place[2]

    def step(at, carry):
        tile[...] = outer(left[:, pl.ds(pl.multiple_of(at * 2 * width, 2 * width), 2 * width)], right[...])
        k = lax.bitwise_xor(z, at)
        own[k, 0:width, :] = tile[pl.ds(pl.multiple_of(y * width, width), width), :]
        sent = tile[pl.ds(pl.multiple_of((1 - y) * width, width), width), :].astype(BF)

        @pl.when(k < half)
        def _():
            near[k, 0:width, :] = sent

        @pl.when(k >= half)
        def _():
            far[k - half, 0:width, :] = sent

        return carry

    lax.fori_loop(0, depth, step, 0)


def to_team(value, n, near, keep, columns):
    keep[0:n, columns] = value[0:n]
    near[0:n, columns] = value[n : 2 * n].astype(BF)
    keep[n : 2 * n, columns] = value[2 * n : 3 * n]
    near[n : 2 * n, columns] = value[3 * n : 4 * n].astype(BF)


def at_group(place, n_group, i):
    depth = n_group // 2
    dy, k = divmod(i, depth)
    y = place[2]
    return lax.rem(place[1] - k + depth, depth) * 2 + (y if dy == 0 else 1 - y)


def relay_kernel(counts, place, *refs):
    outs = refs[sum(counts) :]
    for out, count in zip(outs, counts):
        parts, refs = refs[:count], refs[count:]
        at = 0
        for part in parts:
            out[at : at + part.shape[0]] = part[...]
            at += part.shape[0]


def relay(place, *tasks, after=()):
    outs = [
        shape((sum(part.shape[0] for part in task), *task[0].shape[1:]), task[0].dtype)
        for task in tasks
    ]
    flat = [part for task in tasks for part in task]
    return call(
        partial(relay_kernel, [len(task) for task in tasks]), outs, place, *flat, after=after
    )


def group_blocks(place, quarters):
    half = quarters[0].shape[0]
    for q, quarter in enumerate(quarters):
        for i in range(half):
            dz, dy = q % 2 * half + i, q // 2
            z = lax.bitwise_xor(place[1], dz)
            yield z * 2 + lax.bitwise_xor(place[2], dy), quarter.at[i]


def assemble(place, quarters, rows, whole):
    for g, block in group_blocks(place, quarters):
        whole[pl.ds(pl.multiple_of(g * rows, rows), rows), :] = block[0:rows]


def prepare_first_kernel(place, att, small, first_o):
    t = place[0]
    d, joint = att.shape
    width = joint // 3
    part = width // TEAM
    for i in range(3):
        first_o[0, 0:d, i * part : (i + 1) * part] = chosen(
            t,
            [
                att[:, i * width + s * part : i * width + (s + 1) * part]
                for s in range(TEAM)
            ],
        )
    first_o[0, d : d + EXTRA, :] = small[...]


def prepare_rest_kernel(n_group, place, hid, back, rest_o):
    t = place[0]
    d = hid.shape[0]
    f = hid.shape[1] // n_group
    w = f // TEAM
    for g in range(n_group):
        rest_o[0:d, g * w : (g + 1) * w] = chosen(
            t, [hid[:, g * f + s * w : g * f + (s + 1) * w] for s in range(TEAM)]
        )
    rest_o[d : d + w, :] = back[pl.ds(pl.multiple_of(t * w, w), w), :]


def attention_kernel(
    n_group, d, f, n, place, p0, p1, p2, p3, own_out, other_out, *refs
):
    first, refs = refs[:4], refs[4:]
    (
        joint_o, probs_o, mixed_o, near_o, keep_o, vec_o, hb_o, wout_o, wfirst_o, token_s, small_s,
    ) = refs
    blocks = (p0, p1, p2, p3)
    t, y = place[0], place[2]
    part = wout_o.shape[0]
    width = wout_o.shape[1]
    w = f // TEAM
    assemble(place, first, d, wfirst_o)
    for g, block in group_blocks(place, first):
        small_s[g] = block[d : d + EXTRA, :].astype(F32)
    small = [small_s[g] for g in range(n_group)]
    vec_o[...] = jnp.concatenate([s[0:8, 0:d] for s in small], 1)
    hb_o[...] = jnp.concatenate(
        [chosen(t, [s[8:9, i * w : (i + 1) * w] for i in range(TEAM)]) for s in small], 1
    )
    for at in range(part // (2 * d)):
        wout_o[pl.ds(pl.multiple_of((at * 2 + y) * d, d), d), :] = own_out[
            at * d : (at + 1) * d
        ]
        wout_o[pl.ds(pl.multiple_of((at * 2 + 1 - y) * d, d), d), :] = other_out[
            at * d : (at + 1) * d
        ]
    for b in range(TEAM):
        token_s[b * n : (b + 1) * n] = blocks[b][0:n]
    mine = pl.ds(pl.multiple_of(t * part, part), part)
    for i in range(3):
        value = times(token_s[...], wfirst_o[:, i * part : (i + 1) * part])
        if i == 0:
            value = value + vec_o[0:1, mine]
        if i == 2:
            value = value + vec_o[1:2, mine]
        joint_o[:, i * part : (i + 1) * part] = value.astype(BF)
    scale = HD ** (-0.5)
    low = lax.broadcasted_iota(jnp.int32, (1, PAIR), 1) < HD
    zero = jnp.zeros((), BF)
    for b in range(TEAM):
        rows = slice(b * n, (b + 1) * n)
        ends = ends_of(blocks[b], n)
        same = segments(ends, (n, 1), 0) == segments(ends, (1, n), 1)
        for pair in range(part // PAIR):
            at = pair * PAIR
            query = joint_o[rows, at : at + PAIR]
            keys = joint_o[rows, part + at : part + at + PAIR]
            values = joint_o[rows, 2 * part + at : 2 * part + at + PAIR]
            mixed = []
            for h in range(2):
                sided = jnp.where(low, query, zero) if h == 0 else jnp.where(low, zero, query)
                scores = jnp.where(same, against(sided, keys) * scale, -1000000000.0)
                expo = jnp.exp(scores - jnp.max(scores, -1, keepdims=True))
                probs = expo / jnp.sum(expo, -1, keepdims=True)
                probs_o[(b * (part // PAIR) + pair) * 2 + h] = probs
                mixed.append(times(probs.astype(BF), values))
            mixed_o[rows, at : at + PAIR] = jnp.where(low, mixed[0], mixed[1]).astype(BF)
    for at in range(0, width, part):
        columns = slice(at, at + part)
        to_team(times(mixed_o[...], wout_o[:, columns]), n, near_o, keep_o, columns)


def norm_kernel(place, tokens, keep, got, far, vec, normed_o, low_o, hat_o, factor_o):
    n = tokens.shape[0]
    attn = keep[0:n] + got[0:n].astype(F32) + far[...].astype(F32) + vec[2:3]
    hat, factor = normalise(tokens[...].astype(F32) + attn)
    normed = hat * vec[3:4] + vec[4:5]
    normed_o[...] = normed
    low_o[...] = normed.astype(BF)
    hat_o[...] = hat
    factor_o[...] = jnp.broadcast_to(factor, factor_o.shape)


def gelu_parts(pre):
    bell = 0.5 * (1.0 + lax.erf(pre * (2.0**-0.5)))
    return bell, jnp.exp(-0.5 * pre * pre) * (2.0 * 3.141592653589793) ** -0.5


def feed_kernel(
    n_group, d, place, hb, x0, x1, x2, x3, rest, pre_o, act_o, near_o, keep_o, x_o, rest_s, sems
):
    n = x0.shape[0]
    w = rest.shape[1] - d
    tiles = rest.shape[2] // 256
    loads = [
        pltpu.make_async_copy(block, x_o.at[pl.ds(b * n, n)], sems.at[b])
        for b, block in enumerate((x0, x1, x2, x3))
    ]

    def weights(at, rows, first):
        part = (slice(None), rows, pl.ds(at * 256, 256))
        return pltpu.make_async_copy(rest.at[part], rest_s.at[part], sems.at[first + at])

    entering = [weights(at, pl.ds(0, d), 4) for at in range(tiles)]
    leaving = [weights(at, pl.ds(d, w), 4 + tiles) for at in range(tiles)]
    for load in loads + entering + leaving:
        load.start()
    for load in loads:
        load.wait()
    for at in range(tiles):
        columns = slice(at * 256, (at + 1) * 256)
        entering[at].wait()
        weight = rest_s[:, 0:d, columns].reshape(n_group * d, 256)
        pre = times(x_o[...], weight) + hb[:, columns]
        pre_o[:, columns] = pre
        act_o[:, columns] = (pre * gelu_parts(pre)[0]).astype(BF)
    for at in range(tiles):
        columns = slice(at * 256, (at + 1) * 256)
        leaving[at].wait()
        weight = rest_s[:, d : d + w, columns].reshape(n_group * w, 256)
        to_team(times(act_o[...], weight), n, near_o, keep_o, columns)


def second_kernel(
    place, normed, keep, got, far, vec, cotangent, packed, layer_o, d_second_o, d_out_o, sums_o
):
    n = normed.shape[0]
    out = keep[0:n] + got[0:n].astype(F32) + far[...].astype(F32) + vec[5:6]
    hat, factor = normalise(normed[...] + out)
    live = jnp.where(segments(ends_of(packed, n), (n, 1), 0) < SEQS, 1.0, 0.0)
    layer_o[...] = ((hat * vec[6:7] + vec[7:8]) * live).astype(BF)
    d_final = cotangent[...].astype(F32) * live
    d_second = normalise_back(d_final * vec[6:7], hat, factor)
    d_second_o[...] = d_second
    d_out = d_second.astype(BF)
    d_out_o[...] = d_out
    sums_o[...] = jnp.zeros_like(sums_o)
    sums_o[0:1] = column_sum(d_out.astype(F32))
    sums_o[1:2] = column_sum(d_final * hat)
    sums_o[2:3] = column_sum(d_final)


def back_grad_kernel(place, d0, d1, d2, d3, act, grad_o, d_out_o):
    n = d0.shape[0]
    for b, block in enumerate((d0, d1, d2, d3)):
        d_out_o[b * n : (b + 1) * n] = block[...]

    def step(at, carry):
        rows = pl.ds(pl.multiple_of(at * 256, 256), 256)
        grad_o[rows, :] = outer(act[:, rows], d_out_o[...]).astype(BF)
        return carry

    lax.fori_loop(0, grad_o.shape[0] // 256, step, 0)


def feed_back_kernel(
    n_group, d, n, place, d_out, pre, rest, d_pre_o, near_o, keep_o, hb_o, rest_s, sems
):
    w = rest.shape[1] - d
    tiles = rest.shape[2] // 256

    def weights(at, rows, count, first):
        part = (pl.ds(at * (256 // count), 256 // count), pl.ds(rows, count))
        return pltpu.make_async_copy(rest.at[part], rest_s.at[part], sems.at[first + at])

    leaving = [weights(at, d, w, 0) for at in range(tiles)]
    entering = [weights(at, 0, d, tiles) for at in range(tiles)]
    for load in leaving + entering:
        load.start()
    for at in range(tiles):
        columns = slice(at * 256, (at + 1) * 256)
        leaving[at].wait()
        per = 256 // w
        weight = rest_s[at * per : (at + 1) * per, d : d + w, :].reshape(256, rest.shape[2])
        d_act = against(d_out[...], weight)
        value = pre[:, columns]
        bell, slope = gelu_parts(value)
        d_pre = (d_act * (bell + value * slope)).astype(BF)
        d_pre_o[:, columns] = d_pre
        hb_o[:, columns] = column_sum(d_pre.astype(F32))
    for at in range(tiles):
        columns = slice(at * 256, (at + 1) * 256)
        entering[at].wait()
        per = 256 // d
        weight = rest_s[at * per : (at + 1) * per, 0:d, :].reshape(256, rest.shape[2])
        to_team(against(d_pre_o[...], weight), n, near_o, keep_o, columns)


def hidden_grad_kernel(n_group, d, place, x, d_pre, own_o, near_o, far_o, tile):
    grad_tiles(place, n_group, d, x, d_pre, own_o, near_o, far_o, tile)


def norm_back_kernel(
    place, d_second, keep, got, far, hat, factor, vec, d_first_o, d_attn_o, sums_o
):
    n = d_second.shape[0]
    d_normed = d_second[...] + keep[0:n] + got[0:n].astype(F32) + far[...].astype(F32)
    d_first = normalise_back(d_normed * vec[3:4], hat[...], factor[:, 0:1])
    d_first_o[...] = d_first
    d_attn = d_first.astype(BF)
    d_attn_o[...] = d_attn
    sums_o[...] = jnp.zeros_like(sums_o)
    sums_o[0:1] = column_sum(d_attn.astype(F32))
    sums_o[1:2] = column_sum(d_normed * hat[...])
    sums_o[2:3] = column_sum(d_normed)


def attention_back_kernel(
    n_group, d, f, n, place, a0, a1, a2, a3, wout, joint, probs_in, p0, p1, p2, p3,
    sums1, sums2, d_hb,
    d_joint_o, own_o, near_o, far_o, attn_o, token_s, tile, vec_s, small_s,
):
    t, z, y = place[0], place[1], place[2]
    depth = n_group // 2
    part = wout.shape[0]
    w = f // TEAM
    for b in range(TEAM):
        token_s[b * n : (b + 1) * n] = (p0, p1, p2, p3)[b][0:n]
        attn_o[b * n : (b + 1) * n] = (a0, a1, a2, a3)[b][...]
    d_mixed = against(attn_o[...], wout[...]).astype(BF)
    scale = HD ** (-0.5)
    low = lax.broadcasted_iota(jnp.int32, (1, PAIR), 1) < HD
    zero = jnp.zeros((), BF)
    for b in range(TEAM):
        rows = slice(b * n, (b + 1) * n)
        for pair in range(part // PAIR):
            at = pair * PAIR
            query = joint[rows, at : at + PAIR]
            keys = joint[rows, part + at : part + at + PAIR]
            values = joint[rows, 2 * part + at : 2 * part + at + PAIR]
            d_mix = d_mixed[rows, at : at + PAIR]
            d_query, d_keys, d_values = [], [], []
            for h in range(2):
                probs = probs_in[(b * (part // PAIR) + pair) * 2 + h]
                sided = jnp.where(low, d_mix, zero) if h == 0 else jnp.where(low, zero, d_mix)
                d_probs = against(sided, values)
                d_scores = (
                    probs * (d_probs - jnp.sum(probs * d_probs, -1, keepdims=True))
                ).astype(BF)
                d_values.append(outer(probs.astype(BF), d_mix))
                d_query.append(times(d_scores, keys))
                d_keys.append(outer(d_scores, query))
            for i, (value, factor) in enumerate(
                ((d_query, scale), (d_keys, scale), (d_values, 1.0))
            ):
                d_joint_o[rows, i * part + at : i * part + at + PAIR] = (
                    jnp.where(low, value[0], value[1]) * factor
                ).astype(BF)
    vec_s[...] = jnp.zeros_like(vec_s)
    mine = pl.ds(pl.multiple_of(t * part, part), part)
    vec_s[0:1, mine] = column_sum(d_joint_o[:, 0:part].astype(F32))
    vec_s[1:2, mine] = column_sum(d_joint_o[:, 2 * part : 3 * part].astype(F32))
    vec_s[2:5, :] = sums1[0:3]
    vec_s[5:8, :] = sums2[0:3]
    small_s[...] = jnp.zeros_like(small_s)
    for g in range(n_group):
        small_s[g, 0:8, 0:d] = vec_s[:, g * d : (g + 1) * d]
        row = d_hb[:, g * w : (g + 1) * w]
        small_s[g, 8:9, 0:f] = jnp.concatenate(
            [jnp.where(t == i, row, jnp.zeros_like(row)) for i in range(TEAM)], 1
        )
    grad_tiles(place, n_group, d, token_s, d_joint_o, own_o, near_o, far_o, tile)
    half = depth // 2
    for k in range(depth):
        g = lax.bitwise_xor(z, k) * 2
        own_o[k, d : d + EXTRA, :] = small_s[g + y]
        sent_o = far_o if k >= half else near_o
        sent_o[k % half, d : d + EXTRA, :] = small_s[g + 1 - y].astype(BF)


def token_back_kernel(
    n, d, place, d_joint, first, mixed, d_attn, near_o, keep_o, out_own_o, out_other_o, heads_s
):
    y = place[2]
    heads_s[...] = outer(mixed[...], d_attn[...])
    for at in range(mixed.shape[1] // (2 * d)):
        out_own_o[at * d : (at + 1) * d] = heads_s[
            pl.ds(pl.multiple_of((at * 2 + y) * d, d), d), :
        ]
        out_other_o[at * d : (at + 1) * d] = heads_s[
            pl.ds(pl.multiple_of((at * 2 + 1 - y) * d, d), d), :
        ].astype(BF)

    def step(at, carry):
        columns = pl.ds(pl.multiple_of(at * 256, 256), 256)
        to_team(against(d_joint[...], first[columns, :]), n, near_o, keep_o, columns)
        return carry

    lax.fori_loop(0, keep_o.shape[1] // 256, step, 0)


def add_far_kernel(place, own, got, sum_o):
    half = sum_o.shape[0]
    sum_o[...] = (own[half : 2 * half] + got[0:half].astype(F32)).astype(BF)


def add_near_kernel(place, own, got, far, keep_o, send_o):
    half = far.shape[0]
    total = own[0:half] + got[got.shape[0] - half :].astype(F32) + far[...].astype(F32)
    keep_o[...] = total[0 : half // 2]
    send_o[...] = total[half // 2 :].astype(BF)


def back_out_kernel(place, b0, b1, b2, b3, back_o):
    w = b0.shape[0]
    for i in range(TEAM):
        block = of_member(place[0], i, [b[...] for b in (b0, b1, b2, b3)])
        back_o[i * w : (i + 1) * w] = block.astype(F32)


def hidden_out_kernel(n_group, place, h0, h1, h2, h3, hidden_o):
    w = h0.shape[1] // n_group
    for i in range(TEAM):
        block = of_member(place[0], i, [h[...] for h in (h0, h1, h2, h3)]).astype(F32)
        for g in range(n_group):
            at = (g * TEAM + i) * w
            hidden_o[:, at : at + w] = block[:, g * w : (g + 1) * w]


def attention_out_kernel(
    heads_at, f, place, j0, j1, j2, j3, o0, o1, o2, o3, joint_o, out_o, *small_o
):
    t, z = place[0], place[1]
    d = out_o.shape[0]
    part = j0.shape[1] // 3
    width = part * TEAM
    total = jnp.zeros((EXTRA, 3 * part), F32)
    for i in range(TEAM):
        block = of_member(t, i, [j[...] for j in (j0, j1, j2, j3)]).astype(F32)
        for s in range(3):
            at = s * width + i * part
            joint_o[:, at : at + part] = block[0:d, s * part : (s + 1) * part]
        total = total + block[d : d + EXTRA]
    outs = [o[...] for o in (o0, o1, o2, o3)]
    out = of_member(t, TEAM - 1, outs)
    for i in range(TEAM - 1):
        out = jnp.where(z // heads_at == i, of_member(t, i, outs), out)
    out_o[...] = out.astype(F32)
    for i in range(8):
        small_o[i][...] = total[i : i + 1, 0:d]
    small_o[8][...] = total[8:9, 0:f]


def shards(
    tokens,
    lengths,
    cotangent,
    attention_in,
    query_bias,
    value_bias,
    attention_out,
    out_bias,
    first_gain,
    first_shift,
    hidden_in,
    hidden_bias,
    hidden_out,
    output_bias,
    second_gain,
    second_shift,
):
    at = Places()
    n_group, depth, place = at.n_group, at.depth, at.place
    n, width = tokens.shape
    d = attention_in.shape[0]
    f = hidden_bias.shape[0]
    w = f // TEAM
    part = width // TEAM
    inner = w * n_group
    all_rows = TEAM * n

    vectors = (
        query_bias,
        value_bias,
        out_bias,
        first_gain,
        first_shift,
        output_bias,
        second_gain,
        second_shift,
    )
    small = jnp.concatenate(
        [
            jnp.pad(jnp.stack(vectors), ((0, 0), (0, 3 * part - d))),
            jnp.pad(hidden_bias[None], ((0, EXTRA - 9), (0, 3 * part - f))),
        ],
        0,
    )
    extra = jnp.pad(lengths.astype(BF), ((0, EXTRA - 1), (0, width - lengths.shape[1])))
    packed = jnp.concatenate([tokens, extra], 0)
    (first_near,) = call(
        prepare_first_kernel,
        [shape((1, d + EXTRA, 3 * part), BF)],
        place,
        attention_in,
        small,
    )
    def widen(blocks):
        for flip in list(at.steps_down(at.half // 2))[::-1]:
            blocks = (blocks, at.send_z(blocks, flip))
            if flip < at.half // 2:
                (blocks,) = relay(place, blocks)
        return blocks

    heads_mine, heads_first = [], []
    for i in range(at.heads_at):
        home = at.t * at.heads_at + i
        value = jnp.where(at.z == home, attention_out, jnp.zeros_like(attention_out))
        for flip in at.steps_down(at.half):
            value = value + at.send_heads(value, i, flip, False)
            if flip == at.half:
                heads_first.append(value)
        heads_mine.append(value)
    out_mine = jnp.concatenate(heads_mine, 0)
    out_other = at.send_y(out_mine)
    packed_far = at.send_team(packed, 2)
    packed = [packed, at.send_team(packed, 1), packed_far, at.send_team(packed_far, 1)]

    (first_near,) = relay(place, widen(first_near), after=heads_first)
    (rest_mine,) = call(
        partial(prepare_rest_kernel, n_group),
        [shape((d + w, width), BF)],
        place,
        hidden_in,
        hidden_out,
        after=[first_near],
    )
    rest_all = lax.all_gather(rest_mine, "group", axis=0)
    first_far = at.other_half(first_near)
    first_near_y = at.send_y(first_near)
    (first_sent,) = relay(place, (first_far,), after=[first_near_y, out_other, *packed])
    first_all = [first_near, first_far, first_near_y, at.send_y(first_sent)]

    joint, probs, mixed, near, keep, vec, hb, w_out, w_first = call(
        partial(attention_kernel, n_group, d, f, n),
        [
            shape((all_rows, 3 * part), BF),
            shape((TEAM * H // TEAM, n, n), F32),
            shape((all_rows, part), BF),
            shape((2 * n, width), BF),
            shape((2 * n, width), F32),
            shape((8, width), F32),
            shape((1, inner), F32),
            shape((part, width), BF),
            shape((width, 3 * part), BF),
        ],
        place,
        *packed,
        out_mine,
        out_other,
        *first_all,
        scratch=[
            pltpu.VMEM((all_rows, width), BF),
            pltpu.VMEM((n_group, EXTRA, 3 * part), F32),
        ],
    )
    normed, normed_low, hat, factor = call(
        norm_kernel,
        [
            shape((n, width), F32),
            shape((n, width), BF),
            shape((n, width), F32),
            shape((n, 128), F32),
        ],
        place,
        tokens,
        *at.scatter_team(near, keep),
        vec,
    )

    pre, act, near, keep, normed4 = call(
        partial(feed_kernel, n_group, d),
        [
            shape((all_rows, inner), F32),
            shape((all_rows, inner), BF),
            shape((2 * n, width), BF),
            shape((2 * n, width), F32),
            shape((all_rows, width), BF),
        ],
        place,
        hb,
        copied=[*at.gather_team(normed_low), rest_all],
        scratch=[
            pltpu.VMEM((n_group, d + w, width), BF),
            pltpu.SemaphoreType.DMA((4 + 2 * (inner // 256),)),
        ],
    )
    layer_out, d_second, d_out, sums2 = call(
        second_kernel,
        [
            shape((n, width), BF),
            shape((n, width), F32),
            shape((n, width), BF),
            shape((8, width), F32),
        ],
        place,
        normed,
        *at.scatter_team(near, keep),
        vec,
        cotangent,
        packed[0],
    )

    def add_near(own, came_y, came_z, after=()):
        half, *rest = came_z.shape
        return call(
            add_near_kernel,
            [shape((half // 2, *rest), F32), shape((half // 2, *rest), BF)],
            place,
            own,
            came_y,
            came_z,
            after=after,
        )

    def sum_group(keep, send):
        flip = at.half // 2
        while flip > 1:
            total = keep + at.send_z(send, flip).astype(F32)
            flip //= 2
            keep, send = total[:flip], total[flip:].astype(BF)
        return at.over_copies((keep + at.send_z(send, 1).astype(F32))[0].astype(BF))

    half = depth // 2
    def add_far(own, came, after=()):
        half, rest = own.shape[0] // 2, own.shape[1:]
        return call(add_far_kernel, [shape((half, *rest), BF)], place, own, came, after=after)[0]

    grad_back, d_out4 = call(
        back_grad_kernel,
        [shape((inner, width), BF), shape((all_rows, width), BF)],
        place,
        *at.gather_team(d_out),
        act,
    )
    g_back = at.over_copies(
        lax.psum_scatter(grad_back, "group", scatter_dimension=0, tiled=True)
    )
    d_pre, near, keep, d_hb = call(
        partial(feed_back_kernel, n_group, d, n),
        [
            shape((all_rows, inner), BF),
            shape((2 * n, width), BF),
            shape((2 * n, width), F32),
            shape((1, inner), F32),
        ],
        place,
        d_out4,
        pre,
        copied=[rest_all],
        scratch=[
            pltpu.VMEM((n_group, d + w, width), BF),
            pltpu.SemaphoreType.DMA((2 * (inner // 256),)),
        ],
    )
    own_hidden, near_hidden, far_hidden = call(
        partial(hidden_grad_kernel, n_group, d),
        [shape((depth, d, inner), F32)] + [shape((half, d, inner), BF)] * 2,
        place,
        normed4,
        d_pre,
        scratch=[pltpu.VMEM((2 * d, inner), F32)],
    )
    d_first, d_attn, sums1 = call(
        norm_back_kernel,
        [shape((n, width), F32), shape((n, width), BF), shape((8, width), F32)],
        place,
        d_second,
        *at.scatter_team(near, keep),
        hat,
        factor,
        vec,
        after=[far_hidden],
    )
    heads_rows = at.heads_at * d
    sent_hidden = add_far(own_hidden, at.send_y(far_hidden))
    came_hidden = at.other_half(sent_hidden)
    d_joint, own_joint, near_joint, far_joint, d_attn4 = call(
        partial(attention_back_kernel, n_group, d, f, n),
        [
            shape((all_rows, 3 * part), BF),
            shape((depth, d + EXTRA, 3 * part), F32),
            shape((half, d + EXTRA, 3 * part), BF),
            shape((half, d + EXTRA, 3 * part), BF),
            shape((all_rows, width), BF),
        ],
        place,
        *at.gather_team(d_attn),
        w_out,
        joint,
        probs,
        *packed,
        sums1,
        sums2,
        d_hb,
        after=[sent_hidden],
        scratch=[
            pltpu.VMEM((all_rows, width), BF),
            pltpu.VMEM((2 * d, 3 * part), F32),
            pltpu.VMEM((8, width), F32),
            pltpu.VMEM((n_group, EXTRA, 3 * part), F32),
        ],
    )
    sent_joint = add_far(own_joint, at.send_y(far_joint), [came_hidden])
    (sent_y,) = relay(place, (near_hidden,), after=[sent_joint])
    came_joint = at.other_half(sent_joint)
    hidden_parts = add_near(own_hidden, at.send_y(sent_y), came_hidden)
    g_hidden = sum_group(*hidden_parts)
    joint_parts = add_near(own_joint, at.send_y(near_joint), came_joint)
    g_joint = sum_group(*joint_parts)
    near, keep, out_own, out_sent = call(
        partial(token_back_kernel, n, d),
        [
            shape((2 * n, width), BF),
            shape((2 * n, width), F32),
            shape((heads_rows, width), F32),
            shape((heads_rows, width), BF),
        ],
        place,
        d_joint,
        w_first,
        mixed,
        d_attn4,
        after=[],
        scratch=[pltpu.VMEM((part, width), F32)],
    )
    kept, got, far = at.scatter_team(near, keep)
    out_sum = out_own + at.send_y(out_sent).astype(F32)
    g_out = jnp.zeros((d, width), F32)
    for i in range(at.heads_at):
        block = out_sum[i * d : (i + 1) * d]
        flips = list(at.steps_down(at.half))[::-1]
        for flip in flips:
            block = block + at.send_heads(block.astype(BF), i, flip, True).astype(F32)
        here = at.z == at.t * at.heads_at + i
        g_out = g_out + jnp.where(here, block, jnp.zeros_like(block))
    g_out = at.over_copies(g_out.astype(BF))
    grad_tokens = d_first + kept[:n] + got[:n].astype(F32) + far.astype(F32)

    (g_hidden_out,) = call(
        back_out_kernel, [shape((f, width), F32)], place, *at.gather_team(g_back)
    )
    (g_hidden_in,) = call(
        partial(hidden_out_kernel, n_group),
        [shape((d, TEAM * inner), F32)],
        place,
        *at.gather_team(g_hidden),
    )
    g_attention_in, g_attention_out, *g_small = call(
        partial(attention_out_kernel, at.heads_at, f),
        [shape((d, 3 * width), F32), shape((d, width), F32)]
        + [shape((1, d), F32)] * 8
        + [shape((1, f), F32)],
        place,
        *at.gather_team(g_joint),
        *at.gather_team(g_out),
        after=[g_hidden_out, g_hidden_in],
    )
    g_qb, g_vb, g_ob, g_g1, g_s1, g_outb, g_g2, g_s2, g_hb = (v.reshape(-1) for v in g_small)
    return (
        layer_out,
        grad_tokens,
        g_attention_in,
        g_qb,
        g_vb,
        g_attention_out,
        g_ob,
        g_g1,
        g_s1,
        g_hidden_in,
        g_hb,
        g_hidden_out,
        g_outb,
        g_g2,
        g_s2,
    )


def solution(mesh):
    rows = P(("replica", "group"), None)
    matrix = P("group", None)
    vector = P("group")
    params = (
        matrix,
        vector,
        vector,
        matrix,
        vector,
        vector,
        vector,
        matrix,
        vector,
        matrix,
        vector,
        vector,
        vector,
    )
    return jax.shard_map(
        shards,
        mesh=mesh,
        in_specs=(rows, rows, rows) + params,
        out_specs=(rows, rows) + params,
        check_vma=False,
    )
```

```python
from functools import partial

import jax
import jax.numpy as jnp
from jax import lax
from jax.experimental import pallas as pl
from jax.experimental.pallas import tpu as pltpu
from jax.sharding import PartitionSpec as P

H = 16
HD = 64
SEQS = 4
TEAM = 4
EXTRA = 16
PAIR = 2 * HD
BF = jnp.bfloat16
F32 = jnp.float32


class Places:
    def __init__(self):
        self.n_group = lax.axis_size("group")
        self.n_replica = lax.axis_size("replica")
        self.depth = self.n_group // 2
        self.half = self.depth // 2
        self.heads_at = self.depth // TEAM
        place = lax.axis_index("group")
        self.z = place // 2
        self.t = lax.axis_index("replica") % TEAM
        self.place = jnp.stack([self.t, self.z, place % 2]).astype(jnp.int32)

    def send_z(self, value, flip):
        return lax.ppermute(
            value, "group", [(g, g ^ (2 * flip)) for g in range(self.n_group)]
        )

    def send_y(self, value):
        return lax.ppermute(value, "group", [(g, g ^ 1) for g in range(self.n_group)])

    def send_team(self, value, flip):
        return lax.ppermute(value, "replica", [(r, r ^ flip) for r in range(self.n_replica)])

    def send_heads(self, value, at, flip, back):
        pairs = []
        for r in range(self.n_replica):
            home = r % TEAM * self.heads_at + at
            for z in range(self.depth):
                if (z ^ home) & (2 * flip - 1) == 0:
                    for y in range(2):
                        near = r * self.n_group + z * 2 + y
                        pairs.append((near ^ (2 * flip), near) if back else (near, near ^ (2 * flip)))
        return lax.ppermute(value, ("replica", "group"), pairs)

    def steps_down(self, top):
        while top >= 1:
            yield top
            top //= 2

    def other_half(self, blocks):
        return self.send_z(blocks, self.half)

    def spread_heads(self, block):
        for flip in (2, 1):
            pairs = []
            for r in range(self.n_replica):
                for g in range(self.n_group):
                    apart = r % TEAM ^ g // 2 // self.heads_at
                    if apart == 0 or (flip == 1 and apart == 2):
                        pairs.append((r * self.n_group + g, (r ^ flip) * self.n_group + g))
            block = block + lax.ppermute(block, ("replica", "group"), pairs)
        return block

    def gather_team(self, block):
        far = self.send_team(block, 2)
        near = self.send_team(block, 1)
        return [block, near, far, self.send_team(far, 1)]

    def scatter_near(self, near, keep):
        n = near.shape[0] // 2
        got = self.send_team(near, 1)
        return got, (keep[n:] + got[n:].astype(F32)).astype(BF)

    def scatter_team(self, near, keep):
        got, sent = self.scatter_near(near, keep)
        return keep, got, self.send_team(sent, 2)

    def over_copies(self, value):
        teams = self.n_replica // TEAM
        if teams == 1:
            return value
        return lax.psum(
            value,
            "replica",
            axis_index_groups=[
                [team * TEAM + t for team in range(teams)] for t in range(TEAM)
            ],
        )


def call(kernel, outs, place, *args, scratch=(), after=()):
    specs = [pl.BlockSpec(memory_space=pltpu.VMEM)] * len(args)
    body = kernel
    if after:
        read = len(args)
        specs += [pl.BlockSpec(memory_space=pl.ANY)] * len(after)
        args = (*args, *after)

        def body(place, *refs):
            kernel(place, *refs[:read], *refs[read + len(after) :])

    return pl.pallas_call(
        body,
        name=getattr(kernel, "func", kernel).__name__,
        out_shape=outs,
        in_specs=[pl.BlockSpec(memory_space=pltpu.SMEM)] + specs,
        out_specs=[pl.BlockSpec(memory_space=pltpu.VMEM)] * len(outs),
        scratch_shapes=list(scratch),
        compiler_params=pltpu.CompilerParams(vmem_limit_bytes=16 << 20),
        cost_estimate=pl.CostEstimate(flops=0, bytes_accessed=0, transcendentals=0),
    )(place, *args)


def shape(dims, dtype):
    return jax.ShapeDtypeStruct(tuple(dims), dtype)


def times(left, right):
    return jnp.dot(left, right, preferred_element_type=F32)


def against(left, weight):
    return lax.dot_general(left, weight, (((1,), (1,)), ((), ())), preferred_element_type=F32)


def outer(left, right):
    return lax.dot_general(left, right, (((0,), (0,)), ((), ())), preferred_element_type=F32)


def chosen(index, cases):
    result = cases[-1]
    for at in range(len(cases) - 2, -1, -1):
        result = jnp.where(index == at, cases[at], result)
    return result


def of_member(t, member, blocks):
    return chosen(t, [blocks[i ^ member] for i in range(TEAM)])


def column_sum(value):
    return jnp.sum(value, 0, keepdims=True)


def ends_of(block, n):
    row = block[n : n + EXTRA, 0:128].astype(F32)[0:1]
    lane = lax.broadcasted_iota(jnp.int32, (1, 128), 1)
    return [
        jnp.sum(jnp.where(lane <= s, row, 0.0), axis=1, keepdims=True) for s in range(SEQS)
    ]


def segments(ends, dims, axis):
    place = lax.broadcasted_iota(jnp.int32, dims, axis).astype(F32)
    total = jnp.zeros(dims, F32)
    for end in ends:
        total = total + jnp.where(place >= end, 1.0, 0.0)
    return total


def normalise(value):
    centre = jnp.mean(value, -1, keepdims=True)
    offset = value - centre
    spread = jnp.mean(offset * offset, -1, keepdims=True)
    factor = lax.rsqrt(spread + 1e-06)
    return offset * factor, factor


def normalise_back(d_hat, hat, factor):
    return factor * (
        d_hat
        - jnp.mean(d_hat, -1, keepdims=True)
        - hat * jnp.mean(d_hat * hat, -1, keepdims=True)
    )


def grad_tiles(place, n_group, width, left, right, own, near, far, tile):
    depth = n_group // 2
    half = depth // 2
    z, y = place[1], place[2]

    def step(at, carry):
        tile[...] = outer(left[:, pl.ds(pl.multiple_of(at * 2 * width, 2 * width), 2 * width)], right[...])
        k = lax.bitwise_xor(z, at)
        own[k, 0:width, :] = tile[pl.ds(pl.multiple_of(y * width, width), width), :]
        sent = tile[pl.ds(pl.multiple_of((1 - y) * width, width), width), :].astype(BF)

        @pl.when(k < half)
        def _():
            near[k, 0:width, :] = sent

        @pl.when(k >= half)
        def _():
            far[k - half, 0:width, :] = sent

        return carry

    lax.fori_loop(0, depth, step, 0)


def to_team(value, n, near, keep, columns):
    keep[0:n, columns] = value[0:n]
    near[0:n, columns] = value[n : 2 * n].astype(BF)
    keep[n : 2 * n, columns] = value[2 * n : 3 * n]
    near[n : 2 * n, columns] = value[3 * n : 4 * n].astype(BF)


def at_group(place, n_group, i):
    depth = n_group // 2
    dy, k = divmod(i, depth)
    y = place[2]
    return lax.rem(place[1] - k + depth, depth) * 2 + (y if dy == 0 else 1 - y)


def relay_kernel(counts, place, *refs):
    outs = refs[sum(counts) :]
    for out, count in zip(outs, counts):
        parts, refs = refs[:count], refs[count:]
        at = 0
        for part in parts:
            out[at : at + part.shape[0]] = part[...]
            at += part.shape[0]


def relay(place, *tasks, after=()):
    outs = [
        shape((sum(part.shape[0] for part in task), *task[0].shape[1:]), task[0].dtype)
        for task in tasks
    ]
    flat = [part for task in tasks for part in task]
    return call(
        partial(relay_kernel, [len(task) for task in tasks]), outs, place, *flat, after=after
    )


def group_blocks(place, quarters):
    half = quarters[0].shape[0]
    for q, quarter in enumerate(quarters):
        for i in range(half):
            dz, dy = q % 2 * half + i, q // 2
            z = lax.bitwise_xor(place[1], dz)
            yield z * 2 + lax.bitwise_xor(place[2], dy), quarter.at[i]


def assemble(place, quarters, rows, whole):
    for g, block in group_blocks(place, quarters):
        whole[pl.ds(pl.multiple_of(g * rows, rows), rows), :] = block[0:rows]


def prepare_first_kernel(place, att, small, first_o):
    t = place[0]
    d, joint = att.shape
    width = joint // 3
    part = width // TEAM
    for i in range(3):
        first_o[0, 0:d, i * part : (i + 1) * part] = chosen(
            t,
            [
                att[:, i * width + s * part : i * width + (s + 1) * part]
                for s in range(TEAM)
            ],
        )
    first_o[0, d : d + EXTRA, :] = small[...]


def prepare_rest_kernel(n_group, place, hid, back, rest_o):
    t = place[0]
    d = hid.shape[0]
    f = hid.shape[1] // n_group
    w = f // TEAM
    for g in range(n_group):
        rest_o[0:d, g * w : (g + 1) * w] = chosen(
            t, [hid[:, g * f + s * w : g * f + (s + 1) * w] for s in range(TEAM)]
        )
    rest_o[d : d + w, :] = back[pl.ds(pl.multiple_of(t * w, w), w), :]


def attention_kernel(
    n_group, d, f, n, place, p0, p1, p2, p3, own_out, other_out, *refs
):
    first, refs = refs[:4], refs[4:]
    (
        joint_o, probs_o, mixed_o, near_o, keep_o, vec_o, hb_o, wout_o, first_s, token_s, small_s,
    ) = refs
    blocks = (p0, p1, p2, p3)
    t, y = place[0], place[2]
    part = wout_o.shape[0]
    width = wout_o.shape[1]
    w = f // TEAM
    assemble(place, first, d, first_s)
    for g, block in group_blocks(place, first):
        small_s[g] = block[d : d + EXTRA, :].astype(F32)
    small = [small_s[g] for g in range(n_group)]
    vec_o[...] = jnp.concatenate([s[0:8, 0:d] for s in small], 1)
    hb_o[...] = jnp.concatenate(
        [chosen(t, [s[8:9, i * w : (i + 1) * w] for i in range(TEAM)]) for s in small], 1
    )
    for at in range(part // (2 * d)):
        wout_o[pl.ds(pl.multiple_of((at * 2 + y) * d, d), d), :] = own_out[
            at * d : (at + 1) * d
        ]
        wout_o[pl.ds(pl.multiple_of((at * 2 + 1 - y) * d, d), d), :] = other_out[
            at * d : (at + 1) * d
        ]
    for b in range(TEAM):
        token_s[b * n : (b + 1) * n] = blocks[b][0:n]
    mine = pl.ds(pl.multiple_of(t * part, part), part)
    for i in range(3):
        value = times(token_s[...], first_s[:, i * part : (i + 1) * part])
        if i == 0:
            value = value + vec_o[0:1, mine]
        if i == 2:
            value = value + vec_o[1:2, mine]
        joint_o[:, i * part : (i + 1) * part] = value.astype(BF)
    scale = HD ** (-0.5)
    low = lax.broadcasted_iota(jnp.int32, (1, PAIR), 1) < HD
    zero = jnp.zeros((), BF)
    for b in range(TEAM):
        rows = slice(b * n, (b + 1) * n)
        ends = ends_of(blocks[b], n)
        same = segments(ends, (n, 1), 0) == segments(ends, (1, n), 1)
        for pair in range(part // PAIR):
            at = pair * PAIR
            query = joint_o[rows, at : at + PAIR]
            keys = joint_o[rows, part + at : part + at + PAIR]
            values = joint_o[rows, 2 * part + at : 2 * part + at + PAIR]
            mixed = []
            for h in range(2):
                sided = jnp.where(low, query, zero) if h == 0 else jnp.where(low, zero, query)
                scores = jnp.where(same, against(sided, keys) * scale, -1000000000.0)
                expo = jnp.exp(scores - jnp.max(scores, -1, keepdims=True))
                probs = expo / jnp.sum(expo, -1, keepdims=True)
                probs = probs.astype(BF)
                probs_o[(b * (part // PAIR) + pair) * 2 + h] = probs
                mixed.append(times(probs, values))
            mixed_o[rows, at : at + PAIR] = jnp.where(low, mixed[0], mixed[1]).astype(BF)
    for at in range(0, width, part):
        columns = slice(at, at + part)
        to_team(times(mixed_o[...], wout_o[:, columns]), n, near_o, keep_o, columns)


def norm_kernel(place, tokens, keep, got, far, vec, normed_o, low_o, hat_o, factor_o):
    n = tokens.shape[0]
    attn = keep[0:n] + got[0:n].astype(F32) + far[...].astype(F32) + vec[2:3]
    hat, factor = normalise(tokens[...].astype(F32) + attn)
    normed = hat * vec[3:4] + vec[4:5]
    normed_o[...] = normed
    low_o[...] = normed.astype(BF)
    hat_o[...] = hat
    factor_o[...] = jnp.broadcast_to(factor, factor_o.shape)


def gelu_parts(pre):
    bell = 0.5 * (1.0 + lax.erf(pre * (2.0**-0.5)))
    return bell, jnp.exp(-0.5 * pre * pre) * (2.0 * 3.141592653589793) ** -0.5


def feed_kernel(
    n_group, d, place, x0, x1, x2, x3, hb, rest, pre_o, act_o, near_o, keep_o, x_o
):
    n = x0.shape[0]
    w = rest.shape[1] - d
    for b, block in enumerate((x0, x1, x2, x3)):
        x_o[b * n : (b + 1) * n] = block[...]

    def entering(at, carry):
        columns = pl.ds(pl.multiple_of(at * 256, 256), 256)
        weight = rest[:, 0:d, columns].reshape(n_group * d, 256)
        pre = times(x_o[...], weight) + hb[:, columns]
        pre_o[:, columns] = pre
        act_o[:, columns] = (pre * gelu_parts(pre)[0]).astype(BF)
        return carry

    lax.fori_loop(0, pre_o.shape[1] // 256, entering, 0)

    def leaving(at, carry):
        columns = pl.ds(pl.multiple_of(at * 256, 256), 256)
        weight = rest[:, d : d + w, columns].reshape(n_group * w, 256)
        to_team(times(act_o[...], weight), n, near_o, keep_o, columns)
        return carry

    lax.fori_loop(0, keep_o.shape[1] // 256, leaving, 0)


def second_kernel(
    place, normed, keep, got, far, vec, cotangent, packed, layer_o, d_second_o, d_out_o, sums_o
):
    n = normed.shape[0]
    out = keep[0:n] + got[0:n].astype(F32) + far[...].astype(F32) + vec[5:6]
    hat, factor = normalise(normed[...] + out)
    live = jnp.where(segments(ends_of(packed, n), (n, 1), 0) < SEQS, 1.0, 0.0)
    layer_o[...] = ((hat * vec[6:7] + vec[7:8]) * live).astype(BF)
    d_final = cotangent[...].astype(F32) * live
    d_second = normalise_back(d_final * vec[6:7], hat, factor)
    d_second_o[...] = d_second
    d_out = d_second.astype(BF)
    d_out_o[...] = d_out
    sums_o[...] = jnp.zeros_like(sums_o)
    sums_o[0:1] = column_sum(d_out.astype(F32))
    sums_o[1:2] = column_sum(d_final * hat)
    sums_o[2:3] = column_sum(d_final)


def back_grad_kernel(place, d0, d1, d2, d3, act, grad_o, d_out_o):
    n = d0.shape[0]
    for b, block in enumerate((d0, d1, d2, d3)):
        d_out_o[b * n : (b + 1) * n] = block[...]

    def step(at, carry):
        rows = pl.ds(pl.multiple_of(at * 256, 256), 256)
        grad_o[rows, :] = outer(act[:, rows], d_out_o[...]).astype(BF)
        return carry

    lax.fori_loop(0, grad_o.shape[0] // 256, step, 0)


def feed_back_kernel(n_group, d, n, place, d_out, rest, pre, d_pre_o, near_o, keep_o, hb_o):
    w = rest.shape[1] - d
    per = 256 // w

    def through(at, carry):
        columns = pl.ds(pl.multiple_of(at * 256, 256), 256)
        weight = rest[pl.ds(at * per, per), d : d + w, :].reshape(256, rest.shape[2])
        d_act = against(d_out[...], weight)
        value = pre[:, columns]
        bell, slope = gelu_parts(value)
        d_pre = (d_act * (bell + value * slope)).astype(BF)
        d_pre_o[:, columns] = d_pre
        hb_o[:, columns] = column_sum(d_pre.astype(F32))
        return carry

    lax.fori_loop(0, pre.shape[1] // 256, through, 0)
    rows = 256 // d

    def entering(at, carry):
        columns = pl.ds(pl.multiple_of(at * 256, 256), 256)
        weight = rest[pl.ds(at * rows, rows), 0:d, :].reshape(256, rest.shape[2])
        to_team(against(d_pre_o[...], weight), n, near_o, keep_o, columns)
        return carry

    lax.fori_loop(0, keep_o.shape[1] // 256, entering, 0)


def hidden_grad_kernel(n_group, d, place, x, d_pre, own_o, near_o, far_o, tile):
    grad_tiles(place, n_group, d, x, d_pre, own_o, near_o, far_o, tile)


def norm_back_kernel(
    place, d_second, keep, got, far, hat, factor, vec, d_first_o, d_attn_o, sums_o
):
    n = d_second.shape[0]
    d_normed = d_second[...] + keep[0:n] + got[0:n].astype(F32) + far[...].astype(F32)
    d_first = normalise_back(d_normed * vec[3:4], hat[...], factor[:, 0:1])
    d_first_o[...] = d_first
    d_attn = d_first.astype(BF)
    d_attn_o[...] = d_attn
    sums_o[...] = jnp.zeros_like(sums_o)
    sums_o[0:1] = column_sum(d_attn.astype(F32))
    sums_o[1:2] = column_sum(d_normed * hat[...])
    sums_o[2:3] = column_sum(d_normed)


def attention_back_kernel(
    n_group, d, f, n, place, a0, a1, a2, a3, wout, joint, probs_in, p0, p1, p2, p3,
    sums1, sums2, d_hb,
    d_joint_o, own_o, near_o, far_o, attn_o, token_s, tile, vec_s, small_s,
):
    t, z, y = place[0], place[1], place[2]
    depth = n_group // 2
    part = wout.shape[0]
    w = f // TEAM
    for b in range(TEAM):
        token_s[b * n : (b + 1) * n] = (p0, p1, p2, p3)[b][0:n]
        attn_o[b * n : (b + 1) * n] = (a0, a1, a2, a3)[b][...]
    d_mixed = against(attn_o[...], wout[...]).astype(BF)
    scale = HD ** (-0.5)
    low = lax.broadcasted_iota(jnp.int32, (1, PAIR), 1) < HD
    zero = jnp.zeros((), BF)
    for b in range(TEAM):
        rows = slice(b * n, (b + 1) * n)
        for pair in range(part // PAIR):
            at = pair * PAIR
            query = joint[rows, at : at + PAIR]
            keys = joint[rows, part + at : part + at + PAIR]
            values = joint[rows, 2 * part + at : 2 * part + at + PAIR]
            d_mix = d_mixed[rows, at : at + PAIR]
            d_query, d_keys, d_values = [], [], []
            for h in range(2):
                low_probs = probs_in[(b * (part // PAIR) + pair) * 2 + h]
                probs = low_probs.astype(F32)
                sided = jnp.where(low, d_mix, zero) if h == 0 else jnp.where(low, zero, d_mix)
                d_probs = against(sided, values)
                d_scores = (
                    probs * (d_probs - jnp.sum(probs * d_probs, -1, keepdims=True))
                ).astype(BF)
                d_values.append(outer(low_probs, d_mix))
                d_query.append(times(d_scores, keys))
                d_keys.append(outer(d_scores, query))
            for i, (value, factor) in enumerate(
                ((d_query, scale), (d_keys, scale), (d_values, 1.0))
            ):
                d_joint_o[rows, i * part + at : i * part + at + PAIR] = (
                    jnp.where(low, value[0], value[1]) * factor
                ).astype(BF)
    vec_s[...] = jnp.zeros_like(vec_s)
    mine = pl.ds(pl.multiple_of(t * part, part), part)
    vec_s[0:1, mine] = column_sum(d_joint_o[:, 0:part].astype(F32))
    vec_s[1:2, mine] = column_sum(d_joint_o[:, 2 * part : 3 * part].astype(F32))
    vec_s[2:5, :] = sums1[0:3]
    vec_s[5:8, :] = sums2[0:3]
    small_s[...] = jnp.zeros_like(small_s)
    for g in range(n_group):
        small_s[g, 0:8, 0:d] = vec_s[:, g * d : (g + 1) * d]
        row = d_hb[:, g * w : (g + 1) * w]
        small_s[g, 8:9, 0:f] = jnp.concatenate(
            [jnp.where(t == i, row, jnp.zeros_like(row)) for i in range(TEAM)], 1
        )
    grad_tiles(place, n_group, d, token_s, d_joint_o, own_o, near_o, far_o, tile)
    half = depth // 2
    for k in range(depth):
        g = lax.bitwise_xor(z, k) * 2
        own_o[k, d : d + EXTRA, :] = small_s[g + y]
        sent_o = far_o if k >= half else near_o
        sent_o[k % half, d : d + EXTRA, :] = small_s[g + 1 - y].astype(BF)


def token_back_kernel(
    n, d, place, d_joint, mixed, d_attn, f0, f1, f2, f3,
    near_o, keep_o, out_own_o, out_other_o, heads_s, first_s,
):
    y = place[2]
    assemble(place, (f0, f1, f2, f3), d, first_s)
    heads_s[...] = outer(mixed[...], d_attn[...])
    for at in range(mixed.shape[1] // (2 * d)):
        out_own_o[at * d : (at + 1) * d] = heads_s[
            pl.ds(pl.multiple_of((at * 2 + y) * d, d), d), :
        ]
        out_other_o[at * d : (at + 1) * d] = heads_s[
            pl.ds(pl.multiple_of((at * 2 + 1 - y) * d, d), d), :
        ].astype(BF)

    def step(at, carry):
        columns = pl.ds(pl.multiple_of(at * 256, 256), 256)
        to_team(against(d_joint[...], first_s[columns, :]), n, near_o, keep_o, columns)
        return carry

    lax.fori_loop(0, keep_o.shape[1] // 256, step, 0)


def add_far_kernel(place, own, got, sum_o):
    half = sum_o.shape[0]
    sum_o[...] = (own[half : 2 * half] + got[0:half].astype(F32)).astype(BF)


def add_near_kernel(place, own, got, far, keep_o, send_o):
    half = far.shape[0]
    total = own[0:half] + got[got.shape[0] - half :].astype(F32) + far[...].astype(F32)
    keep_o[...] = total[0 : half // 2]
    send_o[...] = total[half // 2 :].astype(BF)


def back_out_kernel(place, b0, b1, b2, b3, back_o):
    w = b0.shape[0]
    for i in range(TEAM):
        block = of_member(place[0], i, [b[...] for b in (b0, b1, b2, b3)])
        back_o[i * w : (i + 1) * w] = block.astype(F32)


def hidden_out_kernel(n_group, place, h0, h1, h2, h3, hidden_o):
    w = h0.shape[1] // n_group
    for i in range(TEAM):
        block = of_member(place[0], i, [h[...] for h in (h0, h1, h2, h3)]).astype(F32)
        for g in range(n_group):
            at = (g * TEAM + i) * w
            hidden_o[:, at : at + w] = block[:, g * w : (g + 1) * w]


def attention_out_kernel(f, place, j0, j1, j2, j3, out, joint_o, out_o, *small_o):
    t = place[0]
    d = out_o.shape[0]
    part = j0.shape[1] // 3
    width = part * TEAM
    total = jnp.zeros((EXTRA, 3 * part), F32)
    for i in range(TEAM):
        block = of_member(t, i, [j[...] for j in (j0, j1, j2, j3)]).astype(F32)
        for s in range(3):
            at = s * width + i * part
            joint_o[:, at : at + part] = block[0:d, s * part : (s + 1) * part]
        total = total + block[d : d + EXTRA]
    out_o[...] = out[...].astype(F32)
    for i in range(8):
        small_o[i][...] = total[i : i + 1, 0:d]
    small_o[8][...] = total[8:9, 0:f]


def shards(
    tokens,
    lengths,
    cotangent,
    attention_in,
    query_bias,
    value_bias,
    attention_out,
    out_bias,
    first_gain,
    first_shift,
    hidden_in,
    hidden_bias,
    hidden_out,
    output_bias,
    second_gain,
    second_shift,
):
    at = Places()
    n_group, depth, place = at.n_group, at.depth, at.place
    n, width = tokens.shape
    d = attention_in.shape[0]
    f = hidden_bias.shape[0]
    w = f // TEAM
    part = width // TEAM
    inner = w * n_group
    all_rows = TEAM * n

    vectors = (
        query_bias,
        value_bias,
        out_bias,
        first_gain,
        first_shift,
        output_bias,
        second_gain,
        second_shift,
    )
    small = jnp.concatenate(
        [
            jnp.pad(jnp.stack(vectors), ((0, 0), (0, 3 * part - d))),
            jnp.pad(hidden_bias[None], ((0, EXTRA - 9), (0, 3 * part - f))),
        ],
        0,
    )
    extra = jnp.pad(lengths.astype(BF), ((0, EXTRA - 1), (0, width - lengths.shape[1])))
    packed = jnp.concatenate([tokens, extra], 0)
    (first_near,) = call(
        prepare_first_kernel,
        [shape((1, d + EXTRA, 3 * part), BF)],
        place,
        attention_in,
        small,
    )
    def widen(blocks):
        for flip in list(at.steps_down(at.half // 2))[::-1]:
            blocks = (blocks, at.send_z(blocks, flip))
            if flip < at.half // 2:
                (blocks,) = relay(place, blocks)
        return blocks

    heads_mine, heads_first = [], []
    for i in range(at.heads_at):
        home = at.t * at.heads_at + i
        value = jnp.where(at.z == home, attention_out, jnp.zeros_like(attention_out))
        for flip in at.steps_down(at.half):
            value = value + at.send_heads(value, i, flip, False)
            if flip == at.half:
                heads_first.append(value)
        heads_mine.append(value)
    out_mine = jnp.concatenate(heads_mine, 0)
    out_other = at.send_y(out_mine)
    packed_far = at.send_team(packed, 2)
    packed = [packed, at.send_team(packed, 1), packed_far, at.send_team(packed_far, 1)]

    (first_near,) = relay(place, widen(first_near), after=heads_first)
    (rest_mine,) = call(
        partial(prepare_rest_kernel, n_group),
        [shape((d + w, width), BF)],
        place,
        hidden_in,
        hidden_out,
        after=[first_near],
    )
    rest_all = lax.all_gather(rest_mine, "group", axis=0)
    first_far = at.other_half(first_near)
    first_near_y = at.send_y(first_near)
    (first_sent,) = relay(place, (first_far,), after=[first_near_y, out_other, *packed])
    first_all = [first_near, first_far, first_near_y, at.send_y(first_sent)]

    joint, probs, mixed, near, keep, vec, hb, w_out = call(
        partial(attention_kernel, n_group, d, f, n),
        [
            shape((all_rows, 3 * part), BF),
            shape((TEAM * H // TEAM, n, n), BF),
            shape((all_rows, part), BF),
            shape((2 * n, width), BF),
            shape((2 * n, width), F32),
            shape((8, width), F32),
            shape((1, inner), F32),
            shape((part, width), BF),
        ],
        place,
        *packed,
        out_mine,
        out_other,
        *first_all,
        scratch=[
            pltpu.VMEM((width, 3 * part), BF),
            pltpu.VMEM((all_rows, width), BF),
            pltpu.VMEM((n_group, EXTRA, 3 * part), F32),
        ],
    )
    normed, normed_low, hat, factor = call(
        norm_kernel,
        [
            shape((n, width), F32),
            shape((n, width), BF),
            shape((n, width), F32),
            shape((n, 128), F32),
        ],
        place,
        tokens,
        *at.scatter_team(near, keep),
        vec,
    )

    pre, act, near, keep, normed4 = call(
        partial(feed_kernel, n_group, d),
        [
            shape((all_rows, inner), F32),
            shape((all_rows, inner), BF),
            shape((2 * n, width), BF),
            shape((2 * n, width), F32),
            shape((all_rows, width), BF),
        ],
        place,
        *at.gather_team(normed_low),
        hb,
        rest_all,
    )
    layer_out, d_second, d_out, sums2 = call(
        second_kernel,
        [
            shape((n, width), BF),
            shape((n, width), F32),
            shape((n, width), BF),
            shape((8, width), F32),
        ],
        place,
        normed,
        *at.scatter_team(near, keep),
        vec,
        cotangent,
        packed[0],
    )

    def add_near(own, came_y, came_z, after=()):
        half, *rest = came_z.shape
        return call(
            add_near_kernel,
            [shape((half // 2, *rest), F32), shape((half // 2, *rest), BF)],
            place,
            own,
            came_y,
            came_z,
            after=after,
        )

    def sum_group(keep, send):
        flip = at.half // 2
        while flip > 1:
            total = keep + at.send_z(send, flip).astype(F32)
            flip //= 2
            keep, send = total[:flip], total[flip:].astype(BF)
        return at.over_copies((keep + at.send_z(send, 1).astype(F32))[0].astype(BF))

    half = depth // 2
    def add_far(own, came, after=()):
        half, rest = own.shape[0] // 2, own.shape[1:]
        return call(add_far_kernel, [shape((half, *rest), BF)], place, own, came, after=after)[0]

    grad_back, d_out4 = call(
        back_grad_kernel,
        [shape((inner, width), BF), shape((all_rows, width), BF)],
        place,
        *at.gather_team(d_out),
        act,
    )
    g_back = at.over_copies(
        lax.psum_scatter(grad_back, "group", scatter_dimension=0, tiled=True)
    )
    d_pre, near, keep, d_hb = call(
        partial(feed_back_kernel, n_group, d, n),
        [
            shape((all_rows, inner), BF),
            shape((2 * n, width), BF),
            shape((2 * n, width), F32),
            shape((1, inner), F32),
        ],
        place,
        d_out4,
        rest_all,
        pre,
    )
    own_hidden, near_hidden, far_hidden = call(
        partial(hidden_grad_kernel, n_group, d),
        [shape((depth, d, inner), F32)] + [shape((half, d, inner), BF)] * 2,
        place,
        normed4,
        d_pre,
        scratch=[pltpu.VMEM((2 * d, inner), F32)],
    )
    d_first, d_attn, sums1 = call(
        norm_back_kernel,
        [shape((n, width), F32), shape((n, width), BF), shape((8, width), F32)],
        place,
        d_second,
        *at.scatter_team(near, keep),
        hat,
        factor,
        vec,
        after=[far_hidden],
    )
    heads_rows = at.heads_at * d
    sent_hidden = add_far(own_hidden, at.send_y(far_hidden))
    came_hidden = at.other_half(sent_hidden)
    d_joint, own_joint, near_joint, far_joint, d_attn4 = call(
        partial(attention_back_kernel, n_group, d, f, n),
        [
            shape((all_rows, 3 * part), BF),
            shape((depth, d + EXTRA, 3 * part), F32),
            shape((half, d + EXTRA, 3 * part), BF),
            shape((half, d + EXTRA, 3 * part), BF),
            shape((all_rows, width), BF),
        ],
        place,
        *at.gather_team(d_attn),
        w_out,
        joint,
        probs,
        *packed,
        sums1,
        sums2,
        d_hb,
        after=[sent_hidden],
        scratch=[
            pltpu.VMEM((all_rows, width), BF),
            pltpu.VMEM((2 * d, 3 * part), F32),
            pltpu.VMEM((8, width), F32),
            pltpu.VMEM((n_group, EXTRA, 3 * part), F32),
        ],
    )
    sent_joint = add_far(own_joint, at.send_y(far_joint), [came_hidden])
    (sent_y,) = relay(place, (near_hidden,), after=[sent_joint])
    came_joint = at.other_half(sent_joint)
    hidden_parts = add_near(own_hidden, at.send_y(sent_y), came_hidden)
    g_hidden = sum_group(*hidden_parts)
    back_far = at.send_team(g_back, 2)
    joint_parts = add_near(own_joint, at.send_y(near_joint), came_joint, [back_far])
    g_joint = sum_group(*joint_parts)
    near, keep, out_own, out_sent = call(
        partial(token_back_kernel, n, d),
        [
            shape((2 * n, width), BF),
            shape((2 * n, width), F32),
            shape((heads_rows, width), F32),
            shape((heads_rows, width), BF),
        ],
        place,
        d_joint,
        mixed,
        d_attn4,
        *first_all,
        after=[],
        scratch=[pltpu.VMEM((part, width), F32), pltpu.VMEM((width, 3 * part), BF)],
    )
    kept, got, far = at.scatter_team(near, keep)
    out_sum = out_own + at.send_y(out_sent).astype(F32)
    g_out = jnp.zeros((d, width), F32)
    for i in range(at.heads_at):
        block = out_sum[i * d : (i + 1) * d]
        flips = list(at.steps_down(at.half))[::-1]
        for flip in flips:
            block = block + at.send_heads(block.astype(BF), i, flip, True).astype(F32)
        here = at.z == at.t * at.heads_at + i
        g_out = g_out + jnp.where(here, block, jnp.zeros_like(block))
    g_out = at.over_copies(g_out.astype(BF))
    grad_tokens = d_first + kept[:n] + got[:n].astype(F32) + far.astype(F32)

    (g_hidden_out,) = call(
        back_out_kernel, [shape((f, width), F32)], place, g_back, at.send_team(g_back, 1), back_far, at.send_team(back_far, 1)
    )
    (g_hidden_in,) = call(
        partial(hidden_out_kernel, n_group),
        [shape((d, TEAM * inner), F32)],
        place,
        *at.gather_team(g_hidden),
    )
    joint_far = at.send_team(g_joint, 2)
    (joint_sent,) = relay(place, (joint_far,), after=[g_hidden_out, g_hidden_in, grad_tokens])
    g_attention_in, g_attention_out, *g_small = call(
        partial(attention_out_kernel, f),
        [shape((d, 3 * width), F32), shape((d, width), F32)]
        + [shape((1, d), F32)] * 8
        + [shape((1, f), F32)],
        place,
        g_joint,
        at.send_team(g_joint, 1),
        joint_far,
        at.send_team(joint_sent, 1),
        at.spread_heads(g_out),
    )
    g_qb, g_vb, g_ob, g_g1, g_s1, g_outb, g_g2, g_s2, g_hb = (v.reshape(-1) for v in g_small)
    return (
        layer_out,
        grad_tokens,
        g_attention_in,
        g_qb,
        g_vb,
        g_attention_out,
        g_ob,
        g_g1,
        g_s1,
        g_hidden_in,
        g_hb,
        g_hidden_out,
        g_outb,
        g_g2,
        g_s2,
    )


def solution(mesh):
    rows = P(("replica", "group"), None)
    matrix = P("group", None)
    vector = P("group")
    params = (
        matrix,
        vector,
        vector,
        matrix,
        vector,
        vector,
        vector,
        matrix,
        vector,
        matrix,
        vector,
        vector,
        vector,
    )
    return jax.shard_map(
        shards,
        mesh=mesh,
        in_specs=(rows, rows, rows) + params,
        out_specs=(rows, rows) + params,
        check_vma=False,
    )
```

```python
from functools import partial

import jax
import jax.numpy as jnp
from jax import lax
from jax.experimental import pallas as pl
from jax.experimental.pallas import tpu as pltpu
from jax.sharding import PartitionSpec as P

H = 16
HD = 64
SEQS = 4
TEAM = 4
EXTRA = 16
PAIR = 2 * HD
BF = jnp.bfloat16
F32 = jnp.float32


class Places:
    def __init__(self):
        self.n_group = lax.axis_size("group")
        self.n_replica = lax.axis_size("replica")
        self.depth = self.n_group // 2
        self.half = self.depth // 2
        self.heads_at = self.depth // TEAM
        place = lax.axis_index("group")
        self.z = place // 2
        self.t = lax.axis_index("replica") % TEAM
        self.place = jnp.stack([self.t, self.z, place % 2]).astype(jnp.int32)

    def send_z(self, value, flip):
        return lax.ppermute(
            value, "group", [(g, g ^ (2 * flip)) for g in range(self.n_group)]
        )

    def send_y(self, value):
        return lax.ppermute(value, "group", [(g, g ^ 1) for g in range(self.n_group)])

    def send_team(self, value, flip):
        return lax.ppermute(value, "replica", [(r, r ^ flip) for r in range(self.n_replica)])

    def send_heads(self, value, at, flip, back):
        pairs = []
        for r in range(self.n_replica):
            home = r % TEAM * self.heads_at + at
            for z in range(self.depth):
                if (z ^ home) & (2 * flip - 1) == 0:
                    for y in range(2):
                        near = r * self.n_group + z * 2 + y
                        pairs.append((near ^ (2 * flip), near) if back else (near, near ^ (2 * flip)))
        return lax.ppermute(value, ("replica", "group"), pairs)

    def steps_down(self, top):
        while top >= 1:
            yield top
            top //= 2

    def other_half(self, blocks):
        return self.send_z(blocks, self.half)

    def spread_heads(self, block):
        for flip in (2, 1):
            pairs = []
            for r in range(self.n_replica):
                for g in range(self.n_group):
                    apart = r % TEAM ^ g // 2 // self.heads_at
                    if apart == 0 or (flip == 1 and apart == 2):
                        pairs.append((r * self.n_group + g, (r ^ flip) * self.n_group + g))
            block = block + lax.ppermute(block, ("replica", "group"), pairs)
        return block

    def gather_team(self, block):
        far = self.send_team(block, 2)
        near = self.send_team(block, 1)
        return [block, near, far, self.send_team(far, 1)]

    def scatter_near(self, near, keep):
        n = near.shape[0] // 2
        got = self.send_team(near, 1)
        return got, (keep[n:] + got[n:].astype(F32)).astype(BF)

    def scatter_team(self, near, keep):
        got, sent = self.scatter_near(near, keep)
        return keep, got, self.send_team(sent, 2)

    def over_copies(self, value):
        teams = self.n_replica // TEAM
        if teams == 1:
            return value
        return lax.psum(
            value,
            "replica",
            axis_index_groups=[
                [team * TEAM + t for team in range(teams)] for t in range(TEAM)
            ],
        )


def call(kernel, outs, place, *args, scratch=(), after=()):
    specs = [pl.BlockSpec(memory_space=pltpu.VMEM)] * len(args)
    body = kernel
    if after:
        read = len(args)
        specs += [pl.BlockSpec(memory_space=pl.ANY)] * len(after)
        args = (*args, *after)

        def body(place, *refs):
            kernel(place, *refs[:read], *refs[read + len(after) :])

    return pl.pallas_call(
        body,
        name=getattr(kernel, "func", kernel).__name__,
        out_shape=outs,
        in_specs=[pl.BlockSpec(memory_space=pltpu.SMEM)] + specs,
        out_specs=[pl.BlockSpec(memory_space=pltpu.VMEM)] * len(outs),
        scratch_shapes=list(scratch),
        compiler_params=pltpu.CompilerParams(vmem_limit_bytes=16 << 20),
        cost_estimate=pl.CostEstimate(flops=0, bytes_accessed=0, transcendentals=0),
    )(place, *args)


def shape(dims, dtype):
    return jax.ShapeDtypeStruct(tuple(dims), dtype)


def times(left, right):
    return jnp.dot(left, right, preferred_element_type=F32)


def against(left, weight):
    return lax.dot_general(left, weight, (((1,), (1,)), ((), ())), preferred_element_type=F32)


def outer(left, right):
    return lax.dot_general(left, right, (((0,), (0,)), ((), ())), preferred_element_type=F32)


def chosen(index, cases):
    result = cases[-1]
    for at in range(len(cases) - 2, -1, -1):
        result = jnp.where(index == at, cases[at], result)
    return result


def of_member(t, member, blocks):
    return chosen(t, [blocks[i ^ member] for i in range(TEAM)])


def column_sum(value):
    return jnp.sum(value, 0, keepdims=True)


def ends_of(block, n):
    row = block[n : n + EXTRA, 0:128].astype(F32)[0:1]
    lane = lax.broadcasted_iota(jnp.int32, (1, 128), 1)
    return [
        jnp.sum(jnp.where(lane <= s, row, 0.0), axis=1, keepdims=True) for s in range(SEQS)
    ]


def segments(ends, dims, axis):
    place = lax.broadcasted_iota(jnp.int32, dims, axis).astype(F32)
    total = jnp.zeros(dims, F32)
    for end in ends:
        total = total + jnp.where(place >= end, 1.0, 0.0)
    return total


def normalise(value):
    centre = jnp.mean(value, -1, keepdims=True)
    offset = value - centre
    spread = jnp.mean(offset * offset, -1, keepdims=True)
    factor = lax.rsqrt(spread + 1e-06)
    return offset * factor, factor


def normalise_back(d_hat, hat, factor):
    return factor * (
        d_hat
        - jnp.mean(d_hat, -1, keepdims=True)
        - hat * jnp.mean(d_hat * hat, -1, keepdims=True)
    )


def grad_tiles(place, n_group, width, left, right, own, near, far, tile):
    depth = n_group // 2
    half = depth // 2
    z, y = place[1], place[2]

    def step(at, carry):
        tile[...] = outer(left[:, pl.ds(pl.multiple_of(at * 2 * width, 2 * width), 2 * width)], right[...])
        k = lax.bitwise_xor(z, at)
        own[k, 0:width, :] = tile[pl.ds(pl.multiple_of(y * width, width), width), :]
        sent = tile[pl.ds(pl.multiple_of((1 - y) * width, width), width), :].astype(BF)

        @pl.when(k < half)
        def _():
            near[k, 0:width, :] = sent

        @pl.when(k >= half)
        def _():
            far[k - half, 0:width, :] = sent

        return carry

    lax.fori_loop(0, depth, step, 0)


def to_team(value, n, near, keep, columns):
    keep[0:n, columns] = value[0:n]
    near[0:n, columns] = value[n : 2 * n].astype(BF)
    keep[n : 2 * n, columns] = value[2 * n : 3 * n]
    near[n : 2 * n, columns] = value[3 * n : 4 * n].astype(BF)


def at_group(place, n_group, i):
    depth = n_group // 2
    dy, k = divmod(i, depth)
    y = place[2]
    return lax.rem(place[1] - k + depth, depth) * 2 + (y if dy == 0 else 1 - y)


def relay_kernel(counts, place, *refs):
    outs = refs[sum(counts) :]
    for out, count in zip(outs, counts):
        parts, refs = refs[:count], refs[count:]
        at = 0
        for part in parts:
            out[at : at + part.shape[0]] = part[...]
            at += part.shape[0]


def relay(place, *tasks, after=()):
    outs = [
        shape((sum(part.shape[0] for part in task), *task[0].shape[1:]), task[0].dtype)
        for task in tasks
    ]
    flat = [part for task in tasks for part in task]
    return call(
        partial(relay_kernel, [len(task) for task in tasks]), outs, place, *flat, after=after
    )


def group_blocks(place, quarters):
    half = quarters[0].shape[0]
    for q, quarter in enumerate(quarters):
        for i in range(half):
            dz, dy = q % 2 * half + i, q // 2
            z = lax.bitwise_xor(place[1], dz)
            yield z * 2 + lax.bitwise_xor(place[2], dy), quarter.at[i]


def assemble(place, quarters, rows, whole):
    for g, block in group_blocks(place, quarters):
        whole[pl.ds(pl.multiple_of(g * rows, rows), rows), :] = block[0:rows]


def prepare_first_kernel(place, att, small, first_o):
    t = place[0]
    d, joint = att.shape
    width = joint // 3
    part = width // TEAM
    for i in range(3):
        first_o[0, 0:d, i * part : (i + 1) * part] = chosen(
            t,
            [
                att[:, i * width + s * part : i * width + (s + 1) * part]
                for s in range(TEAM)
            ],
        )
    first_o[0, d : d + EXTRA, :] = small[...]


def prepare_rest_kernel(n_group, place, hid, back, rest_o):
    t = place[0]
    d = hid.shape[0]
    f = hid.shape[1] // n_group
    w = f // TEAM
    for g in range(n_group):
        rest_o[0:d, g * w : (g + 1) * w] = chosen(
            t, [hid[:, g * f + s * w : g * f + (s + 1) * w] for s in range(TEAM)]
        )
    rest_o[d : d + w, :] = back[pl.ds(pl.multiple_of(t * w, w), w), :]


def attention_kernel(
    n_group, d, f, n, place, p0, p1, p2, p3, own_out, other_out, *refs
):
    first, refs = refs[:4], refs[4:]
    (
        joint_o, probs_o, mixed_o, near_o, keep_o, vec_o, hb_o, wout_o, first_s, token_s, small_s,
    ) = refs
    blocks = (p0, p1, p2, p3)
    t, y = place[0], place[2]
    part = wout_o.shape[0]
    width = wout_o.shape[1]
    w = f // TEAM
    assemble(place, first, d, first_s)
    for g, block in group_blocks(place, first):
        small_s[g] = block[d : d + EXTRA, :].astype(F32)
    small = [small_s[g] for g in range(n_group)]
    vec_o[...] = jnp.concatenate([s[0:8, 0:d] for s in small], 1)
    hb_o[...] = jnp.concatenate(
        [chosen(t, [s[8:9, i * w : (i + 1) * w] for i in range(TEAM)]) for s in small], 1
    )
    for at in range(part // (2 * d)):
        wout_o[pl.ds(pl.multiple_of((at * 2 + y) * d, d), d), :] = own_out[
            at * d : (at + 1) * d
        ]
        wout_o[pl.ds(pl.multiple_of((at * 2 + 1 - y) * d, d), d), :] = other_out[
            at * d : (at + 1) * d
        ]
    for b in range(TEAM):
        token_s[b * n : (b + 1) * n] = blocks[b][0:n]
    mine = pl.ds(pl.multiple_of(t * part, part), part)
    for i in range(3):
        value = times(token_s[...], first_s[:, i * part : (i + 1) * part])
        if i == 0:
            value = value + vec_o[0:1, mine]
        if i == 2:
            value = value + vec_o[1:2, mine]
        joint_o[:, i * part : (i + 1) * part] = value.astype(BF)
    scale = HD ** (-0.5)
    low = lax.broadcasted_iota(jnp.int32, (1, PAIR), 1) < HD
    zero = jnp.zeros((), BF)
    for b in range(TEAM):
        rows = slice(b * n, (b + 1) * n)
        ends = ends_of(blocks[b], n)
        same = segments(ends, (n, 1), 0) == segments(ends, (1, n), 1)
        for pair in range(part // PAIR):
            at = pair * PAIR
            query = joint_o[rows, at : at + PAIR]
            keys = joint_o[rows, part + at : part + at + PAIR]
            values = joint_o[rows, 2 * part + at : 2 * part + at + PAIR]
            mixed = []
            for h in range(2):
                sided = jnp.where(low, query, zero) if h == 0 else jnp.where(low, zero, query)
                scores = jnp.where(same, against(sided, keys) * scale, -1000000000.0)
                expo = jnp.exp(scores - jnp.max(scores, -1, keepdims=True))
                probs = expo / jnp.sum(expo, -1, keepdims=True)
                probs = probs.astype(BF)
                probs_o[(b * (part // PAIR) + pair) * 2 + h] = probs
                mixed.append(times(probs, values))
            mixed_o[rows, at : at + PAIR] = jnp.where(low, mixed[0], mixed[1]).astype(BF)
    for at in range(0, width, part):
        columns = slice(at, at + part)
        to_team(times(mixed_o[...], wout_o[:, columns]), n, near_o, keep_o, columns)


def norm_kernel(place, tokens, keep, got, far, vec, normed_o, low_o, hat_o, factor_o):
    n = tokens.shape[0]
    attn = keep[0:n] + got[0:n].astype(F32) + far[...].astype(F32) + vec[2:3]
    hat, factor = normalise(tokens[...].astype(F32) + attn)
    normed = hat * vec[3:4] + vec[4:5]
    normed_o[...] = normed
    low_o[...] = normed.astype(BF)
    hat_o[...] = hat
    factor_o[...] = jnp.broadcast_to(factor, factor_o.shape)


def gelu_parts(pre):
    bell = 0.5 * (1.0 + lax.erf(pre * (2.0**-0.5)))
    return bell, jnp.exp(-0.5 * pre * pre) * (2.0 * 3.141592653589793) ** -0.5


def feed_kernel(
    n_group, d, place, x0, x1, x2, x3, hb, rest, pre_o, act_o, near_o, keep_o, x_o
):
    n = x0.shape[0]
    w = rest.shape[1] - d
    for b, block in enumerate((x0, x1, x2, x3)):
        x_o[b * n : (b + 1) * n] = block[...]

    def entering(at, carry):
        columns = pl.ds(pl.multiple_of(at * 256, 256), 256)
        weight = rest[:, 0:d, columns].reshape(n_group * d, 256)
        pre = times(x_o[...], weight) + hb[:, columns]
        pre_o[:, columns] = pre
        act_o[:, columns] = (pre * gelu_parts(pre)[0]).astype(BF)
        return carry

    lax.fori_loop(0, pre_o.shape[1] // 256, entering, 0)

    def leaving(at, carry):
        columns = pl.ds(pl.multiple_of(at * 256, 256), 256)
        weight = rest[:, d : d + w, columns].reshape(n_group * w, 256)
        to_team(times(act_o[...], weight), n, near_o, keep_o, columns)
        return carry

    lax.fori_loop(0, keep_o.shape[1] // 256, leaving, 0)


def second_kernel(
    place, normed, keep, got, far, vec, cotangent, packed, layer_o, d_second_o, d_out_o, sums_o
):
    n = normed.shape[0]
    out = keep[0:n] + got[0:n].astype(F32) + far[...].astype(F32) + vec[5:6]
    hat, factor = normalise(normed[...] + out)
    live = jnp.where(segments(ends_of(packed, n), (n, 1), 0) < SEQS, 1.0, 0.0)
    layer_o[...] = ((hat * vec[6:7] + vec[7:8]) * live).astype(BF)
    d_final = cotangent[...].astype(F32) * live
    d_second = normalise_back(d_final * vec[6:7], hat, factor)
    d_second_o[...] = d_second
    d_out = d_second.astype(BF)
    d_out_o[...] = d_out
    sums_o[...] = jnp.zeros_like(sums_o)
    sums_o[0:1] = column_sum(d_out.astype(F32))
    sums_o[1:2] = column_sum(d_final * hat)
    sums_o[2:3] = column_sum(d_final)


def back_grad_kernel(place, d0, d1, d2, d3, act, grad_o, d_out_o):
    n = d0.shape[0]
    for b, block in enumerate((d0, d1, d2, d3)):
        d_out_o[b * n : (b + 1) * n] = block[...]

    def step(at, carry):
        rows = pl.ds(pl.multiple_of(at * 256, 256), 256)
        grad_o[rows, :] = outer(act[:, rows], d_out_o[...]).astype(BF)
        return carry

    lax.fori_loop(0, grad_o.shape[0] // 256, step, 0)


def feed_back_kernel(n_group, d, n, place, d_out, rest, pre, d_pre_o, near_o, keep_o, hb_o):
    w = rest.shape[1] - d
    per = 256 // w

    def through(at, carry):
        columns = pl.ds(pl.multiple_of(at * 256, 256), 256)
        weight = rest[pl.ds(at * per, per), d : d + w, :].reshape(256, rest.shape[2])
        d_act = against(d_out[...], weight)
        value = pre[:, columns]
        bell, slope = gelu_parts(value)
        d_pre = (d_act * (bell + value * slope)).astype(BF)
        d_pre_o[:, columns] = d_pre
        hb_o[:, columns] = column_sum(d_pre.astype(F32))
        return carry

    lax.fori_loop(0, pre.shape[1] // 256, through, 0)
    rows = 256 // d

    def entering(at, carry):
        columns = pl.ds(pl.multiple_of(at * 256, 256), 256)
        weight = rest[pl.ds(at * rows, rows), 0:d, :].reshape(256, rest.shape[2])
        to_team(against(d_pre_o[...], weight), n, near_o, keep_o, columns)
        return carry

    lax.fori_loop(0, keep_o.shape[1] // 256, entering, 0)


def hidden_grad_kernel(n_group, d, place, x, d_pre, own_o, near_o, far_o, tile):
    grad_tiles(place, n_group, d, x, d_pre, own_o, near_o, far_o, tile)


def norm_back_kernel(
    place, d_second, keep, got, far, hat, factor, vec, d_first_o, d_attn_o, sums_o
):
    n = d_second.shape[0]
    d_normed = d_second[...] + keep[0:n] + got[0:n].astype(F32) + far[...].astype(F32)
    d_first = normalise_back(d_normed * vec[3:4], hat[...], factor[:, 0:1])
    d_first_o[...] = d_first
    d_attn = d_first.astype(BF)
    d_attn_o[...] = d_attn
    sums_o[...] = jnp.zeros_like(sums_o)
    sums_o[0:1] = column_sum(d_attn.astype(F32))
    sums_o[1:2] = column_sum(d_normed * hat[...])
    sums_o[2:3] = column_sum(d_normed)


def attention_back_kernel(
    n_group, d, f, n, place, d_attn, wout, joint, probs_in, p0, p1, p2, p3,
    sums1, sums2, d_hb,
    d_joint_o, own_o, near_o, far_o, token_s, tile, vec_s, small_s,
):
    t, z, y = place[0], place[1], place[2]
    depth = n_group // 2
    part = wout.shape[0]
    w = f // TEAM
    for b in range(TEAM):
        token_s[b * n : (b + 1) * n] = (p0, p1, p2, p3)[b][0:n]
    d_mixed = against(d_attn[...], wout[...]).astype(BF)
    scale = HD ** (-0.5)
    low = lax.broadcasted_iota(jnp.int32, (1, PAIR), 1) < HD
    zero = jnp.zeros((), BF)
    for b in range(TEAM):
        rows = slice(b * n, (b + 1) * n)
        for pair in range(part // PAIR):
            at = pair * PAIR
            query = joint[rows, at : at + PAIR]
            keys = joint[rows, part + at : part + at + PAIR]
            values = joint[rows, 2 * part + at : 2 * part + at + PAIR]
            d_mix = d_mixed[rows, at : at + PAIR]
            d_query, d_keys, d_values = [], [], []
            for h in range(2):
                low_probs = probs_in[(b * (part // PAIR) + pair) * 2 + h]
                probs = low_probs.astype(F32)
                sided = jnp.where(low, d_mix, zero) if h == 0 else jnp.where(low, zero, d_mix)
                d_probs = against(sided, values)
                d_scores = (
                    probs * (d_probs - jnp.sum(probs * d_probs, -1, keepdims=True))
                ).astype(BF)
                d_values.append(outer(low_probs, d_mix))
                d_query.append(times(d_scores, keys))
                d_keys.append(outer(d_scores, query))
            for i, (value, factor) in enumerate(
                ((d_query, scale), (d_keys, scale), (d_values, 1.0))
            ):
                d_joint_o[rows, i * part + at : i * part + at + PAIR] = (
                    jnp.where(low, value[0], value[1]) * factor
                ).astype(BF)
    vec_s[...] = jnp.zeros_like(vec_s)
    mine = pl.ds(pl.multiple_of(t * part, part), part)
    vec_s[0:1, mine] = column_sum(d_joint_o[:, 0:part].astype(F32))
    vec_s[1:2, mine] = column_sum(d_joint_o[:, 2 * part : 3 * part].astype(F32))
    vec_s[2:5, :] = sums1[0:3]
    vec_s[5:8, :] = sums2[0:3]
    small_s[...] = jnp.zeros_like(small_s)
    for g in range(n_group):
        small_s[g, 0:8, 0:d] = vec_s[:, g * d : (g + 1) * d]
        row = d_hb[:, g * w : (g + 1) * w]
        small_s[g, 8:9, 0:f] = jnp.concatenate(
            [jnp.where(t == i, row, jnp.zeros_like(row)) for i in range(TEAM)], 1
        )
    grad_tiles(place, n_group, d, token_s, d_joint_o, own_o, near_o, far_o, tile)
    half = depth // 2
    for k in range(depth):
        g = lax.bitwise_xor(z, k) * 2
        own_o[k, d : d + EXTRA, :] = small_s[g + y]
        sent_o = far_o if k >= half else near_o
        sent_o[k % half, d : d + EXTRA, :] = small_s[g + 1 - y].astype(BF)


def out_grad_kernel(d, place, mixed, a0, a1, a2, a3, out_own_o, out_other_o, attn_o, heads_s):
    n = a0.shape[0]
    y = place[2]
    for b, block in enumerate((a0, a1, a2, a3)):
        attn_o[b * n : (b + 1) * n] = block[...]
    heads_s[...] = outer(mixed[...], attn_o[...])
    for at in range(mixed.shape[1] // (2 * d)):
        out_own_o[at * d : (at + 1) * d] = heads_s[
            pl.ds(pl.multiple_of((at * 2 + y) * d, d), d), :
        ]
        out_other_o[at * d : (at + 1) * d] = heads_s[
            pl.ds(pl.multiple_of((at * 2 + 1 - y) * d, d), d), :
        ].astype(BF)


def token_back_kernel(n, d, place, d_joint, f0, f1, f2, f3, near_o, keep_o, first_s):
    assemble(place, (f0, f1, f2, f3), d, first_s)

    def step(at, carry):
        columns = pl.ds(pl.multiple_of(at * 256, 256), 256)
        to_team(against(d_joint[...], first_s[columns, :]), n, near_o, keep_o, columns)
        return carry

    lax.fori_loop(0, keep_o.shape[1] // 256, step, 0)


def add_far_kernel(place, own, got, sum_o):
    half = sum_o.shape[0]
    sum_o[...] = (own[half : 2 * half] + got[0:half].astype(F32)).astype(BF)


def add_near_kernel(place, own, got, far, keep_o, send_o):
    half = far.shape[0]
    total = own[0:half] + got[got.shape[0] - half :].astype(F32) + far[...].astype(F32)
    keep_o[...] = total[0 : half // 2]
    send_o[...] = total[half // 2 :].astype(BF)


def back_out_kernel(place, b0, b1, b2, b3, back_o):
    w = b0.shape[0]
    for i in range(TEAM):
        block = of_member(place[0], i, [b[...] for b in (b0, b1, b2, b3)])
        back_o[i * w : (i + 1) * w] = block.astype(F32)


def hidden_out_kernel(n_group, place, h0, h1, h2, h3, hidden_o):
    w = h0.shape[1] // n_group
    for i in range(TEAM):
        block = of_member(place[0], i, [h[...] for h in (h0, h1, h2, h3)]).astype(F32)
        for g in range(n_group):
            at = (g * TEAM + i) * w
            hidden_o[:, at : at + w] = block[:, g * w : (g + 1) * w]


def attention_out_kernel(f, place, j0, j1, j2, j3, out, joint_o, out_o, *small_o):
    t = place[0]
    d = out_o.shape[0]
    part = j0.shape[1] // 3
    width = part * TEAM
    total = jnp.zeros((EXTRA, 3 * part), F32)
    for i in range(TEAM):
        block = of_member(t, i, [j[...] for j in (j0, j1, j2, j3)]).astype(F32)
        for s in range(3):
            at = s * width + i * part
            joint_o[:, at : at + part] = block[0:d, s * part : (s + 1) * part]
        total = total + block[d : d + EXTRA]
    out_o[...] = out[...].astype(F32)
    for i in range(8):
        small_o[i][...] = total[i : i + 1, 0:d]
    small_o[8][...] = total[8:9, 0:f]


def shards(
    tokens,
    lengths,
    cotangent,
    attention_in,
    query_bias,
    value_bias,
    attention_out,
    out_bias,
    first_gain,
    first_shift,
    hidden_in,
    hidden_bias,
    hidden_out,
    output_bias,
    second_gain,
    second_shift,
):
    at = Places()
    n_group, depth, place = at.n_group, at.depth, at.place
    n, width = tokens.shape
    d = attention_in.shape[0]
    f = hidden_bias.shape[0]
    w = f // TEAM
    part = width // TEAM
    inner = w * n_group
    all_rows = TEAM * n

    vectors = (
        query_bias,
        value_bias,
        out_bias,
        first_gain,
        first_shift,
        output_bias,
        second_gain,
        second_shift,
    )
    small = jnp.concatenate(
        [
            jnp.pad(jnp.stack(vectors), ((0, 0), (0, 3 * part - d))),
            jnp.pad(hidden_bias[None], ((0, EXTRA - 9), (0, 3 * part - f))),
        ],
        0,
    )
    extra = jnp.pad(lengths.astype(BF), ((0, EXTRA - 1), (0, width - lengths.shape[1])))
    packed = jnp.concatenate([tokens, extra], 0)
    (first_near,) = call(
        prepare_first_kernel,
        [shape((1, d + EXTRA, 3 * part), BF)],
        place,
        attention_in,
        small,
    )
    def widen(blocks):
        for flip in list(at.steps_down(at.half // 2))[::-1]:
            blocks = (blocks, at.send_z(blocks, flip))
            if flip < at.half // 2:
                (blocks,) = relay(place, blocks)
        return blocks

    heads_mine, heads_first = [], []
    for i in range(at.heads_at):
        home = at.t * at.heads_at + i
        value = jnp.where(at.z == home, attention_out, jnp.zeros_like(attention_out))
        for flip in at.steps_down(at.half):
            value = value + at.send_heads(value, i, flip, False)
            if flip == at.half:
                heads_first.append(value)
        heads_mine.append(value)
    out_mine = jnp.concatenate(heads_mine, 0)
    out_other = at.send_y(out_mine)
    packed_far = at.send_team(packed, 2)
    packed = [packed, at.send_team(packed, 1), packed_far, at.send_team(packed_far, 1)]

    (first_near,) = relay(place, widen(first_near), after=heads_first)
    (rest_mine,) = call(
        partial(prepare_rest_kernel, n_group),
        [shape((d + w, width), BF)],
        place,
        hidden_in,
        hidden_out,
        after=[first_near],
    )
    rest_all = lax.all_gather(rest_mine, "group", axis=0)
    first_far = at.other_half(first_near)
    first_near_y = at.send_y(first_near)
    (first_sent,) = relay(place, (first_far,), after=[first_near_y, out_other, *packed])
    first_all = [first_near, first_far, first_near_y, at.send_y(first_sent)]

    joint, probs, mixed, near, keep, vec, hb, w_out = call(
        partial(attention_kernel, n_group, d, f, n),
        [
            shape((all_rows, 3 * part), BF),
            shape((TEAM * H // TEAM, n, n), BF),
            shape((all_rows, part), BF),
            shape((2 * n, width), BF),
            shape((2 * n, width), F32),
            shape((8, width), F32),
            shape((1, inner), F32),
            shape((part, width), BF),
        ],
        place,
        *packed,
        out_mine,
        out_other,
        *first_all,
        scratch=[
            pltpu.VMEM((width, 3 * part), BF),
            pltpu.VMEM((all_rows, width), BF),
            pltpu.VMEM((n_group, EXTRA, 3 * part), F32),
        ],
    )
    normed, normed_low, hat, factor = call(
        norm_kernel,
        [
            shape((n, width), F32),
            shape((n, width), BF),
            shape((n, width), F32),
            shape((n, 128), F32),
        ],
        place,
        tokens,
        *at.scatter_team(near, keep),
        vec,
    )

    pre, act, near, keep, normed4 = call(
        partial(feed_kernel, n_group, d),
        [
            shape((all_rows, inner), F32),
            shape((all_rows, inner), BF),
            shape((2 * n, width), BF),
            shape((2 * n, width), F32),
            shape((all_rows, width), BF),
        ],
        place,
        *at.gather_team(normed_low),
        hb,
        rest_all,
    )
    layer_out, d_second, d_out, sums2 = call(
        second_kernel,
        [
            shape((n, width), BF),
            shape((n, width), F32),
            shape((n, width), BF),
            shape((8, width), F32),
        ],
        place,
        normed,
        *at.scatter_team(near, keep),
        vec,
        cotangent,
        packed[0],
    )

    def add_near(own, came_y, came_z, after=()):
        half, *rest = came_z.shape
        return call(
            add_near_kernel,
            [shape((half // 2, *rest), F32), shape((half // 2, *rest), BF)],
            place,
            own,
            came_y,
            came_z,
            after=after,
        )

    def sum_group(keep, send):
        flip = at.half // 2
        while flip > 1:
            total = keep + at.send_z(send, flip).astype(F32)
            flip //= 2
            keep, send = total[:flip], total[flip:].astype(BF)
        return at.over_copies((keep + at.send_z(send, 1).astype(F32))[0].astype(BF))

    half = depth // 2
    def add_far(own, came, after=()):
        half, rest = own.shape[0] // 2, own.shape[1:]
        return call(add_far_kernel, [shape((half, *rest), BF)], place, own, came, after=after)[0]

    grad_back, d_out4 = call(
        back_grad_kernel,
        [shape((inner, width), BF), shape((all_rows, width), BF)],
        place,
        *at.gather_team(d_out),
        act,
    )
    g_back = at.over_copies(
        lax.psum_scatter(grad_back, "group", scatter_dimension=0, tiled=True)
    )
    d_pre, near, keep, d_hb = call(
        partial(feed_back_kernel, n_group, d, n),
        [
            shape((all_rows, inner), BF),
            shape((2 * n, width), BF),
            shape((2 * n, width), F32),
            shape((1, inner), F32),
        ],
        place,
        d_out4,
        rest_all,
        pre,
    )
    own_hidden, near_hidden, far_hidden = call(
        partial(hidden_grad_kernel, n_group, d),
        [shape((depth, d, inner), F32)] + [shape((half, d, inner), BF)] * 2,
        place,
        normed4,
        d_pre,
        scratch=[pltpu.VMEM((2 * d, inner), F32)],
    )
    d_first, d_attn, sums1 = call(
        norm_back_kernel,
        [shape((n, width), F32), shape((n, width), BF), shape((8, width), F32)],
        place,
        d_second,
        *at.scatter_team(near, keep),
        hat,
        factor,
        vec,
        after=[far_hidden],
    )
    heads_rows = at.heads_at * d
    sent_hidden = add_far(own_hidden, at.send_y(far_hidden))
    came_hidden = at.other_half(sent_hidden)
    out_own, out_sent, d_attn4 = call(
        partial(out_grad_kernel, d),
        [
            shape((heads_rows, width), F32),
            shape((heads_rows, width), BF),
            shape((all_rows, width), BF),
        ],
        place,
        mixed,
        *at.gather_team(d_attn),
        after=[sent_hidden],
        scratch=[pltpu.VMEM((part, width), F32)],
    )
    d_joint, own_joint, near_joint, far_joint = call(
        partial(attention_back_kernel, n_group, d, f, n),
        [
            shape((all_rows, 3 * part), BF),
            shape((depth, d + EXTRA, 3 * part), F32),
            shape((half, d + EXTRA, 3 * part), BF),
            shape((half, d + EXTRA, 3 * part), BF),
        ],
        place,
        d_attn4,
        w_out,
        joint,
        probs,
        *packed,
        sums1,
        sums2,
        d_hb,
        scratch=[
            pltpu.VMEM((all_rows, width), BF),
            pltpu.VMEM((2 * d, 3 * part), F32),
            pltpu.VMEM((8, width), F32),
            pltpu.VMEM((n_group, EXTRA, 3 * part), F32),
        ],
    )
    out_sum = out_own + at.send_y(out_sent).astype(F32)
    sent_joint = add_far(own_joint, at.send_y(far_joint), [came_hidden, out_sum])
    blocks = []
    for i in range(at.heads_at):
        block = out_sum[i * d : (i + 1) * d]
        for flip in list(at.steps_down(at.half))[:0:-1]:
            block = block + at.send_heads(block.astype(BF), i, flip, True).astype(F32)
        blocks.append(block)
    (sent_y,) = relay(place, (near_hidden,), after=[sent_joint])
    came_joint = at.other_half(sent_joint)
    hidden_parts = add_near(own_hidden, at.send_y(sent_y), came_hidden, blocks)
    g_out = jnp.zeros((d, width), F32)
    for i, block in enumerate(blocks):
        block = block + at.send_heads(block.astype(BF), i, at.half, True).astype(F32)
        here = at.z == at.t * at.heads_at + i
        g_out = g_out + jnp.where(here, block, jnp.zeros_like(block))
    g_hidden = sum_group(*hidden_parts)
    back_far = at.send_team(g_back, 2)
    joint_parts = add_near(own_joint, at.send_y(near_joint), came_joint, [g_out])
    g_joint = sum_group(*joint_parts)
    near, keep = call(
        partial(token_back_kernel, n, d),
        [shape((2 * n, width), BF), shape((2 * n, width), F32)],
        place,
        d_joint,
        *first_all,
        after=[],
        scratch=[pltpu.VMEM((width, 3 * part), BF)],
    )
    kept, got, far = at.scatter_team(near, keep)
    g_out = at.over_copies(g_out.astype(BF))
    grad_tokens = d_first + kept[:n] + got[:n].astype(F32) + far.astype(F32)

    (g_hidden_out,) = call(
        back_out_kernel, [shape((f, width), F32)], place, g_back, at.send_team(g_back, 1), back_far, at.send_team(back_far, 1)
    )
    (g_hidden_in,) = call(
        partial(hidden_out_kernel, n_group),
        [shape((d, TEAM * inner), F32)],
        place,
        *at.gather_team(g_hidden),
    )
    joint_far = at.send_team(g_joint, 2)
    (joint_sent,) = relay(place, (joint_far,), after=[g_hidden_out, g_hidden_in, grad_tokens])
    g_attention_in, g_attention_out, *g_small = call(
        partial(attention_out_kernel, f),
        [shape((d, 3 * width), F32), shape((d, width), F32)]
        + [shape((1, d), F32)] * 8
        + [shape((1, f), F32)],
        place,
        g_joint,
        at.send_team(g_joint, 1),
        joint_far,
        at.send_team(joint_sent, 1),
        at.spread_heads(g_out),
    )
    g_qb, g_vb, g_ob, g_g1, g_s1, g_outb, g_g2, g_s2, g_hb = (v.reshape(-1) for v in g_small)
    return (
        layer_out,
        grad_tokens,
        g_attention_in,
        g_qb,
        g_vb,
        g_attention_out,
        g_ob,
        g_g1,
        g_s1,
        g_hidden_in,
        g_hb,
        g_hidden_out,
        g_outb,
        g_g2,
        g_s2,
    )


def solution(mesh):
    rows = P(("replica", "group"), None)
    matrix = P("group", None)
    vector = P("group")
    params = (
        matrix,
        vector,
        vector,
        matrix,
        vector,
        vector,
        vector,
        matrix,
        vector,
        matrix,
        vector,
        vector,
        vector,
    )
    return jax.shard_map(
        shards,
        mesh=mesh,
        in_specs=(rows, rows, rows) + params,
        out_specs=(rows, rows) + params,
        check_vma=False,
    )
```

```python
from functools import partial

import jax
import jax.numpy as jnp
from jax import lax
from jax.experimental import pallas as pl
from jax.experimental.pallas import tpu as pltpu
from jax.sharding import PartitionSpec as P

H = 16
HD = 64
SEQS = 4
TEAM = 4
EXTRA = 16
PAIR = 2 * HD
BF = jnp.bfloat16
F32 = jnp.float32


class Places:
    def __init__(self):
        self.n_group = lax.axis_size("group")
        self.n_replica = lax.axis_size("replica")
        self.depth = self.n_group // 2
        self.half = self.depth // 2
        self.heads_at = self.depth // TEAM
        place = lax.axis_index("group")
        self.z = place // 2
        self.t = lax.axis_index("replica") % TEAM
        self.place = jnp.stack([self.t, self.z, place % 2]).astype(jnp.int32)

    def send_z(self, value, flip):
        return lax.ppermute(
            value, "group", [(g, g ^ (2 * flip)) for g in range(self.n_group)]
        )

    def send_y(self, value):
        return lax.ppermute(value, "group", [(g, g ^ 1) for g in range(self.n_group)])

    def send_team(self, value, flip):
        return lax.ppermute(value, "replica", [(r, r ^ flip) for r in range(self.n_replica)])

    def send_heads(self, value, at, flip, back):
        pairs = []
        for r in range(self.n_replica):
            home = r % TEAM * self.heads_at + at
            for z in range(self.depth):
                if (z ^ home) & (2 * flip - 1) == 0:
                    for y in range(2):
                        near = r * self.n_group + z * 2 + y
                        pairs.append((near ^ (2 * flip), near) if back else (near, near ^ (2 * flip)))
        return lax.ppermute(value, ("replica", "group"), pairs)

    def steps_down(self, top):
        while top >= 1:
            yield top
            top //= 2

    def other_half(self, blocks):
        return self.send_z(blocks, self.half)

    def spread_heads(self, block):
        for flip in (2, 1):
            pairs = []
            for r in range(self.n_replica):
                for g in range(self.n_group):
                    apart = r % TEAM ^ g // 2 // self.heads_at
                    if apart == 0 or (flip == 1 and apart == 2):
                        pairs.append((r * self.n_group + g, (r ^ flip) * self.n_group + g))
            block = block + lax.ppermute(block, ("replica", "group"), pairs)
        return block

    def gather_team(self, block):
        far = self.send_team(block, 2)
        near = self.send_team(block, 1)
        return [block, near, far, self.send_team(far, 1)]

    def scatter_near(self, near, keep):
        n = near.shape[0] // 2
        got = self.send_team(near, 1)
        return got, (keep[n:] + got[n:].astype(F32)).astype(BF)

    def scatter_team(self, near, keep):
        got, sent = self.scatter_near(near, keep)
        return keep, got, self.send_team(sent, 2)

    def over_copies(self, value):
        teams = self.n_replica // TEAM
        if teams == 1:
            return value
        return lax.psum(
            value,
            "replica",
            axis_index_groups=[
                [team * TEAM + t for team in range(teams)] for t in range(TEAM)
            ],
        )


def call(kernel, outs, place, *args, scratch=(), after=(), copied=()):
    specs = [pl.BlockSpec(memory_space=pltpu.VMEM)] * len(args)
    specs += [pl.BlockSpec(memory_space=pltpu.HBM)] * len(copied)
    args = (*args, *copied)
    body = kernel
    if after:
        read = len(args)
        specs += [pl.BlockSpec(memory_space=pl.ANY)] * len(after)
        args = (*args, *after)

        def body(place, *refs):
            kernel(place, *refs[:read], *refs[read + len(after) :])

    return pl.pallas_call(
        body,
        name=getattr(kernel, "func", kernel).__name__,
        out_shape=outs,
        in_specs=[pl.BlockSpec(memory_space=pltpu.SMEM)] + specs,
        out_specs=[pl.BlockSpec(memory_space=pltpu.VMEM)] * len(outs),
        scratch_shapes=list(scratch),
        compiler_params=pltpu.CompilerParams(vmem_limit_bytes=16 << 20),
        cost_estimate=pl.CostEstimate(flops=0, bytes_accessed=0, transcendentals=0),
    )(place, *args)


def shape(dims, dtype):
    return jax.ShapeDtypeStruct(tuple(dims), dtype)


def times(left, right):
    return jnp.dot(left, right, preferred_element_type=F32)


def against(left, weight):
    return lax.dot_general(left, weight, (((1,), (1,)), ((), ())), preferred_element_type=F32)


def outer(left, right):
    return lax.dot_general(left, right, (((0,), (0,)), ((), ())), preferred_element_type=F32)


def chosen(index, cases):
    result = cases[-1]
    for at in range(len(cases) - 2, -1, -1):
        result = jnp.where(index == at, cases[at], result)
    return result


def of_member(t, member, blocks):
    return chosen(t, [blocks[i ^ member] for i in range(TEAM)])


def column_sum(value):
    return jnp.sum(value, 0, keepdims=True)


def ends_of(block, n):
    row = block[n : n + EXTRA, 0:128].astype(F32)[0:1]
    lane = lax.broadcasted_iota(jnp.int32, (1, 128), 1)
    return [
        jnp.sum(jnp.where(lane <= s, row, 0.0), axis=1, keepdims=True) for s in range(SEQS)
    ]


def segments(ends, dims, axis):
    place = lax.broadcasted_iota(jnp.int32, dims, axis).astype(F32)
    total = jnp.zeros(dims, F32)
    for end in ends:
        total = total + jnp.where(place >= end, 1.0, 0.0)
    return total


def normalise(value):
    centre = jnp.mean(value, -1, keepdims=True)
    offset = value - centre
    spread = jnp.mean(offset * offset, -1, keepdims=True)
    factor = lax.rsqrt(spread + 1e-06)
    return offset * factor, factor


def normalise_back(d_hat, hat, factor):
    return factor * (
        d_hat
        - jnp.mean(d_hat, -1, keepdims=True)
        - hat * jnp.mean(d_hat * hat, -1, keepdims=True)
    )


def grad_tiles(place, n_group, width, left, right, own, near, far, tile):
    depth = n_group // 2
    half = depth // 2
    z, y = place[1], place[2]

    def step(at, carry):
        tile[...] = outer(left[:, pl.ds(pl.multiple_of(at * 2 * width, 2 * width), 2 * width)], right[...])
        k = lax.bitwise_xor(z, at)
        own[k, 0:width, :] = tile[pl.ds(pl.multiple_of(y * width, width), width), :]
        sent = tile[pl.ds(pl.multiple_of((1 - y) * width, width), width), :].astype(BF)

        @pl.when(k < half)
        def _():
            near[k, 0:width, :] = sent

        @pl.when(k >= half)
        def _():
            far[k - half, 0:width, :] = sent

        return carry

    lax.fori_loop(0, depth, step, 0)


def to_team(value, n, near, keep, columns):
    keep[0:n, columns] = value[0:n]
    near[0:n, columns] = value[n : 2 * n].astype(BF)
    keep[n : 2 * n, columns] = value[2 * n : 3 * n]
    near[n : 2 * n, columns] = value[3 * n : 4 * n].astype(BF)


def at_group(place, n_group, i):
    depth = n_group // 2
    dy, k = divmod(i, depth)
    y = place[2]
    return lax.rem(place[1] - k + depth, depth) * 2 + (y if dy == 0 else 1 - y)


def relay_kernel(counts, place, *refs):
    outs = refs[sum(counts) :]
    for out, count in zip(outs, counts):
        parts, refs = refs[:count], refs[count:]
        at = 0
        for part in parts:
            out[at : at + part.shape[0]] = part[...]
            at += part.shape[0]


def relay(place, *tasks, after=()):
    outs = [
        shape((sum(part.shape[0] for part in task), *task[0].shape[1:]), task[0].dtype)
        for task in tasks
    ]
    flat = [part for task in tasks for part in task]
    return call(
        partial(relay_kernel, [len(task) for task in tasks]), outs, place, *flat, after=after
    )


def group_blocks(place, quarters):
    half = quarters[0].shape[0]
    for q, quarter in enumerate(quarters):
        for i in range(half):
            dz, dy = q % 2 * half + i, q // 2
            z = lax.bitwise_xor(place[1], dz)
            yield z * 2 + lax.bitwise_xor(place[2], dy), quarter.at[i]


def assemble(place, quarters, rows, whole):
    for g, block in group_blocks(place, quarters):
        whole[pl.ds(pl.multiple_of(g * rows, rows), rows), :] = block[0:rows]


def prepare_first_kernel(place, att, small, first_o):
    t = place[0]
    d, joint = att.shape
    width = joint // 3
    part = width // TEAM
    for i in range(3):
        first_o[0, 0:d, i * part : (i + 1) * part] = chosen(
            t,
            [
                att[:, i * width + s * part : i * width + (s + 1) * part]
                for s in range(TEAM)
            ],
        )
    first_o[0, d : d + EXTRA, :] = small[...]


def prepare_rest_kernel(n_group, place, hid, back, rest_o):
    t = place[0]
    d = hid.shape[0]
    f = hid.shape[1] // n_group
    w = f // TEAM
    for g in range(n_group):
        rest_o[0:d, g * w : (g + 1) * w] = chosen(
            t, [hid[:, g * f + s * w : g * f + (s + 1) * w] for s in range(TEAM)]
        )
    rest_o[d : d + w, :] = back[pl.ds(pl.multiple_of(t * w, w), w), :]


def attention_kernel(
    n_group, d, f, n, place, p0, p1, p2, p3, own_out, other_out, *refs
):
    first, refs = refs[:4], refs[4:]
    (
        joint_o, probs_o, mixed_o, near_o, keep_o, vec_o, hb_o, wout_o, first_s, token_s, small_s,
    ) = refs
    blocks = (p0, p1, p2, p3)
    t, y = place[0], place[2]
    part = wout_o.shape[0]
    width = wout_o.shape[1]
    w = f // TEAM
    assemble(place, first, d, first_s)
    for g, block in group_blocks(place, first):
        small_s[g] = block[d : d + EXTRA, :].astype(F32)
    small = [small_s[g] for g in range(n_group)]
    vec_o[...] = jnp.concatenate([s[0:8, 0:d] for s in small], 1)
    hb_o[...] = jnp.concatenate(
        [chosen(t, [s[8:9, i * w : (i + 1) * w] for i in range(TEAM)]) for s in small], 1
    )
    for at in range(part // (2 * d)):
        wout_o[pl.ds(pl.multiple_of((at * 2 + y) * d, d), d), :] = own_out[
            at * d : (at + 1) * d
        ]
        wout_o[pl.ds(pl.multiple_of((at * 2 + 1 - y) * d, d), d), :] = other_out[
            at * d : (at + 1) * d
        ]
    for b in range(TEAM):
        token_s[b * n : (b + 1) * n] = blocks[b][0:n]
    mine = pl.ds(pl.multiple_of(t * part, part), part)
    for i in range(3):
        value = times(token_s[...], first_s[:, i * part : (i + 1) * part])
        if i == 0:
            value = value + vec_o[0:1, mine]
        if i == 2:
            value = value + vec_o[1:2, mine]
        joint_o[:, i * part : (i + 1) * part] = value.astype(BF)
    scale = HD ** (-0.5)
    low = lax.broadcasted_iota(jnp.int32, (1, PAIR), 1) < HD
    zero = jnp.zeros((), BF)
    for b in range(TEAM):
        rows = slice(b * n, (b + 1) * n)
        ends = ends_of(blocks[b], n)
        same = segments(ends, (n, 1), 0) == segments(ends, (1, n), 1)
        for pair in range(part // PAIR):
            at = pair * PAIR
            query = joint_o[rows, at : at + PAIR]
            keys = joint_o[rows, part + at : part + at + PAIR]
            values = joint_o[rows, 2 * part + at : 2 * part + at + PAIR]
            mixed = []
            for h in range(2):
                sided = jnp.where(low, query, zero) if h == 0 else jnp.where(low, zero, query)
                scores = jnp.where(same, against(sided, keys) * scale, -1000000000.0)
                expo = jnp.exp(scores - jnp.max(scores, -1, keepdims=True))
                probs = expo / jnp.sum(expo, -1, keepdims=True)
                probs = probs.astype(BF)
                probs_o[(b * (part // PAIR) + pair) * 2 + h] = probs
                mixed.append(times(probs, values))
            mixed_o[rows, at : at + PAIR] = jnp.where(low, mixed[0], mixed[1]).astype(BF)
    for at in range(0, width, part):
        columns = slice(at, at + part)
        to_team(times(mixed_o[...], wout_o[:, columns]), n, near_o, keep_o, columns)


def norm_kernel(place, tokens, keep, got, far, vec, normed_o, low_o, hat_o, factor_o):
    n = tokens.shape[0]
    attn = keep[0:n] + got[0:n].astype(F32) + far[...].astype(F32) + vec[2:3]
    hat, factor = normalise(tokens[...].astype(F32) + attn)
    normed = hat * vec[3:4] + vec[4:5]
    normed_o[...] = normed
    low_o[...] = normed.astype(BF)
    hat_o[...] = hat
    factor_o[...] = jnp.broadcast_to(factor, factor_o.shape)


def gelu_parts(pre):
    bell = 0.5 * (1.0 + lax.erf(pre * (2.0**-0.5)))
    return bell, jnp.exp(-0.5 * pre * pre) * (2.0 * 3.141592653589793) ** -0.5


def feed_kernel(
    n_group, d, place, x0, x1, x2, x3, hb, rest, pre_o, act_o, near_o, keep_o, x_o, rest_s, sems
):
    n = x0.shape[0]
    w = rest.shape[1] - d
    tiles = rest.shape[2] // 256

    def weights(at, rows, first):
        part = (slice(None), rows, pl.ds(at * 256, 256))
        return pltpu.make_async_copy(rest.at[part], rest_s.at[part], sems.at[first + at])

    entering = [weights(at, pl.ds(0, d), 0) for at in range(tiles)]
    leaving = [weights(at, pl.ds(d, w), tiles) for at in range(tiles)]
    for load in entering + leaving:
        load.start()
    for b, block in enumerate((x0, x1, x2, x3)):
        x_o[b * n : (b + 1) * n] = block[...]
    for at in range(tiles):
        columns = slice(at * 256, (at + 1) * 256)
        entering[at].wait()
        weight = rest_s[:, 0:d, columns].reshape(n_group * d, 256)
        pre = times(x_o[...], weight) + hb[:, columns]
        pre_o[:, columns] = pre
        act_o[:, columns] = (pre * gelu_parts(pre)[0]).astype(BF)
    for at in range(tiles):
        columns = slice(at * 256, (at + 1) * 256)
        leaving[at].wait()
        weight = rest_s[:, d : d + w, columns].reshape(n_group * w, 256)
        to_team(times(act_o[...], weight), n, near_o, keep_o, columns)


def second_kernel(
    place, normed, keep, got, far, vec, cotangent, packed, layer_o, d_second_o, d_out_o, sums_o
):
    n = normed.shape[0]
    out = keep[0:n] + got[0:n].astype(F32) + far[...].astype(F32) + vec[5:6]
    hat, factor = normalise(normed[...] + out)
    live = jnp.where(segments(ends_of(packed, n), (n, 1), 0) < SEQS, 1.0, 0.0)
    layer_o[...] = ((hat * vec[6:7] + vec[7:8]) * live).astype(BF)
    d_final = cotangent[...].astype(F32) * live
    d_second = normalise_back(d_final * vec[6:7], hat, factor)
    d_second_o[...] = d_second
    d_out = d_second.astype(BF)
    d_out_o[...] = d_out
    sums_o[...] = jnp.zeros_like(sums_o)
    sums_o[0:1] = column_sum(d_out.astype(F32))
    sums_o[1:2] = column_sum(d_final * hat)
    sums_o[2:3] = column_sum(d_final)


def back_grad_kernel(place, d0, d1, d2, d3, act, grad_o, d_out_o):
    n = d0.shape[0]
    for b, block in enumerate((d0, d1, d2, d3)):
        d_out_o[b * n : (b + 1) * n] = block[...]

    def step(at, carry):
        rows = pl.ds(pl.multiple_of(at * 256, 256), 256)
        grad_o[rows, :] = outer(act[:, rows], d_out_o[...]).astype(BF)
        return carry

    lax.fori_loop(0, grad_o.shape[0] // 256, step, 0)


def feed_back_kernel(
    n_group, d, n, place, d_out, pre, rest, d_pre_o, near_o, keep_o, hb_o, rest_s, sems
):
    w = rest.shape[1] - d
    tiles = rest.shape[2] // 256

    def weights(at, rows, count, first):
        part = (pl.ds(at * (256 // count), 256 // count), pl.ds(rows, count))
        return pltpu.make_async_copy(rest.at[part], rest_s.at[part], sems.at[first + at])

    leaving = [weights(at, d, w, 0) for at in range(tiles)]
    entering = [weights(at, 0, d, tiles) for at in range(tiles)]
    for load in leaving + entering:
        load.start()
    for at in range(tiles):
        columns = slice(at * 256, (at + 1) * 256)
        leaving[at].wait()
        per = 256 // w
        weight = rest_s[at * per : (at + 1) * per, d : d + w, :].reshape(256, rest.shape[2])
        d_act = against(d_out[...], weight)
        value = pre[:, columns]
        bell, slope = gelu_parts(value)
        d_pre = (d_act * (bell + value * slope)).astype(BF)
        d_pre_o[:, columns] = d_pre
        hb_o[:, columns] = column_sum(d_pre.astype(F32))
    for at in range(tiles):
        columns = slice(at * 256, (at + 1) * 256)
        entering[at].wait()
        per = 256 // d
        weight = rest_s[at * per : (at + 1) * per, 0:d, :].reshape(256, rest.shape[2])
        to_team(against(d_pre_o[...], weight), n, near_o, keep_o, columns)


def hidden_grad_kernel(n_group, d, place, x, d_pre, own_o, near_o, far_o, tile):
    grad_tiles(place, n_group, d, x, d_pre, own_o, near_o, far_o, tile)


def norm_back_kernel(
    place, d_second, keep, got, far, hat, factor, vec, d_first_o, d_attn_o, sums_o
):
    n = d_second.shape[0]
    d_normed = d_second[...] + keep[0:n] + got[0:n].astype(F32) + far[...].astype(F32)
    d_first = normalise_back(d_normed * vec[3:4], hat[...], factor[:, 0:1])
    d_first_o[...] = d_first
    d_attn = d_first.astype(BF)
    d_attn_o[...] = d_attn
    sums_o[...] = jnp.zeros_like(sums_o)
    sums_o[0:1] = column_sum(d_attn.astype(F32))
    sums_o[1:2] = column_sum(d_normed * hat[...])
    sums_o[2:3] = column_sum(d_normed)


def attention_back_kernel(
    n_group, d, f, n, place, d_attn, wout, joint, probs_in, p0, p1, p2, p3,
    sums1, sums2, d_hb,
    d_joint_o, own_o, near_o, far_o, token_s, tile, vec_s, small_s,
):
    t, z, y = place[0], place[1], place[2]
    depth = n_group // 2
    part = wout.shape[0]
    w = f // TEAM
    for b in range(TEAM):
        token_s[b * n : (b + 1) * n] = (p0, p1, p2, p3)[b][0:n]
    d_mixed = against(d_attn[...], wout[...]).astype(BF)
    scale = HD ** (-0.5)
    low = lax.broadcasted_iota(jnp.int32, (1, PAIR), 1) < HD
    zero = jnp.zeros((), BF)
    for b in range(TEAM):
        rows = slice(b * n, (b + 1) * n)
        for pair in range(part // PAIR):
            at = pair * PAIR
            query = joint[rows, at : at + PAIR]
            keys = joint[rows, part + at : part + at + PAIR]
            values = joint[rows, 2 * part + at : 2 * part + at + PAIR]
            d_mix = d_mixed[rows, at : at + PAIR]
            d_query, d_keys, d_values = [], [], []
            for h in range(2):
                low_probs = probs_in[(b * (part // PAIR) + pair) * 2 + h]
                probs = low_probs.astype(F32)
                sided = jnp.where(low, d_mix, zero) if h == 0 else jnp.where(low, zero, d_mix)
                d_probs = against(sided, values)
                d_scores = (
                    probs * (d_probs - jnp.sum(probs * d_probs, -1, keepdims=True))
                ).astype(BF)
                d_values.append(outer(low_probs, d_mix))
                d_query.append(times(d_scores, keys))
                d_keys.append(outer(d_scores, query))
            for i, (value, factor) in enumerate(
                ((d_query, scale), (d_keys, scale), (d_values, 1.0))
            ):
                d_joint_o[rows, i * part + at : i * part + at + PAIR] = (
                    jnp.where(low, value[0], value[1]) * factor
                ).astype(BF)
    vec_s[...] = jnp.zeros_like(vec_s)
    mine = pl.ds(pl.multiple_of(t * part, part), part)
    vec_s[0:1, mine] = column_sum(d_joint_o[:, 0:part].astype(F32))
    vec_s[1:2, mine] = column_sum(d_joint_o[:, 2 * part : 3 * part].astype(F32))
    vec_s[2:5, :] = sums1[0:3]
    vec_s[5:8, :] = sums2[0:3]
    small_s[...] = jnp.zeros_like(small_s)
    for g in range(n_group):
        small_s[g, 0:8, 0:d] = vec_s[:, g * d : (g + 1) * d]
        row = d_hb[:, g * w : (g + 1) * w]
        small_s[g, 8:9, 0:f] = jnp.concatenate(
            [jnp.where(t == i, row, jnp.zeros_like(row)) for i in range(TEAM)], 1
        )
    grad_tiles(place, n_group, d, token_s, d_joint_o, own_o, near_o, far_o, tile)
    half = depth // 2
    for k in range(depth):
        g = lax.bitwise_xor(z, k) * 2
        own_o[k, d : d + EXTRA, :] = small_s[g + y]
        sent_o = far_o if k >= half else near_o
        sent_o[k % half, d : d + EXTRA, :] = small_s[g + 1 - y].astype(BF)


def out_grad_kernel(d, place, mixed, a0, a1, a2, a3, out_own_o, out_other_o, attn_o, heads_s):
    n = a0.shape[0]
    y = place[2]
    for b, block in enumerate((a0, a1, a2, a3)):
        attn_o[b * n : (b + 1) * n] = block[...]
    heads_s[...] = outer(mixed[...], attn_o[...])
    for at in range(mixed.shape[1] // (2 * d)):
        out_own_o[at * d : (at + 1) * d] = heads_s[
            pl.ds(pl.multiple_of((at * 2 + y) * d, d), d), :
        ]
        out_other_o[at * d : (at + 1) * d] = heads_s[
            pl.ds(pl.multiple_of((at * 2 + 1 - y) * d, d), d), :
        ].astype(BF)


def token_back_kernel(n, d, place, d_joint, f0, f1, f2, f3, near_o, keep_o, first_s):
    assemble(place, (f0, f1, f2, f3), d, first_s)

    def step(at, carry):
        columns = pl.ds(pl.multiple_of(at * 256, 256), 256)
        to_team(against(d_joint[...], first_s[columns, :]), n, near_o, keep_o, columns)
        return carry

    lax.fori_loop(0, keep_o.shape[1] // 256, step, 0)


def add_far_kernel(place, own, got, sum_o):
    half = sum_o.shape[0]
    sum_o[...] = (own[half : 2 * half] + got[0:half].astype(F32)).astype(BF)


def add_near_kernel(place, own, got, far, keep_o, send_o):
    half = far.shape[0]
    total = own[0:half] + got[got.shape[0] - half :].astype(F32) + far[...].astype(F32)
    keep_o[...] = total[0 : half // 2]
    send_o[...] = total[half // 2 :].astype(BF)


def back_out_kernel(place, b0, b1, b2, b3, back_o):
    w = b0.shape[0]
    for i in range(TEAM):
        block = of_member(place[0], i, [b[...] for b in (b0, b1, b2, b3)])
        back_o[i * w : (i + 1) * w] = block.astype(F32)


def hidden_out_kernel(n_group, place, h0, h1, h2, h3, hidden_o):
    w = h0.shape[1] // n_group
    for i in range(TEAM):
        block = of_member(place[0], i, [h[...] for h in (h0, h1, h2, h3)]).astype(F32)
        for g in range(n_group):
            at = (g * TEAM + i) * w
            hidden_o[:, at : at + w] = block[:, g * w : (g + 1) * w]


def attention_out_kernel(f, place, j0, j1, j2, j3, out, joint_o, out_o, *small_o):
    t = place[0]
    d = out_o.shape[0]
    part = j0.shape[1] // 3
    width = part * TEAM
    total = jnp.zeros((EXTRA, 3 * part), F32)
    for i in range(TEAM):
        block = of_member(t, i, [j[...] for j in (j0, j1, j2, j3)]).astype(F32)
        for s in range(3):
            at = s * width + i * part
            joint_o[:, at : at + part] = block[0:d, s * part : (s + 1) * part]
        total = total + block[d : d + EXTRA]
    out_o[...] = out[...].astype(F32)
    for i in range(8):
        small_o[i][...] = total[i : i + 1, 0:d]
    small_o[8][...] = total[8:9, 0:f]


def shards(
    tokens,
    lengths,
    cotangent,
    attention_in,
    query_bias,
    value_bias,
    attention_out,
    out_bias,
    first_gain,
    first_shift,
    hidden_in,
    hidden_bias,
    hidden_out,
    output_bias,
    second_gain,
    second_shift,
):
    at = Places()
    n_group, depth, place = at.n_group, at.depth, at.place
    n, width = tokens.shape
    d = attention_in.shape[0]
    f = hidden_bias.shape[0]
    w = f // TEAM
    part = width // TEAM
    inner = w * n_group
    all_rows = TEAM * n

    vectors = (
        query_bias,
        value_bias,
        out_bias,
        first_gain,
        first_shift,
        output_bias,
        second_gain,
        second_shift,
    )
    small = jnp.concatenate(
        [
            jnp.pad(jnp.stack(vectors), ((0, 0), (0, 3 * part - d))),
            jnp.pad(hidden_bias[None], ((0, EXTRA - 9), (0, 3 * part - f))),
        ],
        0,
    )
    extra = jnp.pad(lengths.astype(BF), ((0, EXTRA - 1), (0, width - lengths.shape[1])))
    packed = jnp.concatenate([tokens, extra], 0)
    (first_near,) = call(
        prepare_first_kernel,
        [shape((1, d + EXTRA, 3 * part), BF)],
        place,
        attention_in,
        small,
    )
    def widen(blocks):
        for flip in list(at.steps_down(at.half // 2))[::-1]:
            blocks = (blocks, at.send_z(blocks, flip))
            if flip < at.half // 2:
                (blocks,) = relay(place, blocks)
        return blocks

    heads_mine, heads_first = [], []
    for i in range(at.heads_at):
        home = at.t * at.heads_at + i
        value = jnp.where(at.z == home, attention_out, jnp.zeros_like(attention_out))
        for flip in at.steps_down(at.half):
            value = value + at.send_heads(value, i, flip, False)
            if flip == at.half:
                heads_first.append(value)
        heads_mine.append(value)
    out_mine = jnp.concatenate(heads_mine, 0)
    out_other = at.send_y(out_mine)
    packed_far = at.send_team(packed, 2)
    packed = [packed, at.send_team(packed, 1), packed_far, at.send_team(packed_far, 1)]

    (first_near,) = relay(place, widen(first_near), after=heads_first)
    (rest_mine,) = call(
        partial(prepare_rest_kernel, n_group),
        [shape((d + w, width), BF)],
        place,
        hidden_in,
        hidden_out,
        after=[first_near],
    )
    rest_all = lax.all_gather(rest_mine, "group", axis=0)
    first_far = at.other_half(first_near)
    first_near_y = at.send_y(first_near)
    (first_sent,) = relay(place, (first_far,), after=[first_near_y, out_other, *packed])
    first_all = [first_near, first_far, first_near_y, at.send_y(first_sent)]

    joint, probs, mixed, near, keep, vec, hb, w_out = call(
        partial(attention_kernel, n_group, d, f, n),
        [
            shape((all_rows, 3 * part), BF),
            shape((TEAM * H // TEAM, n, n), BF),
            shape((all_rows, part), BF),
            shape((2 * n, width), BF),
            shape((2 * n, width), F32),
            shape((8, width), F32),
            shape((1, inner), F32),
            shape((part, width), BF),
        ],
        place,
        *packed,
        out_mine,
        out_other,
        *first_all,
        scratch=[
            pltpu.VMEM((width, 3 * part), BF),
            pltpu.VMEM((all_rows, width), BF),
            pltpu.VMEM((n_group, EXTRA, 3 * part), F32),
        ],
    )
    normed, normed_low, hat, factor = call(
        norm_kernel,
        [
            shape((n, width), F32),
            shape((n, width), BF),
            shape((n, width), F32),
            shape((n, 128), F32),
        ],
        place,
        tokens,
        *at.scatter_team(near, keep),
        vec,
    )

    pre, act, near, keep, normed4 = call(
        partial(feed_kernel, n_group, d),
        [
            shape((all_rows, inner), F32),
            shape((all_rows, inner), BF),
            shape((2 * n, width), BF),
            shape((2 * n, width), F32),
            shape((all_rows, width), BF),
        ],
        place,
        *at.gather_team(normed_low),
        hb,
        copied=[rest_all],
        scratch=[
            pltpu.VMEM((n_group, d + w, width), BF),
            pltpu.SemaphoreType.DMA((2 * (inner // 256),)),
        ],
    )
    layer_out, d_second, d_out, sums2 = call(
        second_kernel,
        [
            shape((n, width), BF),
            shape((n, width), F32),
            shape((n, width), BF),
            shape((8, width), F32),
        ],
        place,
        normed,
        *at.scatter_team(near, keep),
        vec,
        cotangent,
        packed[0],
    )

    def add_near(own, came_y, came_z, after=()):
        half, *rest = came_z.shape
        return call(
            add_near_kernel,
            [shape((half // 2, *rest), F32), shape((half // 2, *rest), BF)],
            place,
            own,
            came_y,
            came_z,
            after=after,
        )

    def sum_group(keep, send):
        flip = at.half // 2
        while flip > 1:
            total = keep + at.send_z(send, flip).astype(F32)
            flip //= 2
            keep, send = total[:flip], total[flip:].astype(BF)
        return at.over_copies((keep + at.send_z(send, 1).astype(F32))[0].astype(BF))

    half = depth // 2
    def add_far(own, came, after=()):
        half, rest = own.shape[0] // 2, own.shape[1:]
        return call(add_far_kernel, [shape((half, *rest), BF)], place, own, came, after=after)[0]

    grad_back, d_out4 = call(
        back_grad_kernel,
        [shape((inner, width), BF), shape((all_rows, width), BF)],
        place,
        *at.gather_team(d_out),
        act,
    )
    g_back = at.over_copies(
        lax.psum_scatter(grad_back, "group", scatter_dimension=0, tiled=True)
    )
    d_pre, near, keep, d_hb = call(
        partial(feed_back_kernel, n_group, d, n),
        [
            shape((all_rows, inner), BF),
            shape((2 * n, width), BF),
            shape((2 * n, width), F32),
            shape((1, inner), F32),
        ],
        place,
        d_out4,
        pre,
        copied=[rest_all],
        scratch=[
            pltpu.VMEM((n_group, d + w, width), BF),
            pltpu.SemaphoreType.DMA((2 * (inner // 256),)),
        ],
    )
    own_hidden, near_hidden, far_hidden = call(
        partial(hidden_grad_kernel, n_group, d),
        [shape((depth, d, inner), F32)] + [shape((half, d, inner), BF)] * 2,
        place,
        normed4,
        d_pre,
        scratch=[pltpu.VMEM((2 * d, inner), F32)],
    )
    d_first, d_attn, sums1 = call(
        norm_back_kernel,
        [shape((n, width), F32), shape((n, width), BF), shape((8, width), F32)],
        place,
        d_second,
        *at.scatter_team(near, keep),
        hat,
        factor,
        vec,
        after=[far_hidden],
    )
    heads_rows = at.heads_at * d
    sent_hidden = add_far(own_hidden, at.send_y(far_hidden))
    came_hidden = at.other_half(sent_hidden)
    out_own, out_sent, d_attn4 = call(
        partial(out_grad_kernel, d),
        [
            shape((heads_rows, width), F32),
            shape((heads_rows, width), BF),
            shape((all_rows, width), BF),
        ],
        place,
        mixed,
        *at.gather_team(d_attn),
        after=[sent_hidden],
        scratch=[pltpu.VMEM((part, width), F32)],
    )
    d_joint, own_joint, near_joint, far_joint = call(
        partial(attention_back_kernel, n_group, d, f, n),
        [
            shape((all_rows, 3 * part), BF),
            shape((depth, d + EXTRA, 3 * part), F32),
            shape((half, d + EXTRA, 3 * part), BF),
            shape((half, d + EXTRA, 3 * part), BF),
        ],
        place,
        d_attn4,
        w_out,
        joint,
        probs,
        *packed,
        sums1,
        sums2,
        d_hb,
        scratch=[
            pltpu.VMEM((all_rows, width), BF),
            pltpu.VMEM((2 * d, 3 * part), F32),
            pltpu.VMEM((8, width), F32),
            pltpu.VMEM((n_group, EXTRA, 3 * part), F32),
        ],
    )
    out_sum = out_own + at.send_y(out_sent).astype(F32)
    sent_joint = add_far(own_joint, at.send_y(far_joint), [came_hidden, out_sum])
    blocks = []
    for i in range(at.heads_at):
        block = out_sum[i * d : (i + 1) * d]
        for flip in list(at.steps_down(at.half))[:0:-1]:
            block = block + at.send_heads(block.astype(BF), i, flip, True).astype(F32)
        blocks.append(block)
    (sent_y,) = relay(place, (near_hidden,), after=[sent_joint])
    came_joint = at.other_half(sent_joint)
    hidden_parts = add_near(own_hidden, at.send_y(sent_y), came_hidden)
    g_out = jnp.zeros((d, width), F32)
    for i, block in enumerate(blocks):
        block = block + at.send_heads(block.astype(BF), i, at.half, True).astype(F32)
        here = at.z == at.t * at.heads_at + i
        g_out = g_out + jnp.where(here, block, jnp.zeros_like(block))
    g_hidden = sum_group(*hidden_parts)
    back_far = at.send_team(g_back, 2)
    joint_parts = add_near(own_joint, at.send_y(near_joint), came_joint, [g_out])
    g_joint = sum_group(*joint_parts)
    near, keep = call(
        partial(token_back_kernel, n, d),
        [shape((2 * n, width), BF), shape((2 * n, width), F32)],
        place,
        d_joint,
        *first_all,
        after=[],
        scratch=[pltpu.VMEM((width, 3 * part), BF)],
    )
    kept, got, far = at.scatter_team(near, keep)
    g_out = at.over_copies(g_out.astype(BF))
    grad_tokens = d_first + kept[:n] + got[:n].astype(F32) + far.astype(F32)

    (g_hidden_out,) = call(
        back_out_kernel, [shape((f, width), F32)], place, g_back, at.send_team(g_back, 1), back_far, at.send_team(back_far, 1)
    )
    (g_hidden_in,) = call(
        partial(hidden_out_kernel, n_group),
        [shape((d, TEAM * inner), F32)],
        place,
        *at.gather_team(g_hidden),
    )
    joint_far = at.send_team(g_joint, 2)
    (joint_sent,) = relay(place, (joint_far,), after=[g_hidden_out, g_hidden_in, grad_tokens])
    g_attention_in, g_attention_out, *g_small = call(
        partial(attention_out_kernel, f),
        [shape((d, 3 * width), F32), shape((d, width), F32)]
        + [shape((1, d), F32)] * 8
        + [shape((1, f), F32)],
        place,
        g_joint,
        at.send_team(g_joint, 1),
        joint_far,
        at.send_team(joint_sent, 1),
        at.spread_heads(g_out),
    )
    g_qb, g_vb, g_ob, g_g1, g_s1, g_outb, g_g2, g_s2, g_hb = (v.reshape(-1) for v in g_small)
    return (
        layer_out,
        grad_tokens,
        g_attention_in,
        g_qb,
        g_vb,
        g_attention_out,
        g_ob,
        g_g1,
        g_s1,
        g_hidden_in,
        g_hb,
        g_hidden_out,
        g_outb,
        g_g2,
        g_s2,
    )


def solution(mesh):
    rows = P(("replica", "group"), None)
    matrix = P("group", None)
    vector = P("group")
    params = (
        matrix,
        vector,
        vector,
        matrix,
        vector,
        vector,
        vector,
        matrix,
        vector,
        matrix,
        vector,
        vector,
        vector,
    )
    return jax.shard_map(
        shards,
        mesh=mesh,
        in_specs=(rows, rows, rows) + params,
        out_specs=(rows, rows) + params,
        check_vma=False,
    )
```

```python
from functools import partial

import jax
import jax.numpy as jnp
from jax import lax
from jax.experimental import pallas as pl
from jax.experimental.pallas import tpu as pltpu
from jax.sharding import PartitionSpec as P

H = 16
HD = 64
SEQS = 4
TEAM = 4
EXTRA = 16
PAIR = 2 * HD
BF = jnp.bfloat16
F32 = jnp.float32


class Places:
    def __init__(self):
        self.n_group = lax.axis_size("group")
        self.n_replica = lax.axis_size("replica")
        self.depth = self.n_group // 2
        self.half = self.depth // 2
        self.heads_at = self.depth // TEAM
        place = lax.axis_index("group")
        self.z = place // 2
        self.t = lax.axis_index("replica") % TEAM
        self.place = jnp.stack([self.t, self.z, place % 2]).astype(jnp.int32)

    def send_z(self, value, flip):
        return lax.ppermute(
            value, "group", [(g, g ^ (2 * flip)) for g in range(self.n_group)]
        )

    def send_y(self, value):
        return lax.ppermute(value, "group", [(g, g ^ 1) for g in range(self.n_group)])

    def send_team(self, value, flip):
        return lax.ppermute(value, "replica", [(r, r ^ flip) for r in range(self.n_replica)])

    def send_heads(self, value, at, flip, back):
        pairs = []
        for r in range(self.n_replica):
            home = r % TEAM * self.heads_at + at
            for z in range(self.depth):
                if (z ^ home) & (2 * flip - 1) == 0:
                    for y in range(2):
                        near = r * self.n_group + z * 2 + y
                        pairs.append((near ^ (2 * flip), near) if back else (near, near ^ (2 * flip)))
        return lax.ppermute(value, ("replica", "group"), pairs)

    def steps_down(self, top):
        while top >= 1:
            yield top
            top //= 2

    def other_half(self, blocks):
        return self.send_z(blocks, self.half)

    def spread_heads(self, block):
        for flip in (2, 1):
            pairs = []
            for r in range(self.n_replica):
                for g in range(self.n_group):
                    apart = r % TEAM ^ g // 2 // self.heads_at
                    if apart == 0 or (flip == 1 and apart == 2):
                        pairs.append((r * self.n_group + g, (r ^ flip) * self.n_group + g))
            block = block + lax.ppermute(block, ("replica", "group"), pairs)
        return block

    def gather_team(self, block):
        far = self.send_team(block, 2)
        near = self.send_team(block, 1)
        return [block, near, far, self.send_team(far, 1)]

    def scatter_near(self, near, keep):
        n = near.shape[0] // 2
        got = self.send_team(near, 1)
        return got, (keep[n:] + got[n:].astype(F32)).astype(BF)

    def scatter_team(self, near, keep):
        got, sent = self.scatter_near(near, keep)
        return keep, got, self.send_team(sent, 2)

    def over_copies(self, value):
        teams = self.n_replica // TEAM
        if teams == 1:
            return value
        return lax.psum(
            value,
            "replica",
            axis_index_groups=[
                [team * TEAM + t for team in range(teams)] for t in range(TEAM)
            ],
        )


def call(kernel, outs, place, *args, scratch=(), after=()):
    specs = [pl.BlockSpec(memory_space=pltpu.VMEM)] * len(args)
    body = kernel
    if after:
        read = len(args)
        specs += [pl.BlockSpec(memory_space=pl.ANY)] * len(after)
        args = (*args, *after)

        def body(place, *refs):
            kernel(place, *refs[:read], *refs[read + len(after) :])

    return pl.pallas_call(
        body,
        name=getattr(kernel, "func", kernel).__name__,
        out_shape=outs,
        in_specs=[pl.BlockSpec(memory_space=pltpu.SMEM)] + specs,
        out_specs=[pl.BlockSpec(memory_space=pltpu.VMEM)] * len(outs),
        scratch_shapes=list(scratch),
        compiler_params=pltpu.CompilerParams(vmem_limit_bytes=8 << 20),
        cost_estimate=pl.CostEstimate(flops=0, bytes_accessed=0, transcendentals=0),
    )(place, *args)


def shape(dims, dtype):
    return jax.ShapeDtypeStruct(tuple(dims), dtype)


def times(left, right):
    return jnp.dot(left, right, preferred_element_type=F32)


def against(left, weight):
    return lax.dot_general(left, weight, (((1,), (1,)), ((), ())), preferred_element_type=F32)


def outer(left, right):
    return lax.dot_general(left, right, (((0,), (0,)), ((), ())), preferred_element_type=F32)


def chosen(index, cases):
    result = cases[-1]
    for at in range(len(cases) - 2, -1, -1):
        result = jnp.where(index == at, cases[at], result)
    return result


def of_member(t, member, blocks):
    return chosen(t, [blocks[i ^ member] for i in range(TEAM)])


def column_sum(value):
    return jnp.sum(value, 0, keepdims=True)


def ends_of(block, n):
    row = block[n : n + EXTRA, 0:128].astype(F32)[0:1]
    lane = lax.broadcasted_iota(jnp.int32, (1, 128), 1)
    return [
        jnp.sum(jnp.where(lane <= s, row, 0.0), axis=1, keepdims=True) for s in range(SEQS)
    ]


def segments(ends, dims, axis):
    place = lax.broadcasted_iota(jnp.int32, dims, axis).astype(F32)
    total = jnp.zeros(dims, F32)
    for end in ends:
        total = total + jnp.where(place >= end, 1.0, 0.0)
    return total


def normalise(value):
    centre = jnp.mean(value, -1, keepdims=True)
    offset = value - centre
    spread = jnp.mean(offset * offset, -1, keepdims=True)
    factor = lax.rsqrt(spread + 1e-06)
    return offset * factor, factor


def normalise_back(d_hat, hat, factor):
    return factor * (
        d_hat
        - jnp.mean(d_hat, -1, keepdims=True)
        - hat * jnp.mean(d_hat * hat, -1, keepdims=True)
    )


def grad_tiles(place, n_group, width, left, right, own, near, far, tile):
    depth = n_group // 2
    half = depth // 2
    z, y = place[1], place[2]

    def step(at, carry):
        tile[...] = outer(left[:, pl.ds(pl.multiple_of(at * 2 * width, 2 * width), 2 * width)], right[...])
        k = lax.bitwise_xor(z, at)
        own[k, 0:width, :] = tile[pl.ds(pl.multiple_of(y * width, width), width), :]
        sent = tile[pl.ds(pl.multiple_of((1 - y) * width, width), width), :].astype(BF)

        @pl.when(k < half)
        def _():
            near[k, 0:width, :] = sent

        @pl.when(k >= half)
        def _():
            far[k - half, 0:width, :] = sent

        return carry

    lax.fori_loop(0, depth, step, 0)


def to_team(value, n, near, keep, columns):
    keep[0:n, columns] = value[0:n]
    near[0:n, columns] = value[n : 2 * n].astype(BF)
    keep[n : 2 * n, columns] = value[2 * n : 3 * n]
    near[n : 2 * n, columns] = value[3 * n : 4 * n].astype(BF)


def at_group(place, n_group, i):
    depth = n_group // 2
    dy, k = divmod(i, depth)
    y = place[2]
    return lax.rem(place[1] - k + depth, depth) * 2 + (y if dy == 0 else 1 - y)


def relay_kernel(counts, place, *refs):
    outs = refs[sum(counts) :]
    for out, count in zip(outs, counts):
        parts, refs = refs[:count], refs[count:]
        at = 0
        for part in parts:
            out[at : at + part.shape[0]] = part[...]
            at += part.shape[0]


def relay(place, *tasks, after=()):
    outs = [
        shape((sum(part.shape[0] for part in task), *task[0].shape[1:]), task[0].dtype)
        for task in tasks
    ]
    flat = [part for task in tasks for part in task]
    return call(
        partial(relay_kernel, [len(task) for task in tasks]), outs, place, *flat, after=after
    )


def group_blocks(place, quarters):
    half = quarters[0].shape[0]
    for q, quarter in enumerate(quarters):
        for i in range(half):
            dz, dy = q % 2 * half + i, q // 2
            z = lax.bitwise_xor(place[1], dz)
            yield z * 2 + lax.bitwise_xor(place[2], dy), quarter.at[i]


def assemble(place, quarters, rows, whole):
    for g, block in group_blocks(place, quarters):
        whole[pl.ds(pl.multiple_of(g * rows, rows), rows), :] = block[0:rows]


def prepare_first_kernel(place, att, small, first_o):
    t = place[0]
    d, joint = att.shape
    width = joint // 3
    part = width // TEAM
    for i in range(3):
        first_o[0, 0:d, i * part : (i + 1) * part] = chosen(
            t,
            [
                att[:, i * width + s * part : i * width + (s + 1) * part]
                for s in range(TEAM)
            ],
        )
    first_o[0, d : d + EXTRA, :] = small[...]


def prepare_rest_kernel(n_group, place, hid, back, rest_o):
    t = place[0]
    d = hid.shape[0]
    f = hid.shape[1] // n_group
    w = f // TEAM
    for g in range(n_group):
        rest_o[0:d, g * w : (g + 1) * w] = chosen(
            t, [hid[:, g * f + s * w : g * f + (s + 1) * w] for s in range(TEAM)]
        )
    rest_o[d : d + w, :] = back[pl.ds(pl.multiple_of(t * w, w), w), :]


def attention_kernel(
    n_group, d, f, n, place, p0, p1, p2, p3, own_out, other_out, *refs
):
    first, refs = refs[:4], refs[4:]
    (
        joint_o, probs_o, mixed_o, near_o, keep_o, vec_o, hb_o, wout_o, first_s, token_s, small_s,
    ) = refs
    blocks = (p0, p1, p2, p3)
    t, y = place[0], place[2]
    part = wout_o.shape[0]
    width = wout_o.shape[1]
    w = f // TEAM
    assemble(place, first, d, first_s)
    for g, block in group_blocks(place, first):
        small_s[g] = block[d : d + EXTRA, :].astype(F32)
    small = [small_s[g] for g in range(n_group)]
    vec_o[...] = jnp.concatenate([s[0:8, 0:d] for s in small], 1)
    hb_o[...] = jnp.concatenate(
        [chosen(t, [s[8:9, i * w : (i + 1) * w] for i in range(TEAM)]) for s in small], 1
    )
    for at in range(part // (2 * d)):
        wout_o[pl.ds(pl.multiple_of((at * 2 + y) * d, d), d), :] = own_out[
            at * d : (at + 1) * d
        ]
        wout_o[pl.ds(pl.multiple_of((at * 2 + 1 - y) * d, d), d), :] = other_out[
            at * d : (at + 1) * d
        ]
    for b in range(TEAM):
        token_s[b * n : (b + 1) * n] = blocks[b][0:n]
    mine = pl.ds(pl.multiple_of(t * part, part), part)
    for i in range(3):
        value = times(token_s[...], first_s[:, i * part : (i + 1) * part])
        if i == 0:
            value = value + vec_o[0:1, mine]
        if i == 2:
            value = value + vec_o[1:2, mine]
        joint_o[:, i * part : (i + 1) * part] = value.astype(BF)
    scale = HD ** (-0.5)
    low = lax.broadcasted_iota(jnp.int32, (1, PAIR), 1) < HD
    zero = jnp.zeros((), BF)
    for b in range(TEAM):
        rows = slice(b * n, (b + 1) * n)
        ends = ends_of(blocks[b], n)
        same = segments(ends, (n, 1), 0) == segments(ends, (1, n), 1)
        for pair in range(part // PAIR):
            at = pair * PAIR
            query = joint_o[rows, at : at + PAIR]
            keys = joint_o[rows, part + at : part + at + PAIR]
            values = joint_o[rows, 2 * part + at : 2 * part + at + PAIR]
            mixed = []
            for h in range(2):
                sided = jnp.where(low, query, zero) if h == 0 else jnp.where(low, zero, query)
                scores = jnp.where(same, against(sided, keys) * scale, -1000000000.0)
                expo = jnp.exp(scores - jnp.max(scores, -1, keepdims=True))
                probs = expo / jnp.sum(expo, -1, keepdims=True)
                probs = probs.astype(BF)
                probs_o[(b * (part // PAIR) + pair) * 2 + h] = probs
                mixed.append(times(probs, values))
            mixed_o[rows, at : at + PAIR] = jnp.where(low, mixed[0], mixed[1]).astype(BF)
    for at in range(0, width, part):
        columns = slice(at, at + part)
        to_team(times(mixed_o[...], wout_o[:, columns]), n, near_o, keep_o, columns)


def norm_kernel(place, tokens, keep, got, far, vec, normed_o, low_o, hat_o, factor_o):
    n = tokens.shape[0]
    attn = keep[0:n] + got[0:n].astype(F32) + far[...].astype(F32) + vec[2:3]
    hat, factor = normalise(tokens[...].astype(F32) + attn)
    normed = hat * vec[3:4] + vec[4:5]
    normed_o[...] = normed
    low_o[...] = normed.astype(BF)
    hat_o[...] = hat
    factor_o[...] = jnp.broadcast_to(factor, factor_o.shape)


def gelu_parts(pre):
    bell = 0.5 * (1.0 + lax.erf(pre * (2.0**-0.5)))
    return bell, jnp.exp(-0.5 * pre * pre) * (2.0 * 3.141592653589793) ** -0.5


def feed_kernel(
    n_group, d, place, x0, x1, x2, x3, hb, rest, pre_o, act_o, near_o, keep_o, x_o
):
    n = x0.shape[0]
    w = rest.shape[1] - d
    for b, block in enumerate((x0, x1, x2, x3)):
        x_o[b * n : (b + 1) * n] = block[...]

    def entering(at, carry):
        columns = pl.ds(pl.multiple_of(at * 256, 256), 256)
        weight = rest[:, 0:d, columns].reshape(n_group * d, 256)
        pre = times(x_o[...], weight) + hb[:, columns]
        pre_o[:, columns] = pre
        act_o[:, columns] = (pre * gelu_parts(pre)[0]).astype(BF)
        return carry

    lax.fori_loop(0, pre_o.shape[1] // 256, entering, 0)

    def leaving(at, carry):
        columns = pl.ds(pl.multiple_of(at * 256, 256), 256)
        weight = rest[:, d : d + w, columns].reshape(n_group * w, 256)
        to_team(times(act_o[...], weight), n, near_o, keep_o, columns)
        return carry

    lax.fori_loop(0, keep_o.shape[1] // 256, leaving, 0)


def second_kernel(
    place, normed, keep, got, far, vec, cotangent, packed, layer_o, d_second_o, d_out_o, sums_o
):
    n = normed.shape[0]
    out = keep[0:n] + got[0:n].astype(F32) + far[...].astype(F32) + vec[5:6]
    hat, factor = normalise(normed[...] + out)
    live = jnp.where(segments(ends_of(packed, n), (n, 1), 0) < SEQS, 1.0, 0.0)
    layer_o[...] = ((hat * vec[6:7] + vec[7:8]) * live).astype(BF)
    d_final = cotangent[...].astype(F32) * live
    d_second = normalise_back(d_final * vec[6:7], hat, factor)
    d_second_o[...] = d_second
    d_out = d_second.astype(BF)
    d_out_o[...] = d_out
    sums_o[...] = jnp.zeros_like(sums_o)
    sums_o[0:1] = column_sum(d_out.astype(F32))
    sums_o[1:2] = column_sum(d_final * hat)
    sums_o[2:3] = column_sum(d_final)


def back_grad_kernel(place, d0, d1, d2, d3, act, grad_o, d_out_o):
    n = d0.shape[0]
    for b, block in enumerate((d0, d1, d2, d3)):
        d_out_o[b * n : (b + 1) * n] = block[...]

    def step(at, carry):
        rows = pl.ds(pl.multiple_of(at * 256, 256), 256)
        grad_o[rows, :] = outer(act[:, rows], d_out_o[...]).astype(BF)
        return carry

    lax.fori_loop(0, grad_o.shape[0] // 256, step, 0)


def feed_back_kernel(n_group, d, n, place, d_out, rest, pre, d_pre_o, near_o, keep_o, hb_o):
    w = rest.shape[1] - d
    per = 256 // w

    def through(at, carry):
        columns = pl.ds(pl.multiple_of(at * 256, 256), 256)
        weight = rest[pl.ds(at * per, per), d : d + w, :].reshape(256, rest.shape[2])
        d_act = against(d_out[...], weight)
        value = pre[:, columns]
        bell, slope = gelu_parts(value)
        d_pre = (d_act * (bell + value * slope)).astype(BF)
        d_pre_o[:, columns] = d_pre
        hb_o[:, columns] = column_sum(d_pre.astype(F32))
        return carry

    lax.fori_loop(0, pre.shape[1] // 256, through, 0)
    rows = 256 // d

    def entering(at, carry):
        columns = pl.ds(pl.multiple_of(at * 256, 256), 256)
        weight = rest[pl.ds(at * rows, rows), 0:d, :].reshape(256, rest.shape[2])
        to_team(against(d_pre_o[...], weight), n, near_o, keep_o, columns)
        return carry

    lax.fori_loop(0, keep_o.shape[1] // 256, entering, 0)


def hidden_grad_kernel(n_group, d, place, x, d_pre, own_o, near_o, far_o, tile):
    grad_tiles(place, n_group, d, x, d_pre, own_o, near_o, far_o, tile)


def norm_back_kernel(
    place, d_second, keep, got, far, hat, factor, vec, d_first_o, d_attn_o, sums_o
):
    n = d_second.shape[0]
    d_normed = d_second[...] + keep[0:n] + got[0:n].astype(F32) + far[...].astype(F32)
    d_first = normalise_back(d_normed * vec[3:4], hat[...], factor[:, 0:1])
    d_first_o[...] = d_first
    d_attn = d_first.astype(BF)
    d_attn_o[...] = d_attn
    sums_o[...] = jnp.zeros_like(sums_o)
    sums_o[0:1] = column_sum(d_attn.astype(F32))
    sums_o[1:2] = column_sum(d_normed * hat[...])
    sums_o[2:3] = column_sum(d_normed)


def attention_back_kernel(
    n_group, d, f, n, place, d_attn, wout, joint, probs_in, p0, p1, p2, p3,
    sums1, sums2, d_hb,
    d_joint_o, own_o, near_o, far_o, token_s, tile, vec_s, small_s,
):
    t, z, y = place[0], place[1], place[2]
    depth = n_group // 2
    part = wout.shape[0]
    w = f // TEAM
    for b in range(TEAM):
        token_s[b * n : (b + 1) * n] = (p0, p1, p2, p3)[b][0:n]
    d_mixed = against(d_attn[...], wout[...]).astype(BF)
    scale = HD ** (-0.5)
    low = lax.broadcasted_iota(jnp.int32, (1, PAIR), 1) < HD
    zero = jnp.zeros((), BF)
    for b in range(TEAM):
        rows = slice(b * n, (b + 1) * n)
        for pair in range(part // PAIR):
            at = pair * PAIR
            query = joint[rows, at : at + PAIR]
            keys = joint[rows, part + at : part + at + PAIR]
            values = joint[rows, 2 * part + at : 2 * part + at + PAIR]
            d_mix = d_mixed[rows, at : at + PAIR]
            d_query, d_keys, d_values = [], [], []
            for h in range(2):
                low_probs = probs_in[(b * (part // PAIR) + pair) * 2 + h]
                probs = low_probs.astype(F32)
                sided = jnp.where(low, d_mix, zero) if h == 0 else jnp.where(low, zero, d_mix)
                d_probs = against(sided, values)
                d_scores = (
                    probs * (d_probs - jnp.sum(probs * d_probs, -1, keepdims=True))
                ).astype(BF)
                d_values.append(outer(low_probs, d_mix))
                d_query.append(times(d_scores, keys))
                d_keys.append(outer(d_scores, query))
            for i, (value, factor) in enumerate(
                ((d_query, scale), (d_keys, scale), (d_values, 1.0))
            ):
                d_joint_o[rows, i * part + at : i * part + at + PAIR] = (
                    jnp.where(low, value[0], value[1]) * factor
                ).astype(BF)
    vec_s[...] = jnp.zeros_like(vec_s)
    mine = pl.ds(pl.multiple_of(t * part, part), part)
    vec_s[0:1, mine] = column_sum(d_joint_o[:, 0:part].astype(F32))
    vec_s[1:2, mine] = column_sum(d_joint_o[:, 2 * part : 3 * part].astype(F32))
    vec_s[2:5, :] = sums1[0:3]
    vec_s[5:8, :] = sums2[0:3]
    small_s[...] = jnp.zeros_like(small_s)
    for g in range(n_group):
        small_s[g, 0:8, 0:d] = vec_s[:, g * d : (g + 1) * d]
        row = d_hb[:, g * w : (g + 1) * w]
        small_s[g, 8:9, 0:f] = jnp.concatenate(
            [jnp.where(t == i, row, jnp.zeros_like(row)) for i in range(TEAM)], 1
        )
    grad_tiles(place, n_group, d, token_s, d_joint_o, own_o, near_o, far_o, tile)
    half = depth // 2
    for k in range(depth):
        g = lax.bitwise_xor(z, k) * 2
        own_o[k, d : d + EXTRA, :] = small_s[g + y]
        sent_o = far_o if k >= half else near_o
        sent_o[k % half, d : d + EXTRA, :] = small_s[g + 1 - y].astype(BF)


def out_grad_kernel(d, place, mixed, a0, a1, a2, a3, out_own_o, out_other_o, attn_o, heads_s):
    n = a0.shape[0]
    y = place[2]
    for b, block in enumerate((a0, a1, a2, a3)):
        attn_o[b * n : (b + 1) * n] = block[...]
    heads_s[...] = outer(mixed[...], attn_o[...])
    for at in range(mixed.shape[1] // (2 * d)):
        out_own_o[at * d : (at + 1) * d] = heads_s[
            pl.ds(pl.multiple_of((at * 2 + y) * d, d), d), :
        ]
        out_other_o[at * d : (at + 1) * d] = heads_s[
            pl.ds(pl.multiple_of((at * 2 + 1 - y) * d, d), d), :
        ].astype(BF)


def token_back_kernel(n, d, place, d_joint, f0, f1, f2, f3, near_o, keep_o, first_s):
    assemble(place, (f0, f1, f2, f3), d, first_s)

    def step(at, carry):
        columns = pl.ds(pl.multiple_of(at * 256, 256), 256)
        to_team(against(d_joint[...], first_s[columns, :]), n, near_o, keep_o, columns)
        return carry

    lax.fori_loop(0, keep_o.shape[1] // 256, step, 0)


def add_far_kernel(place, own, got, sum_o):
    half = sum_o.shape[0]
    sum_o[...] = (own[half : 2 * half] + got[0:half].astype(F32)).astype(BF)


def add_near_kernel(place, own, got, far, keep_o, send_o):
    half = far.shape[0]
    total = own[0:half] + got[got.shape[0] - half :].astype(F32) + far[...].astype(F32)
    keep_o[...] = total[0 : half // 2]
    send_o[...] = total[half // 2 :].astype(BF)


def back_out_kernel(place, b0, b1, b2, b3, back_o):
    w = b0.shape[0]
    for i in range(TEAM):
        block = of_member(place[0], i, [b[...] for b in (b0, b1, b2, b3)])
        back_o[i * w : (i + 1) * w] = block.astype(F32)


def hidden_out_kernel(n_group, place, h0, h1, h2, h3, hidden_o):
    w = h0.shape[1] // n_group
    for i in range(TEAM):
        block = of_member(place[0], i, [h[...] for h in (h0, h1, h2, h3)]).astype(F32)
        for g in range(n_group):
            at = (g * TEAM + i) * w
            hidden_o[:, at : at + w] = block[:, g * w : (g + 1) * w]


def attention_out_kernel(f, place, j0, j1, j2, j3, out, joint_o, out_o, *small_o):
    t = place[0]
    d = out_o.shape[0]
    part = j0.shape[1] // 3
    width = part * TEAM
    total = jnp.zeros((EXTRA, 3 * part), F32)
    for i in range(TEAM):
        block = of_member(t, i, [j[...] for j in (j0, j1, j2, j3)]).astype(F32)
        for s in range(3):
            at = s * width + i * part
            joint_o[:, at : at + part] = block[0:d, s * part : (s + 1) * part]
        total = total + block[d : d + EXTRA]
    out_o[...] = out[...].astype(F32)
    for i in range(8):
        small_o[i][...] = total[i : i + 1, 0:d]
    small_o[8][...] = total[8:9, 0:f]


def shards(
    tokens,
    lengths,
    cotangent,
    attention_in,
    query_bias,
    value_bias,
    attention_out,
    out_bias,
    first_gain,
    first_shift,
    hidden_in,
    hidden_bias,
    hidden_out,
    output_bias,
    second_gain,
    second_shift,
):
    at = Places()
    n_group, depth, place = at.n_group, at.depth, at.place
    n, width = tokens.shape
    d = attention_in.shape[0]
    f = hidden_bias.shape[0]
    w = f // TEAM
    part = width // TEAM
    inner = w * n_group
    all_rows = TEAM * n

    vectors = (
        query_bias,
        value_bias,
        out_bias,
        first_gain,
        first_shift,
        output_bias,
        second_gain,
        second_shift,
    )
    small = jnp.concatenate(
        [
            jnp.pad(jnp.stack(vectors), ((0, 0), (0, 3 * part - d))),
            jnp.pad(hidden_bias[None], ((0, EXTRA - 9), (0, 3 * part - f))),
        ],
        0,
    )
    extra = jnp.pad(lengths.astype(BF), ((0, EXTRA - 1), (0, width - lengths.shape[1])))
    packed = jnp.concatenate([tokens, extra], 0)
    (first_near,) = call(
        prepare_first_kernel,
        [shape((1, d + EXTRA, 3 * part), BF)],
        place,
        attention_in,
        small,
    )
    def widen(blocks):
        for flip in list(at.steps_down(at.half // 2))[::-1]:
            blocks = (blocks, at.send_z(blocks, flip))
            if flip < at.half // 2:
                (blocks,) = relay(place, blocks)
        return blocks

    heads_mine, heads_first = [], []
    for i in range(at.heads_at):
        home = at.t * at.heads_at + i
        value = jnp.where(at.z == home, attention_out, jnp.zeros_like(attention_out))
        (value,) = relay(place, (value,), after=[first_near])
        for flip in at.steps_down(at.half):
            value = value + at.send_heads(value, i, flip, False)
            if flip == at.half:
                heads_first.append(value)
        heads_mine.append(value)
    out_mine = jnp.concatenate(heads_mine, 0)
    out_other = at.send_y(out_mine)
    packed_far = at.send_team(packed, 2)
    packed = [packed, at.send_team(packed, 1), packed_far, at.send_team(packed_far, 1)]

    (first_near,) = relay(place, widen(first_near), after=heads_first)
    (rest_mine,) = call(
        partial(prepare_rest_kernel, n_group),
        [shape((d + w, width), BF)],
        place,
        hidden_in,
        hidden_out,
        after=[first_near],
    )
    rest_all = lax.all_gather(rest_mine, "group", axis=0)
    first_far = at.other_half(first_near)
    first_near_y = at.send_y(first_near)
    (first_sent,) = relay(place, (first_far,), after=[first_near_y, out_other, *packed])
    first_all = [first_near, first_far, first_near_y, at.send_y(first_sent)]

    joint, probs, mixed, near, keep, vec, hb, w_out = call(
        partial(attention_kernel, n_group, d, f, n),
        [
            shape((all_rows, 3 * part), BF),
            shape((TEAM * H // TEAM, n, n), BF),
            shape((all_rows, part), BF),
            shape((2 * n, width), BF),
            shape((2 * n, width), F32),
            shape((8, width), F32),
            shape((1, inner), F32),
            shape((part, width), BF),
        ],
        place,
        *packed,
        out_mine,
        out_other,
        *first_all,
        scratch=[
            pltpu.VMEM((width, 3 * part), BF),
            pltpu.VMEM((all_rows, width), BF),
            pltpu.VMEM((n_group, EXTRA, 3 * part), F32),
        ],
    )
    normed, normed_low, hat, factor = call(
        norm_kernel,
        [
            shape((n, width), F32),
            shape((n, width), BF),
            shape((n, width), F32),
            shape((n, 128), F32),
        ],
        place,
        tokens,
        *at.scatter_team(near, keep),
        vec,
    )

    pre, act, near, keep, normed4 = call(
        partial(feed_kernel, n_group, d),
        [
            shape((all_rows, inner), F32),
            shape((all_rows, inner), BF),
            shape((2 * n, width), BF),
            shape((2 * n, width), F32),
            shape((all_rows, width), BF),
        ],
        place,
        *at.gather_team(normed_low),
        hb,
        rest_all,
    )
    layer_out, d_second, d_out, sums2 = call(
        second_kernel,
        [
            shape((n, width), BF),
            shape((n, width), F32),
            shape((n, width), BF),
            shape((8, width), F32),
        ],
        place,
        normed,
        *at.scatter_team(near, keep),
        vec,
        cotangent,
        packed[0],
    )

    def add_near(own, came_y, came_z, after=()):
        half, *rest = came_z.shape
        return call(
            add_near_kernel,
            [shape((half // 2, *rest), F32), shape((half // 2, *rest), BF)],
            place,
            own,
            came_y,
            came_z,
            after=after,
        )

    def sum_group(keep, send):
        flip = at.half // 2
        while flip > 1:
            total = keep + at.send_z(send, flip).astype(F32)
            flip //= 2
            keep, send = total[:flip], total[flip:].astype(BF)
        return at.over_copies((keep + at.send_z(send, 1).astype(F32))[0].astype(BF))

    half = depth // 2
    def add_far(own, came, after=()):
        half, rest = own.shape[0] // 2, own.shape[1:]
        return call(add_far_kernel, [shape((half, *rest), BF)], place, own, came, after=after)[0]

    grad_back, d_out4 = call(
        back_grad_kernel,
        [shape((inner, width), BF), shape((all_rows, width), BF)],
        place,
        *at.gather_team(d_out),
        act,
    )
    g_back = at.over_copies(
        lax.psum_scatter(grad_back, "group", scatter_dimension=0, tiled=True)
    )
    d_pre, near, keep, d_hb = call(
        partial(feed_back_kernel, n_group, d, n),
        [
            shape((all_rows, inner), BF),
            shape((2 * n, width), BF),
            shape((2 * n, width), F32),
            shape((1, inner), F32),
        ],
        place,
        d_out4,
        rest_all,
        pre,
    )
    own_hidden, near_hidden, far_hidden = call(
        partial(hidden_grad_kernel, n_group, d),
        [shape((depth, d, inner), F32)] + [shape((half, d, inner), BF)] * 2,
        place,
        normed4,
        d_pre,
        scratch=[pltpu.VMEM((2 * d, inner), F32)],
    )
    d_first, d_attn, sums1 = call(
        norm_back_kernel,
        [shape((n, width), F32), shape((n, width), BF), shape((8, width), F32)],
        place,
        d_second,
        *at.scatter_team(near, keep),
        hat,
        factor,
        vec,
        after=[far_hidden],
    )
    heads_rows = at.heads_at * d
    sent_hidden = add_far(own_hidden, at.send_y(far_hidden))
    came_hidden = at.other_half(sent_hidden)
    out_own, out_sent, d_attn4 = call(
        partial(out_grad_kernel, d),
        [
            shape((heads_rows, width), F32),
            shape((heads_rows, width), BF),
            shape((all_rows, width), BF),
        ],
        place,
        mixed,
        *at.gather_team(d_attn),
        after=[sent_hidden],
        scratch=[pltpu.VMEM((part, width), F32)],
    )
    d_joint, own_joint, near_joint, far_joint = call(
        partial(attention_back_kernel, n_group, d, f, n),
        [
            shape((all_rows, 3 * part), BF),
            shape((depth, d + EXTRA, 3 * part), F32),
            shape((half, d + EXTRA, 3 * part), BF),
            shape((half, d + EXTRA, 3 * part), BF),
        ],
        place,
        d_attn4,
        w_out,
        joint,
        probs,
        *packed,
        sums1,
        sums2,
        d_hb,
        scratch=[
            pltpu.VMEM((all_rows, width), BF),
            pltpu.VMEM((2 * d, 3 * part), F32),
            pltpu.VMEM((8, width), F32),
            pltpu.VMEM((n_group, EXTRA, 3 * part), F32),
        ],
    )
    out_sum = out_own + at.send_y(out_sent).astype(F32)
    sent_joint = add_far(own_joint, at.send_y(far_joint), [came_hidden, out_sum])
    blocks = []
    for i in range(at.heads_at):
        block = out_sum[i * d : (i + 1) * d]
        for flip in list(at.steps_down(at.half))[:0:-1]:
            block = block + at.send_heads(block.astype(BF), i, flip, True).astype(F32)
        blocks.append(block)
    (sent_y,) = relay(place, (near_hidden,), after=[sent_joint])
    came_joint = at.other_half(sent_joint)
    hidden_parts = add_near(own_hidden, at.send_y(sent_y), came_hidden)
    g_out = jnp.zeros((d, width), F32)
    for i, block in enumerate(blocks):
        block = block + at.send_heads(block.astype(BF), i, at.half, True).astype(F32)
        here = at.z == at.t * at.heads_at + i
        g_out = g_out + jnp.where(here, block, jnp.zeros_like(block))
    g_hidden = sum_group(*hidden_parts)
    back_far = at.send_team(g_back, 2)
    joint_parts = add_near(own_joint, at.send_y(near_joint), came_joint, [g_out])
    g_joint = sum_group(*joint_parts)
    near, keep = call(
        partial(token_back_kernel, n, d),
        [shape((2 * n, width), BF), shape((2 * n, width), F32)],
        place,
        d_joint,
        *first_all,
        after=[],
        scratch=[pltpu.VMEM((width, 3 * part), BF)],
    )
    kept, got, far = at.scatter_team(near, keep)
    g_out = at.over_copies(g_out.astype(BF))
    grad_tokens = d_first + kept[:n] + got[:n].astype(F32) + far.astype(F32)

    (g_hidden_out,) = call(
        back_out_kernel, [shape((f, width), F32)], place, g_back, at.send_team(g_back, 1), back_far, at.send_team(back_far, 1)
    )
    (g_hidden_in,) = call(
        partial(hidden_out_kernel, n_group),
        [shape((d, TEAM * inner), F32)],
        place,
        *at.gather_team(g_hidden),
    )
    joint_far = at.send_team(g_joint, 2)
    (joint_sent,) = relay(place, (joint_far,), after=[g_hidden_out, g_hidden_in, grad_tokens])
    g_attention_in, g_attention_out, *g_small = call(
        partial(attention_out_kernel, f),
        [shape((d, 3 * width), F32), shape((d, width), F32)]
        + [shape((1, d), F32)] * 8
        + [shape((1, f), F32)],
        place,
        g_joint,
        at.send_team(g_joint, 1),
        joint_far,
        at.send_team(joint_sent, 1),
        at.spread_heads(g_out),
    )
    g_qb, g_vb, g_ob, g_g1, g_s1, g_outb, g_g2, g_s2, g_hb = (v.reshape(-1) for v in g_small)
    return (
        layer_out,
        grad_tokens,
        g_attention_in,
        g_qb,
        g_vb,
        g_attention_out,
        g_ob,
        g_g1,
        g_s1,
        g_hidden_in,
        g_hb,
        g_hidden_out,
        g_outb,
        g_g2,
        g_s2,
    )


def solution(mesh):
    rows = P(("replica", "group"), None)
    matrix = P("group", None)
    vector = P("group")
    params = (
        matrix,
        vector,
        vector,
        matrix,
        vector,
        vector,
        vector,
        matrix,
        vector,
        matrix,
        vector,
        vector,
        vector,
    )
    return jax.shard_map(
        shards,
        mesh=mesh,
        in_specs=(rows, rows, rows) + params,
        out_specs=(rows, rows) + params,
        check_vma=False,
    )
```

```python
from functools import partial

import jax
import jax.numpy as jnp
from jax import lax
from jax.experimental import pallas as pl
from jax.experimental.pallas import tpu as pltpu
from jax.sharding import PartitionSpec as P

H = 16
HD = 64
SEQS = 4
TEAM = 4
EXTRA = 16
PAIR = 2 * HD
BF = jnp.bfloat16
F32 = jnp.float32


class Places:
    def __init__(self):
        self.n_group = lax.axis_size("group")
        self.n_replica = lax.axis_size("replica")
        self.depth = self.n_group // 2
        self.half = self.depth // 2
        self.heads_at = self.depth // TEAM
        place = lax.axis_index("group")
        self.z = place // 2
        self.t = lax.axis_index("replica") % TEAM
        self.place = jnp.stack([self.t, self.z, place % 2]).astype(jnp.int32)

    def send_z(self, value, flip):
        return lax.ppermute(
            value, "group", [(g, g ^ (2 * flip)) for g in range(self.n_group)]
        )

    def send_y(self, value):
        return lax.ppermute(value, "group", [(g, g ^ 1) for g in range(self.n_group)])

    def send_team(self, value, flip):
        return lax.ppermute(value, "replica", [(r, r ^ flip) for r in range(self.n_replica)])

    def send_heads(self, value, at, flip, back):
        pairs = []
        for r in range(self.n_replica):
            home = r % TEAM * self.heads_at + at
            for z in range(self.depth):
                if (z ^ home) & (2 * flip - 1) == 0:
                    for y in range(2):
                        near = r * self.n_group + z * 2 + y
                        pairs.append((near ^ (2 * flip), near) if back else (near, near ^ (2 * flip)))
        return lax.ppermute(value, ("replica", "group"), pairs)

    def steps_down(self, top):
        while top >= 1:
            yield top
            top //= 2

    def other_half(self, blocks):
        return self.send_z(blocks, self.half)

    def spread_heads(self, block):
        for flip in (2, 1):
            pairs = []
            for r in range(self.n_replica):
                for g in range(self.n_group):
                    apart = r % TEAM ^ g // 2 // self.heads_at
                    if apart == 0 or (flip == 1 and apart == 2):
                        pairs.append((r * self.n_group + g, (r ^ flip) * self.n_group + g))
            block = block + lax.ppermute(block, ("replica", "group"), pairs)
        return block

    def gather_team(self, block):
        far = self.send_team(block, 2)
        near = self.send_team(block, 1)
        return [block, near, far, self.send_team(far, 1)]

    def scatter_near(self, near, keep):
        n = near.shape[0] // 2
        got = self.send_team(near, 1)
        return got, (keep[n:] + got[n:].astype(F32)).astype(BF)

    def scatter_team(self, near, keep):
        got, sent = self.scatter_near(near, keep)
        return keep, got, self.send_team(sent, 2)

    def over_copies(self, value):
        teams = self.n_replica // TEAM
        if teams == 1:
            return value
        return lax.psum(
            value,
            "replica",
            axis_index_groups=[
                [team * TEAM + t for team in range(teams)] for t in range(TEAM)
            ],
        )


def call(kernel, outs, place, *args, scratch=(), after=()):
    specs = [pl.BlockSpec(memory_space=pltpu.VMEM)] * len(args)
    body = kernel
    if after:
        read = len(args)
        specs += [pl.BlockSpec(memory_space=pl.ANY)] * len(after)
        args = (*args, *after)

        def body(place, *refs):
            kernel(place, *refs[:read], *refs[read + len(after) :])

    return pl.pallas_call(
        body,
        name=getattr(kernel, "func", kernel).__name__,
        out_shape=outs,
        in_specs=[pl.BlockSpec(memory_space=pltpu.SMEM)] + specs,
        out_specs=[pl.BlockSpec(memory_space=pltpu.VMEM)] * len(outs),
        scratch_shapes=list(scratch),
        compiler_params=pltpu.CompilerParams(vmem_limit_bytes=16 << 20),
        cost_estimate=pl.CostEstimate(flops=0, bytes_accessed=0, transcendentals=0),
    )(place, *args)


def shape(dims, dtype):
    return jax.ShapeDtypeStruct(tuple(dims), dtype)


def times(left, right):
    return jnp.dot(left, right, preferred_element_type=F32)


def against(left, weight):
    return lax.dot_general(left, weight, (((1,), (1,)), ((), ())), preferred_element_type=F32)


def outer(left, right):
    return lax.dot_general(left, right, (((0,), (0,)), ((), ())), preferred_element_type=F32)


def chosen(index, cases):
    result = cases[-1]
    for at in range(len(cases) - 2, -1, -1):
        result = jnp.where(index == at, cases[at], result)
    return result


def of_member(t, member, blocks):
    return chosen(t, [blocks[i ^ member] for i in range(TEAM)])


def column_sum(value):
    return jnp.sum(value, 0, keepdims=True)


def ends_of(block, n):
    row = block[n : n + EXTRA, 0:128].astype(F32)[0:1]
    lane = lax.broadcasted_iota(jnp.int32, (1, 128), 1)
    return [
        jnp.sum(jnp.where(lane <= s, row, 0.0), axis=1, keepdims=True) for s in range(SEQS)
    ]


def segments(ends, dims, axis):
    place = lax.broadcasted_iota(jnp.int32, dims, axis).astype(F32)
    total = jnp.zeros(dims, F32)
    for end in ends:
        total = total + jnp.where(place >= end, 1.0, 0.0)
    return total


def normalise(value):
    centre = jnp.mean(value, -1, keepdims=True)
    offset = value - centre
    spread = jnp.mean(offset * offset, -1, keepdims=True)
    factor = lax.rsqrt(spread + 1e-06)
    return offset * factor, factor


def normalise_back(d_hat, hat, factor):
    return factor * (
        d_hat
        - jnp.mean(d_hat, -1, keepdims=True)
        - hat * jnp.mean(d_hat * hat, -1, keepdims=True)
    )


def grad_tiles(place, n_group, width, left, right, own, near, far, tile):
    depth = n_group // 2
    half = depth // 2
    z, y = place[1], place[2]

    def step(at, carry):
        tile[...] = outer(left[:, pl.ds(pl.multiple_of(at * 2 * width, 2 * width), 2 * width)], right[...])
        k = lax.bitwise_xor(z, at)
        own[k, 0:width, :] = tile[pl.ds(pl.multiple_of(y * width, width), width), :]
        sent = tile[pl.ds(pl.multiple_of((1 - y) * width, width), width), :].astype(BF)

        @pl.when(k < half)
        def _():
            near[k, 0:width, :] = sent

        @pl.when(k >= half)
        def _():
            far[k - half, 0:width, :] = sent

        return carry

    lax.fori_loop(0, depth, step, 0)


def to_team(value, n, near, keep, columns):
    keep[0:n, columns] = value[0:n]
    near[0:n, columns] = value[n : 2 * n].astype(BF)
    keep[n : 2 * n, columns] = value[2 * n : 3 * n]
    near[n : 2 * n, columns] = value[3 * n : 4 * n].astype(BF)


def at_group(place, n_group, i):
    depth = n_group // 2
    dy, k = divmod(i, depth)
    y = place[2]
    return lax.rem(place[1] - k + depth, depth) * 2 + (y if dy == 0 else 1 - y)


def relay_kernel(counts, place, *refs):
    outs = refs[sum(counts) :]
    for out, count in zip(outs, counts):
        parts, refs = refs[:count], refs[count:]
        at = 0
        for part in parts:
            out[at : at + part.shape[0]] = part[...]
            at += part.shape[0]


def relay(place, *tasks, after=()):
    outs = [
        shape((sum(part.shape[0] for part in task), *task[0].shape[1:]), task[0].dtype)
        for task in tasks
    ]
    flat = [part for task in tasks for part in task]
    return call(
        partial(relay_kernel, [len(task) for task in tasks]), outs, place, *flat, after=after
    )


def group_blocks(place, quarters):
    half = quarters[0].shape[0]
    for q, quarter in enumerate(quarters):
        for i in range(half):
            dz, dy = q % 2 * half + i, q // 2
            z = lax.bitwise_xor(place[1], dz)
            yield z * 2 + lax.bitwise_xor(place[2], dy), quarter.at[i]


def assemble(place, quarters, rows, whole):
    for g, block in group_blocks(place, quarters):
        whole[pl.ds(pl.multiple_of(g * rows, rows), rows), :] = block[0:rows]


def prepare_first_kernel(place, att, small, first_o):
    t = place[0]
    d, joint = att.shape
    width = joint // 3
    part = width // TEAM
    for i in range(3):
        first_o[0, 0:d, i * part : (i + 1) * part] = chosen(
            t,
            [
                att[:, i * width + s * part : i * width + (s + 1) * part]
                for s in range(TEAM)
            ],
        )
    first_o[0, d : d + EXTRA, :] = small[...]


def prepare_rest_kernel(n_group, place, hid, back, rest_o):
    t = place[0]
    d = hid.shape[0]
    f = hid.shape[1] // n_group
    w = f // TEAM
    for g in range(n_group):
        rest_o[0:d, g * w : (g + 1) * w] = chosen(
            t, [hid[:, g * f + s * w : g * f + (s + 1) * w] for s in range(TEAM)]
        )
    rest_o[d : d + w, :] = back[pl.ds(pl.multiple_of(t * w, w), w), :]


def attention_kernel(
    n_group, d, f, n, place, p0, p1, p2, p3, own_out, other_out, *refs
):
    first, refs = refs[:4], refs[4:]
    (
        joint_o, probs_o, mixed_o, near_o, keep_o, vec_o, hb_o, wout_o, first_s, token_s, small_s,
    ) = refs
    blocks = (p0, p1, p2, p3)
    t, y = place[0], place[2]
    part = wout_o.shape[0]
    width = wout_o.shape[1]
    w = f // TEAM
    assemble(place, first, d, first_s)
    for g, block in group_blocks(place, first):
        small_s[g] = block[d : d + EXTRA, :].astype(F32)
    small = [small_s[g] for g in range(n_group)]
    vec_o[...] = jnp.concatenate([s[0:8, 0:d] for s in small], 1)
    hb_o[...] = jnp.concatenate(
        [chosen(t, [s[8:9, i * w : (i + 1) * w] for i in range(TEAM)]) for s in small], 1
    )
    for at in range(part // (2 * d)):
        wout_o[pl.ds(pl.multiple_of((at * 2 + y) * d, d), d), :] = own_out[
            at * d : (at + 1) * d
        ]
        wout_o[pl.ds(pl.multiple_of((at * 2 + 1 - y) * d, d), d), :] = other_out[
            at * d : (at + 1) * d
        ]
    for b in range(TEAM):
        token_s[b * n : (b + 1) * n] = blocks[b][0:n]
    mine = pl.ds(pl.multiple_of(t * part, part), part)
    for i in range(3):
        value = times(token_s[...], first_s[:, i * part : (i + 1) * part])
        if i == 0:
            value = value + vec_o[0:1, mine]
        if i == 2:
            value = value + vec_o[1:2, mine]
        joint_o[:, i * part : (i + 1) * part] = value.astype(BF)
    scale = HD ** (-0.5)
    low = lax.broadcasted_iota(jnp.int32, (1, PAIR), 1) < HD
    zero = jnp.zeros((), BF)
    for b in range(TEAM):
        rows = slice(b * n, (b + 1) * n)
        ends = ends_of(blocks[b], n)
        same = segments(ends, (n, 1), 0) == segments(ends, (1, n), 1)
        for pair in range(part // PAIR):
            at = pair * PAIR
            query = joint_o[rows, at : at + PAIR]
            keys = joint_o[rows, part + at : part + at + PAIR]
            values = joint_o[rows, 2 * part + at : 2 * part + at + PAIR]
            mixed = []
            for h in range(2):
                sided = jnp.where(low, query, zero) if h == 0 else jnp.where(low, zero, query)
                scores = jnp.where(same, against(sided, keys) * scale, -1000000000.0)
                expo = jnp.exp(scores - jnp.max(scores, -1, keepdims=True))
                probs = expo / jnp.sum(expo, -1, keepdims=True)
                probs = probs.astype(BF)
                probs_o[(b * (part // PAIR) + pair) * 2 + h] = probs
                mixed.append(times(probs, values))
            mixed_o[rows, at : at + PAIR] = jnp.where(low, mixed[0], mixed[1]).astype(BF)
    for at in range(0, width, part):
        columns = slice(at, at + part)
        to_team(times(mixed_o[...], wout_o[:, columns]), n, near_o, keep_o, columns)


def norm_kernel(place, tokens, keep, got, far, vec, normed_o, low_o, hat_o, factor_o):
    n = tokens.shape[0]
    attn = keep[0:n] + got[0:n].astype(F32) + far[...].astype(F32) + vec[2:3]
    hat, factor = normalise(tokens[...].astype(F32) + attn)
    normed = hat * vec[3:4] + vec[4:5]
    normed_o[...] = normed
    low_o[...] = normed.astype(BF)
    hat_o[...] = hat
    factor_o[...] = jnp.broadcast_to(factor, factor_o.shape)


def gelu_parts(pre):
    bell = 0.5 * (1.0 + lax.erf(pre * (2.0**-0.5)))
    return bell, jnp.exp(-0.5 * pre * pre) * (2.0 * 3.141592653589793) ** -0.5


def feed_kernel(
    n_group, d, place, x0, x1, x2, x3, hb, rest, pre_o, act_o, near_o, keep_o, x_o
):
    n = x0.shape[0]
    w = rest.shape[1] - d
    for b, block in enumerate((x0, x1, x2, x3)):
        x_o[b * n : (b + 1) * n] = block[...]

    def entering(at, carry):
        columns = pl.ds(pl.multiple_of(at * 256, 256), 256)
        weight = rest[:, 0:d, columns].reshape(n_group * d, 256)
        pre = times(x_o[...], weight) + hb[:, columns]
        pre_o[:, columns] = pre
        act_o[:, columns] = (pre * gelu_parts(pre)[0]).astype(BF)
        return carry

    lax.fori_loop(0, pre_o.shape[1] // 256, entering, 0)

    def leaving(at, carry):
        columns = pl.ds(pl.multiple_of(at * 256, 256), 256)
        weight = rest[:, d : d + w, columns].reshape(n_group * w, 256)
        to_team(times(act_o[...], weight), n, near_o, keep_o, columns)
        return carry

    lax.fori_loop(0, keep_o.shape[1] // 256, leaving, 0)


def second_kernel(
    place, normed, keep, got, far, vec, cotangent, packed, layer_o, d_second_o, d_out_o, sums_o
):
    n = normed.shape[0]
    out = keep[0:n] + got[0:n].astype(F32) + far[...].astype(F32) + vec[5:6]
    hat, factor = normalise(normed[...] + out)
    live = jnp.where(segments(ends_of(packed, n), (n, 1), 0) < SEQS, 1.0, 0.0)
    layer_o[...] = ((hat * vec[6:7] + vec[7:8]) * live).astype(BF)
    d_final = cotangent[...].astype(F32) * live
    d_second = normalise_back(d_final * vec[6:7], hat, factor)
    d_second_o[...] = d_second
    d_out = d_second.astype(BF)
    d_out_o[...] = d_out
    sums_o[...] = jnp.zeros_like(sums_o)
    sums_o[0:1] = column_sum(d_out.astype(F32))
    sums_o[1:2] = column_sum(d_final * hat)
    sums_o[2:3] = column_sum(d_final)


def back_grad_kernel(place, d0, d1, d2, d3, act, grad_o, d_out_o):
    n = d0.shape[0]
    for b, block in enumerate((d0, d1, d2, d3)):
        d_out_o[b * n : (b + 1) * n] = block[...]

    def step(at, carry):
        rows = pl.ds(pl.multiple_of(at * 256, 256), 256)
        grad_o[rows, :] = outer(act[:, rows], d_out_o[...]).astype(BF)
        return carry

    lax.fori_loop(0, grad_o.shape[0] // 256, step, 0)


def feed_back_kernel(n_group, d, n, place, d_out, rest, pre, d_pre_o, near_o, keep_o, hb_o):
    w = rest.shape[1] - d
    per = 256 // w

    def through(at, carry):
        columns = pl.ds(pl.multiple_of(at * 256, 256), 256)
        weight = rest[pl.ds(at * per, per), d : d + w, :].reshape(256, rest.shape[2])
        d_act = against(d_out[...], weight)
        value = pre[:, columns]
        bell, slope = gelu_parts(value)
        d_pre = (d_act * (bell + value * slope)).astype(BF)
        d_pre_o[:, columns] = d_pre
        hb_o[:, columns] = column_sum(d_pre.astype(F32))
        return carry

    lax.fori_loop(0, pre.shape[1] // 256, through, 0)
    rows = 256 // d

    def entering(at, carry):
        columns = pl.ds(pl.multiple_of(at * 256, 256), 256)
        weight = rest[pl.ds(at * rows, rows), 0:d, :].reshape(256, rest.shape[2])
        to_team(against(d_pre_o[...], weight), n, near_o, keep_o, columns)
        return carry

    lax.fori_loop(0, keep_o.shape[1] // 256, entering, 0)


def hidden_grad_kernel(n_group, d, place, x, d_pre, own_o, near_o, far_o, tile):
    grad_tiles(place, n_group, d, x, d_pre, own_o, near_o, far_o, tile)


def norm_back_kernel(
    place, d_second, keep, got, far, hat, factor, vec, d_first_o, d_attn_o, sums_o
):
    n = d_second.shape[0]
    d_normed = d_second[...] + keep[0:n] + got[0:n].astype(F32) + far[...].astype(F32)
    d_first = normalise_back(d_normed * vec[3:4], hat[...], factor[:, 0:1])
    d_first_o[...] = d_first
    d_attn = d_first.astype(BF)
    d_attn_o[...] = d_attn
    sums_o[...] = jnp.zeros_like(sums_o)
    sums_o[0:1] = column_sum(d_attn.astype(F32))
    sums_o[1:2] = column_sum(d_normed * hat[...])
    sums_o[2:3] = column_sum(d_normed)


def attention_back_kernel(
    n_group, d, f, n, place, d_attn, wout, joint, probs_in, p0, p1, p2, p3,
    sums1, sums2, d_hb,
    d_joint_o, own_o, near_o, far_o, token_s, tile, vec_s, small_s,
):
    t, z, y = place[0], place[1], place[2]
    depth = n_group // 2
    part = wout.shape[0]
    w = f // TEAM
    for b in range(TEAM):
        token_s[b * n : (b + 1) * n] = (p0, p1, p2, p3)[b][0:n]
    d_mixed = against(d_attn[...], wout[...]).astype(BF)
    scale = HD ** (-0.5)
    low = lax.broadcasted_iota(jnp.int32, (1, PAIR), 1) < HD
    zero = jnp.zeros((), BF)
    for b in range(TEAM):
        rows = slice(b * n, (b + 1) * n)
        for pair in range(part // PAIR):
            at = pair * PAIR
            query = joint[rows, at : at + PAIR]
            keys = joint[rows, part + at : part + at + PAIR]
            values = joint[rows, 2 * part + at : 2 * part + at + PAIR]
            d_mix = d_mixed[rows, at : at + PAIR]
            d_query, d_keys, d_values = [], [], []
            for h in range(2):
                low_probs = probs_in[(b * (part // PAIR) + pair) * 2 + h]
                probs = low_probs.astype(F32)
                sided = jnp.where(low, d_mix, zero) if h == 0 else jnp.where(low, zero, d_mix)
                d_probs = against(sided, values)
                d_scores = (
                    probs * (d_probs - jnp.sum(probs * d_probs, -1, keepdims=True))
                ).astype(BF)
                d_values.append(outer(low_probs, d_mix))
                d_query.append(times(d_scores, keys))
                d_keys.append(outer(d_scores, query))
            for i, (value, factor) in enumerate(
                ((d_query, scale), (d_keys, scale), (d_values, 1.0))
            ):
                d_joint_o[rows, i * part + at : i * part + at + PAIR] = (
                    jnp.where(low, value[0], value[1]) * factor
                ).astype(BF)
    vec_s[...] = jnp.zeros_like(vec_s)
    mine = pl.ds(pl.multiple_of(t * part, part), part)
    vec_s[0:1, mine] = column_sum(d_joint_o[:, 0:part].astype(F32))
    vec_s[1:2, mine] = column_sum(d_joint_o[:, 2 * part : 3 * part].astype(F32))
    vec_s[2:5, :] = sums1[0:3]
    vec_s[5:8, :] = sums2[0:3]
    small_s[...] = jnp.zeros_like(small_s)
    for g in range(n_group):
        small_s[g, 0:8, 0:d] = vec_s[:, g * d : (g + 1) * d]
        row = d_hb[:, g * w : (g + 1) * w]
        small_s[g, 8:9, 0:f] = jnp.concatenate(
            [jnp.where(t == i, row, jnp.zeros_like(row)) for i in range(TEAM)], 1
        )
    grad_tiles(place, n_group, d, token_s, d_joint_o, own_o, near_o, far_o, tile)
    half = depth // 2
    for k in range(depth):
        g = lax.bitwise_xor(z, k) * 2
        own_o[k, d : d + EXTRA, :] = small_s[g + y]
        sent_o = far_o if k >= half else near_o
        sent_o[k % half, d : d + EXTRA, :] = small_s[g + 1 - y].astype(BF)


def out_grad_kernel(d, place, mixed, a0, a1, a2, a3, out_own_o, out_other_o, attn_o, heads_s):
    n = a0.shape[0]
    y = place[2]
    for b, block in enumerate((a0, a1, a2, a3)):
        attn_o[b * n : (b + 1) * n] = block[...]
    heads_s[...] = outer(mixed[...], attn_o[...])
    for at in range(mixed.shape[1] // (2 * d)):
        out_own_o[at * d : (at + 1) * d] = heads_s[
            pl.ds(pl.multiple_of((at * 2 + y) * d, d), d), :
        ]
        out_other_o[at * d : (at + 1) * d] = heads_s[
            pl.ds(pl.multiple_of((at * 2 + 1 - y) * d, d), d), :
        ].astype(BF)


def token_back_kernel(n, d, place, d_joint, f0, f1, f2, f3, near_o, keep_o, first_s):
    assemble(place, (f0, f1, f2, f3), d, first_s)

    def step(at, carry):
        columns = pl.ds(pl.multiple_of(at * 256, 256), 256)
        to_team(against(d_joint[...], first_s[columns, :]), n, near_o, keep_o, columns)
        return carry

    lax.fori_loop(0, keep_o.shape[1] // 256, step, 0)


def add_far_kernel(place, own, got, sum_o):
    half = sum_o.shape[0]
    sum_o[...] = (own[half : 2 * half] + got[0:half].astype(F32)).astype(BF)


def add_near_kernel(place, own, got, far, keep_o, send_o):
    half = far.shape[0]
    total = own[0:half] + got[got.shape[0] - half :].astype(F32) + far[...].astype(F32)
    keep_o[...] = total[0 : half // 2]
    send_o[...] = total[half // 2 :].astype(BF)


def back_out_kernel(place, b0, b1, b2, b3, back_o):
    w = b0.shape[0]
    for i in range(TEAM):
        block = of_member(place[0], i, [b[...] for b in (b0, b1, b2, b3)])
        back_o[i * w : (i + 1) * w] = block.astype(F32)


def hidden_out_kernel(n_group, place, h0, h1, h2, h3, hidden_o):
    w = h0.shape[1] // n_group
    for i in range(TEAM):
        block = of_member(place[0], i, [h[...] for h in (h0, h1, h2, h3)]).astype(F32)
        for g in range(n_group):
            at = (g * TEAM + i) * w
            hidden_o[:, at : at + w] = block[:, g * w : (g + 1) * w]


def attention_out_kernel(f, place, j0, j1, j2, j3, out, joint_o, out_o, *small_o):
    t = place[0]
    d = out_o.shape[0]
    part = j0.shape[1] // 3
    width = part * TEAM
    total = jnp.zeros((EXTRA, 3 * part), F32)
    for i in range(TEAM):
        block = of_member(t, i, [j[...] for j in (j0, j1, j2, j3)]).astype(F32)
        for s in range(3):
            at = s * width + i * part
            joint_o[:, at : at + part] = block[0:d, s * part : (s + 1) * part]
        total = total + block[d : d + EXTRA]
    out_o[...] = out[...].astype(F32)
    for i in range(8):
        small_o[i][...] = total[i : i + 1, 0:d]
    small_o[8][...] = total[8:9, 0:f]


def shards(
    tokens,
    lengths,
    cotangent,
    attention_in,
    query_bias,
    value_bias,
    attention_out,
    out_bias,
    first_gain,
    first_shift,
    hidden_in,
    hidden_bias,
    hidden_out,
    output_bias,
    second_gain,
    second_shift,
):
    at = Places()
    n_group, depth, place = at.n_group, at.depth, at.place
    n, width = tokens.shape
    d = attention_in.shape[0]
    f = hidden_bias.shape[0]
    w = f // TEAM
    part = width // TEAM
    inner = w * n_group
    all_rows = TEAM * n

    vectors = (
        query_bias,
        value_bias,
        out_bias,
        first_gain,
        first_shift,
        output_bias,
        second_gain,
        second_shift,
    )
    small = jnp.concatenate(
        [
            jnp.pad(jnp.stack(vectors), ((0, 0), (0, 3 * part - d))),
            jnp.pad(hidden_bias[None], ((0, EXTRA - 9), (0, 3 * part - f))),
        ],
        0,
    )
    extra = jnp.pad(lengths.astype(BF), ((0, EXTRA - 1), (0, width - lengths.shape[1])))
    packed = jnp.concatenate([tokens, extra], 0)
    (first_near,) = call(
        prepare_first_kernel,
        [shape((1, d + EXTRA, 3 * part), BF)],
        place,
        attention_in,
        small,
    )
    def widen(blocks):
        for flip in list(at.steps_down(at.half // 2))[::-1]:
            blocks = (blocks, at.send_z(blocks, flip))
            if flip < at.half // 2:
                (blocks,) = relay(place, blocks)
        return blocks

    heads_mine, heads_first = [], []
    for i in range(at.heads_at):
        home = at.t * at.heads_at + i
        value = jnp.where(at.z == home, attention_out, jnp.zeros_like(attention_out))
        for flip in at.steps_down(at.half):
            value = value + at.send_heads(value, i, flip, False)
            if flip == at.half:
                heads_first.append(value)
        heads_mine.append(value)
    out_mine = jnp.concatenate(heads_mine, 0)
    out_other = at.send_y(out_mine)
    packed_far = at.send_team(packed, 2)
    packed = [packed, at.send_team(packed, 1), packed_far, at.send_team(packed_far, 1)]

    (first_near,) = relay(place, widen(first_near), after=heads_first)
    (rest_mine,) = call(
        partial(prepare_rest_kernel, n_group),
        [shape((d + w, width), BF)],
        place,
        hidden_in,
        hidden_out,
        after=[first_near],
    )
    rest_all = lax.all_gather(rest_mine, "group", axis=0)
    first_far = at.other_half(first_near)
    first_near_y = at.send_y(first_near)
    (first_sent,) = relay(place, (first_far,), after=[first_near_y, out_other, *packed])
    first_all = [first_near, first_far, first_near_y, at.send_y(first_sent)]

    joint, probs, mixed, near, keep, vec, hb, w_out = call(
        partial(attention_kernel, n_group, d, f, n),
        [
            shape((all_rows, 3 * part), BF),
            shape((TEAM * H // TEAM, n, n), BF),
            shape((all_rows, part), BF),
            shape((2 * n, width), BF),
            shape((2 * n, width), F32),
            shape((8, width), F32),
            shape((1, inner), F32),
            shape((part, width), BF),
        ],
        place,
        *packed,
        out_mine,
        out_other,
        *first_all,
        scratch=[
            pltpu.VMEM((width, 3 * part), BF),
            pltpu.VMEM((all_rows, width), BF),
            pltpu.VMEM((n_group, EXTRA, 3 * part), F32),
        ],
    )
    normed, normed_low, hat, factor = call(
        norm_kernel,
        [
            shape((n, width), F32),
            shape((n, width), BF),
            shape((n, width), F32),
            shape((n, 128), F32),
        ],
        place,
        tokens,
        *at.scatter_team(near, keep),
        vec,
    )

    pre, act, near, keep, normed4 = call(
        partial(feed_kernel, n_group, d),
        [
            shape((all_rows, inner), F32),
            shape((all_rows, inner), BF),
            shape((2 * n, width), BF),
            shape((2 * n, width), F32),
            shape((all_rows, width), BF),
        ],
        place,
        *at.gather_team(normed_low),
        hb,
        rest_all,
    )
    layer_out, d_second, d_out, sums2 = call(
        second_kernel,
        [
            shape((n, width), BF),
            shape((n, width), F32),
            shape((n, width), BF),
            shape((8, width), F32),
        ],
        place,
        normed,
        *at.scatter_team(near, keep),
        vec,
        cotangent,
        packed[0],
    )

    def add_near(own, came_y, came_z, after=()):
        half, *rest = came_z.shape
        return call(
            add_near_kernel,
            [shape((half // 2, *rest), F32), shape((half // 2, *rest), BF)],
            place,
            own,
            came_y,
            came_z,
            after=after,
        )

    def sum_group(keep, send):
        flip = at.half // 2
        while flip > 1:
            total = keep + at.send_z(send, flip).astype(F32)
            flip //= 2
            keep, send = total[:flip], total[flip:].astype(BF)
        return at.over_copies((keep + at.send_z(send, 1).astype(F32))[0].astype(BF))

    half = depth // 2
    def add_far(own, came, after=()):
        half, rest = own.shape[0] // 2, own.shape[1:]
        return call(add_far_kernel, [shape((half, *rest), BF)], place, own, came, after=after)[0]

    grad_back, d_out4 = call(
        back_grad_kernel,
        [shape((inner, width), BF), shape((all_rows, width), BF)],
        place,
        *at.gather_team(d_out),
        act,
    )
    g_back = at.over_copies(
        lax.psum_scatter(grad_back, "group", scatter_dimension=0, tiled=True)
    )
    d_pre, near, keep, d_hb = call(
        partial(feed_back_kernel, n_group, d, n),
        [
            shape((all_rows, inner), BF),
            shape((2 * n, width), BF),
            shape((2 * n, width), F32),
            shape((1, inner), F32),
        ],
        place,
        d_out4,
        rest_all,
        pre,
    )
    own_hidden, near_hidden, far_hidden = call(
        partial(hidden_grad_kernel, n_group, d),
        [shape((depth, d, inner), F32)] + [shape((half, d, inner), BF)] * 2,
        place,
        normed4,
        d_pre,
        scratch=[pltpu.VMEM((2 * d, inner), F32)],
    )
    d_first, d_attn, sums1 = call(
        norm_back_kernel,
        [shape((n, width), F32), shape((n, width), BF), shape((8, width), F32)],
        place,
        d_second,
        *at.scatter_team(near, keep),
        hat,
        factor,
        vec,
        after=[far_hidden],
    )
    heads_rows = at.heads_at * d
    sent_hidden = add_far(own_hidden, at.send_y(far_hidden))
    came_hidden = at.other_half(sent_hidden)
    out_own, out_sent, d_attn4 = call(
        partial(out_grad_kernel, d),
        [
            shape((heads_rows, width), F32),
            shape((heads_rows, width), BF),
            shape((all_rows, width), BF),
        ],
        place,
        mixed,
        *at.gather_team(d_attn),
        after=[sent_hidden],
        scratch=[pltpu.VMEM((part, width), F32)],
    )
    d_joint, own_joint, near_joint, far_joint = call(
        partial(attention_back_kernel, n_group, d, f, n),
        [
            shape((all_rows, 3 * part), BF),
            shape((depth, d + EXTRA, 3 * part), F32),
            shape((half, d + EXTRA, 3 * part), BF),
            shape((half, d + EXTRA, 3 * part), BF),
        ],
        place,
        d_attn4,
        w_out,
        joint,
        probs,
        *packed,
        sums1,
        sums2,
        d_hb,
        scratch=[
            pltpu.VMEM((all_rows, width), BF),
            pltpu.VMEM((2 * d, 3 * part), F32),
            pltpu.VMEM((8, width), F32),
            pltpu.VMEM((n_group, EXTRA, 3 * part), F32),
        ],
    )
    out_sum = out_own + at.send_y(out_sent).astype(F32)
    sent_joint = add_far(own_joint, at.send_y(far_joint), [came_hidden, out_sum])
    blocks = []
    for i in range(at.heads_at):
        block = out_sum[i * d : (i + 1) * d]
        for flip in list(at.steps_down(at.half))[:0:-1]:
            block = block + at.send_heads(block.astype(BF), i, flip, True).astype(F32)
        blocks.append(block)
    (sent_y,) = relay(place, (near_hidden,), after=[sent_joint])
    came_joint = at.other_half(sent_joint)
    hidden_parts = add_near(own_hidden, at.send_y(sent_y), came_hidden, [came_joint, *blocks])
    g_out = jnp.zeros((d, width), F32)
    for i, block in enumerate(blocks):
        block = block + at.send_heads(block.astype(BF), i, at.half, True).astype(F32)
        here = at.z == at.t * at.heads_at + i
        g_out = g_out + jnp.where(here, block, jnp.zeros_like(block))
    g_hidden = sum_group(*hidden_parts)
    back_far = at.send_team(g_back, 2)
    joint_parts = add_near(own_joint, at.send_y(near_joint), came_joint, [g_out])
    g_joint = sum_group(*joint_parts)
    near, keep = call(
        partial(token_back_kernel, n, d),
        [shape((2 * n, width), BF), shape((2 * n, width), F32)],
        place,
        d_joint,
        *first_all,
        after=[],
        scratch=[pltpu.VMEM((width, 3 * part), BF)],
    )
    kept, got, far = at.scatter_team(near, keep)
    g_out = at.over_copies(g_out.astype(BF))
    grad_tokens = d_first + kept[:n] + got[:n].astype(F32) + far.astype(F32)

    (g_hidden_out,) = call(
        back_out_kernel, [shape((f, width), F32)], place, g_back, at.send_team(g_back, 1), back_far, at.send_team(back_far, 1)
    )
    (g_hidden_in,) = call(
        partial(hidden_out_kernel, n_group),
        [shape((d, TEAM * inner), F32)],
        place,
        *at.gather_team(g_hidden),
    )
    joint_far = at.send_team(g_joint, 2)
    (joint_sent,) = relay(place, (joint_far,), after=[g_hidden_out, g_hidden_in, grad_tokens])
    g_attention_in, g_attention_out, *g_small = call(
        partial(attention_out_kernel, f),
        [shape((d, 3 * width), F32), shape((d, width), F32)]
        + [shape((1, d), F32)] * 8
        + [shape((1, f), F32)],
        place,
        g_joint,
        at.send_team(g_joint, 1),
        joint_far,
        at.send_team(joint_sent, 1),
        at.spread_heads(g_out),
    )
    g_qb, g_vb, g_ob, g_g1, g_s1, g_outb, g_g2, g_s2, g_hb = (v.reshape(-1) for v in g_small)
    return (
        layer_out,
        grad_tokens,
        g_attention_in,
        g_qb,
        g_vb,
        g_attention_out,
        g_ob,
        g_g1,
        g_s1,
        g_hidden_in,
        g_hb,
        g_hidden_out,
        g_outb,
        g_g2,
        g_s2,
    )


def solution(mesh):
    rows = P(("replica", "group"), None)
    matrix = P("group", None)
    vector = P("group")
    params = (
        matrix,
        vector,
        vector,
        matrix,
        vector,
        vector,
        vector,
        matrix,
        vector,
        matrix,
        vector,
        vector,
        vector,
    )
    return jax.shard_map(
        shards,
        mesh=mesh,
        in_specs=(rows, rows, rows) + params,
        out_specs=(rows, rows) + params,
        check_vma=False,
    )
```
